256 devices in a mesh: lat: 32 (over y, z_lo, core), lev: 8 (over x, z_hi).
Axes of the slice: x: 4, y: 4, z: 8 (z_hi: 2, z_lo: 4; z = z_hi * 4 + z_lo), core: 2. Of those that a mesh axis runs over, the one named last changes fastest.
Arguments:
- increment: float32 [2, 16, 128, 2048], P(None, 'lev', 'lat'), may hold values from -6 to 6
- deviations: float32 [2, 16, 128, 2048], P(None, 'lev', 'lat'), may hold values from 3 to 12
- diffuse_x: float32 [16, 128, 2048], P('lev', 'lat'), may hold values from 1000 to 4000
- diffuse_y: float32 [16, 128, 2048], P('lev', 'lat'), may hold values from 256 to 640
- diffuse_z: float32 [16, 128, 2048], P('lev', 'lat'), may hold values from 4 to 64
- sea_mask: int32 [16, 128, 2048], P('lev', 'lat'), may hold values from 0 to 1, as said below
Outputs:
- covariance_out: float32 [2, 16, 128, 2048], P(None, 'lev', 'lat')
The draws below stay inside these ranges and needn't reach their ends.
Inputs may be any that keep to these rules, and one draw needn't show every extreme that they name: `sea_mask`: A cell that is land at one level is land at every deeper level.
All inputs are finite; a program needn't handle non-finite values.
Results may differ from the reference program's by a relative error of at most 0.0003.
Values sent between devices are 32-bit elements; how exact they have to be, the bound alone decides.
A program may use at most 64 MiB of HBM per device.

```python
import math
import jax
import jax.numpy as jnp
from jax import lax

TRACERS = 2
ITERS = 2
NLEV = 16
NY = 128
NX = 2048


def draw_sea_mask(key, part):
    key = jax.random.fold_in(key, 1)
    shallow_key, depth_key = jax.random.split(key)
    shallow = jax.random.randint(shallow_key, (NY, NX), 0, 32) == 0
    depth_draw = jax.random.randint(depth_key, (NY, NX), 0, NLEV)
    depth = jnp.where(shallow, depth_draw, NLEV)
    level_index = jnp.arange(NLEV)[:, None, None]
    return (level_index < depth[None]).astype(jnp.int32)


def block_levels(stream_key, extent, cuts, low, top_value):
    level, own = 1.0, jax.random.fold_in(stream_key, 6)
    for position, blocks in cuts:
        draws = jnp.exp(jax.random.uniform(jax.random.fold_in(own, position), (blocks,), jnp.float32, low / len(cuts), top_value / len(cuts)))
        level = level * jnp.repeat(draws, extent[position] // blocks).reshape([-1 if axis == position else 1 for axis in range(len(extent))])
    return level


def normal_values(own_key, shape, deviation, most, pieces=(), dtype=jnp.bfloat16):
    entries = jax.random.normal(own_key, shape, jnp.float32) * deviation
    if len(pieces) > 0:
        entries = block_levels(own_key, shape, pieces, -0.22, 0.18) * entries
    return jnp.clip(entries, min=-most, max=most).astype(dtype)


def setup_inputs(seed: int = 0) -> dict:
    seeds = jax.random.split(jax.random.key(seed), 7)
    increment = normal_values(seeds[0], (TRACERS, NLEV, NY, NX), 1.0, 6.0, ((1, 8), (2, 32)), jnp.float32)
    deviations = jnp.clip(jnp.exp(math.log(12.0) - 1.3862944 * jax.random.uniform(seeds[1], (TRACERS, NLEV, NY, NX), jnp.float32) ** block_levels(seeds[1], (TRACERS, NLEV, NY, NX), ((1, 8), (2, 32)), -0.2, 0.2)), 3.0, 12.0)
    diffuse_x = jnp.clip(jnp.exp(math.log(4000.0) - 1.3862944 * jax.random.uniform(seeds[2], (NLEV, NY, NX), jnp.float32) ** block_levels(seeds[2], (NLEV, NY, NX), ((0, 8), (1, 32)), -0.2, 0.2)), 1000.0, 4000.0)
    diffuse_y = jnp.clip(jnp.exp(math.log(640.0) - 0.916290732 * jax.random.uniform(seeds[3], (NLEV, NY, NX), jnp.float32) ** block_levels(seeds[3], (NLEV, NY, NX), ((0, 8), (1, 32)), -0.2, 0.2)), 256.0, 640.0)
    diffuse_z = jnp.clip(jnp.exp(math.log(64.0) - 2.7725887 * jax.random.uniform(seeds[4], (NLEV, NY, NX), jnp.float32) ** block_levels(seeds[4], (NLEV, NY, NX), ((0, 8), (1, 32)), -0.2, 0.2)), 4.0, 64.0)
    sea_mask = draw_sea_mask(jax.random.fold_in(seeds[6], 71), 0)
    return dict(increment=increment, deviations=deviations, diffuse_x=diffuse_x, diffuse_y=diffuse_y, diffuse_z=diffuse_z, sea_mask=sea_mask)


def previous_cells(values, axis):
    length = values.shape[axis]
    filler = jnp.zeros_like(lax.slice_in_dim(values, 0, 1, axis=axis))
    return jnp.concatenate([filler, lax.slice_in_dim(values, 0, length - 1, axis=axis)], axis)

def couplings(diffuse, sea, axis):
    return diffuse * sea * previous_cells(sea, axis)

def solve_lines(coupling, state, axis):
    moved_coupling = jnp.moveaxis(coupling, axis, -1)
    next_coupling = jnp.concatenate([moved_coupling[..., 1:], jnp.zeros_like(moved_coupling[..., :1])], -1)
    below_band = -moved_coupling
    above_band = -next_coupling
    diagonal = 1.0 + moved_coupling + next_coupling
    right_side = jnp.moveaxis(jnp.moveaxis(state, 0, -1), axis, -2)
    solved = lax.linalg.tridiagonal_solve(below_band, diagonal, above_band, right_side)
    return jnp.moveaxis(jnp.moveaxis(solved, -2, axis), -1, 0)

def reference(increment, deviations, diffuse_x, diffuse_y, diffuse_z, sea_mask):
    sea = sea_mask.astype(jnp.float32)
    couple_x = couplings(diffuse_x, sea, 2)
    couple_y = couplings(diffuse_y, sea, 1)
    couple_z = couplings(diffuse_z, sea, 0)
    row_index = jnp.arange(NY).astype(jnp.float32)
    row_weight = jnp.cos((-78.0 + 166.0 * (row_index + 0.5) / NY) * (math.pi / 180.0))
    state = deviations * sea[None] * increment
    state = solve_lines(couple_z, state, 0)
    for repeat in range(ITERS):
        state = solve_lines(couple_x, state, 2)
        state = solve_lines(couple_y, state, 1)
    state = state * row_weight[:, None]
    for repeat in range(ITERS):
        state = solve_lines(couple_y, state, 1)
        state = solve_lines(couple_x, state, 2)
    state = solve_lines(couple_z, state, 0)
    return deviations * sea[None] * state
```

```python
import math

import jax
import jax.numpy as jnp
from jax import lax
from jax.experimental import pallas as pl
from jax.experimental.pallas import tpu as pltpu
from jax.sharding import PartitionSpec as P

MESH = pl.DeviceIdType.MESH
F32 = jnp.float32
LEVELS, HALF, TILES, BLOCK, ROWS = 16, 1024, 8, 16, 128
STRIDES = (1, 2, 4, 8, 16, 32, 64, 128, 256, 512, 1024)
TO_COLUMNS, TO_LINES, COUPLINGS, NEXT_ROW, REDUCED, LATITUDE, BACK_COLUMNS, BACK_ROWS = 0, 1, 2, 3, 4, 5, 9, 10


def swap_halves(tile):
    return pltpu.roll(tile, 4, 0)


def from_west(tiles, stride, lane):
    if stride >= 128:
        k = stride // 128
        return [tiles[j - k] if j >= k else swap_halves(tiles[TILES + j - k]) for j in range(TILES)]
    turned = [pltpu.roll(tile, stride, 1) for tile in tiles]
    carry = [swap_halves(turned[-1])] + turned[:-1]
    return [jnp.where(lane < stride, c, t) for c, t in zip(carry, turned)]


def from_east(tiles, stride, lane):
    if stride >= 128:
        k = stride // 128
        return [tiles[j + k] if j + k < TILES else swap_halves(tiles[j + k - TILES]) for j in range(TILES)]
    turned = [pltpu.roll(tile, 128 - stride, 1) for tile in tiles]
    carry = turned[1:] + [swap_halves(turned[0])]
    return [jnp.where(lane >= 128 - stride, c, t) for c, t in zip(carry, turned)]


def paired(rows):
    return jnp.concatenate([rows[:, :HALF], rows[:, HALF:]], axis=0)


def tiles_of(wide):
    return [wide[:, 128 * j : 128 * (j + 1)] for j in range(TILES)]


def kernel(
    inc_hbm, dev_hbm, dx_hbm, dy_hbm, dz_hbm, sea_hbm, out_ref,
    inc, dev, dx, dy, dz, mask, scale,
    z_send, z_recv, z_factor, z_out, g_recv, c_send, c_recv, n_send, n_recv,
    x_factor, x_last, y_factor, r_all, inverse, y_all, grid, zb_recv, zb_out, r_recv,
    in_sem, send_sem, recv_sem,
):
    lat, lev = lax.axis_index("lat"), lax.axis_index("lev")
    y, zl, core = lat // 8, (lat // 2) % 4, lat % 2
    x, zh = lev // 2, lev % 2
    mine = y * 2 + core
    lane = lax.broadcasted_iota(jnp.int32, (8, 128), 1)
    sublane = lax.broadcasted_iota(jnp.int32, (8, 128), 0)

    def at(y_, zl_, core_, x_, zh_):
        return {"lat": y_ * 8 + zl_ * 2 + core_, "lev": x_ * 2 + zh_}

    def send(src, dst, phase, target):
        pltpu.make_async_remote_copy(
            src_ref=src, dst_ref=dst, send_sem=send_sem.at[phase], recv_sem=recv_sem.at[phase],
            device_id=target, device_id_type=MESH,
        ).start()

    def send_or_keep(src, dst, phase, target, here):
        @pl.when(here)
        def _():
            pltpu.make_async_copy(src, dst, recv_sem.at[phase]).start()

        @pl.when(jnp.logical_not(here))
        def _():
            send(src, dst, phase, target)

    def wait(ref, sem):
        pltpu.make_async_copy(ref, ref, sem).wait()

    loads = [
        pltpu.make_async_copy(src, dst, in_sem.at[i])
        for i, (src, dst) in enumerate(
            [(sea_hbm, mask), (dev_hbm, dev), (inc_hbm, inc), (dz_hbm, dz), (dx_hbm, dx), (dy_hbm, dy)]
        )
    ]
    for load in loads:
        load.start()

    zf = (zl + 2) % 4
    greeted = [at(y, zf, core, (x + a) % 4, (zh + b) % 2) for a in (2, 1, 3, 0) for b in (0, 1)]
    greeted += [
        at(y, (zl + a) % 4, (core + d) % 2, x, (zh + b) % 2)
        for a in range(4) for b in range(2) for d in range(2)
        if (a, b, d) != (0, 0, 0) and (a, d) != (2, 0)
    ]
    greeted += [at((y + a) % 4, zl, d, x, zh) for a in (2, 1, 3) for d in range(2)]
    barrier = pltpu.get_barrier_semaphore()
    for target in greeted:
        pl.semaphore_signal(barrier, inc=1, device_id=target, device_id_type=MESH)

    for load in loads[:4]:
        load.wait()
    sea = [paired(mask[l]).astype(F32) for l in range(2)]
    for l in range(2):
        couple = tiles_of(paired(dz[l]) * sea[l])
        for t in range(2):
            factor = paired(dev[t, l]) * sea[l]
            state = tiles_of(factor * paired(inc[t, l]))
            factor = tiles_of(factor)
            for j in range(TILES):
                scale[t, l, 8 * j : 8 * j + 8, :] = factor[j]
                spot = pl.ds(8 * (j % 2), 8)
                z_send[t, j // 2, 0, l, spot, :] = state[j]
                z_send[t, j // 2, 1, l, spot, :] = couple[j]
    for load in loads[4:]:
        load.wait()
    for l in range(2):
        sea_tiles = tiles_of(sea[l])
        west = from_west(sea_tiles, 1, lane)
        west[0] = jnp.where((lane == 0) & (sublane < 4), 0.0, west[0])
        couple_x, couple_y = tiles_of(paired(dx[l])), tiles_of(paired(dy[l]))
        for j in range(TILES):
            c_send[l, 0, 8 * j : 8 * j + 8, :] = couple_x[j] * sea_tiles[j] * west[j]
            c_send[l, 1, 8 * j : 8 * j + 8, :] = couple_y[j] * sea_tiles[j]

    pl.semaphore_wait(barrier, len(greeted))

    for a in (2, 1, 3, 0):
        j = (x + a) % 4
        for t in range(2):
            send(z_send.at[t, j], z_recv.at[lev], TO_COLUMNS, at(y, zf, core, j, t))
    part = (zl % 2) * 2 + core
    lines_core = zl // 2
    for l in range(2):
        zt = 2 * zh + l
        for b in (1, 0):
            target = at(y, zt, lines_core, x, (zh + b) % 2)
            src, dst = c_send.at[l], c_recv.at[:, pl.ds(pl.multiple_of(part * 64, 64), 64)]
            if b == 0:
                send_or_keep(src, dst, COUPLINGS, target, (zl == zt) & (core == lines_core))
            else:
                send(src, dst, COUPLINGS, target)

    def solve_levels(take, put):
        upper, lower = take(0), take(15)
        held = {0: upper, 15: lower}
        for k in range(7):
            held[k + 1] = take(k + 1) + z_factor[0, k] * held[k]
            held[14 - k] = take(14 - k) + z_factor[0, 15 - k] * held[15 - k]
        solved = z_factor[1, 8] * (held[8] + z_factor[0, 7] * held[7])
        put(8, solved)
        up = down = solved
        for k in range(8):
            up = z_factor[1, 7 - k] * held[7 - k] + z_factor[0, 7 - k] * up
            put(7 - k, up)
            if k < 7:
                down = z_factor[1, 9 + k] * held[9 + k] + z_factor[0, 9 + k] * down
                put(9 + k, down)

    wait(z_recv, recv_sem.at[TO_COLUMNS])
    upper = lower = jnp.ones((16, 128), F32)
    for k in range(8):
        c_up = z_recv[(k + 1) // 2, 1, (k + 1) % 2]
        inv = 1.0 / (upper + c_up)
        z_factor[0, k] = c_up * inv
        z_factor[1, k] = inv
        upper = 1.0 + c_up * inv * upper
        if k < 7:
            c_low = z_recv[(15 - k) // 2, 1, (15 - k) % 2]
            inv = 1.0 / (lower + c_low)
            z_factor[0, 15 - k] = c_low * inv
            z_factor[1, 15 - k] = inv
            lower = 1.0 + c_low * inv * lower
    z_factor[1, 8] = 1.0 / (upper + (lower - 1.0))

    def put_first(k, value):
        z_out[k] = value

    solve_levels(lambda k: z_recv[k // 2, 0, k % 2], put_first)

    from_core = zf // 2
    from_part = (zf % 2) * 2 + core
    for a in (2, 1, 3, 0):
        for b in (3, 1, 2, 0):
            x_, zl_ = (x + a) % 4, (zl + b) % 4
            src = z_out.at[x_ * 4 + zl_]
            dst = g_recv.at[pl.ds(pl.multiple_of(from_part * 64 + x * 16, 16), 16)]
            target = at(y, zl_, from_core, x_, zh)
            if a == 0 and b == 0:
                send_or_keep(src, dst, TO_LINES, target, from_core == core)
            else:
                send(src, dst, TO_LINES, target)

    wait(c_recv, recv_sem.at[COUPLINGS])

    def row_at(i, half):
        return pl.ds((i // 4) * 64 + (i % 4) + 32 * half, 8, stride=4)

    for half in range(2):
        n_send[8 * half : 8 * half + 8, :] = c_recv[1, row_at(0, half), :]
    before = (mine + 7) % 8
    send(n_send, n_recv, NEXT_ROW, at(before // 2, zl, before % 2, x, zh))

    def longitude_factor(part_, carry):
        base = pl.multiple_of(part_ * 64, 64)
        k = [c_recv[0, pl.ds(base + 8 * j, 8), :] for j in range(TILES)]
        e = [jnp.ones((8, 128), F32)] * TILES
        for i, stride in enumerate(STRIDES):
            k_east = from_east(k, stride, lane)
            inv = [1.0 / (a + (b + c)) for a, b, c in zip(e, k, k_east)]
            plus = [a * b for a, b in zip(k_east, inv)]
            minus = [a * b for a, b in zip(k, inv)]
            for j in range(TILES):
                x_factor[i, 0, pl.ds(base + 8 * j, 8), :] = plus[j]
                x_factor[i, 1, pl.ds(base + 8 * j, 8), :] = minus[j]
            west = from_west([a * b for a, b in zip(plus, e)], stride, lane)
            east = from_east([a * b for a, b in zip(minus, e)], stride, lane)
            k = from_west([a * b for a, b in zip(plus, k)], stride, lane)
            e = [a + (b + c) for a, b, c in zip(e, west, east)]
        for j in range(TILES):
            x_last[pl.ds(base + 8 * j, 8), :] = 1.0 / e[j]
        return carry

    lax.fori_loop(0, 4, longitude_factor, 0)

    wait(n_recv, recv_sem.at[NEXT_ROW])
    for half in range(2):
        spot = pl.ds(8 * half, 8)
        faces = [c_recv[1, row_at(i, half), :] for i in range(BLOCK)]
        north = jnp.where(mine < 7, n_recv[spot, :], 0.0)
        couple = [None] + [
            jnp.where(faces[i - 1] > 0.0, faces[i] if i < BLOCK else north, 0.0) for i in range(1, BLOCK + 1)
        ]
        ground = jnp.ones((8, 128), F32)
        own, link = jnp.ones((8, 128), F32), couple[1]
        to_own, to_next = [None] * BLOCK, [None] * BLOCK
        for i in range(1, BLOCK):
            inv = 1.0 / (ground + (link + couple[i + 1]))
            to_own[i], to_next[i] = link * inv, couple[i + 1] * inv
            y_factor[0, i, spot, :] = to_own[i]
            y_factor[1, i, spot, :] = to_next[i]
            y_factor[2, i, spot, :] = inv
            own = own + to_own[i] * ground
            link = to_own[i] * couple[i + 1]
            beyond = to_next[i] * ground
            ground = 1.0 + beyond
        r_all[mine, 0, spot, :] = own
        r_all[mine, 1, spot, :] = beyond
        r_all[mine, 2, spot, :] = link
        left, right = to_own[15], to_next[15]
        y_factor[3, 15, spot, :] = left
        y_factor[4, 15, spot, :] = right
        for i in range(BLOCK - 2, 0, -1):
            left = to_own[i] + to_next[i] * left
            right = to_next[i] * right
            y_factor[3, i, spot, :] = left
            y_factor[4, i, spot, :] = right

    ring = []
    for k in (4, 5, 3, 2, 6, 7, 1):
        block = (mine + k) % 8
        ring.append(at(block // 2, zl, block % 2, x, zh))
    for target in ring:
        send(r_all.at[mine], r_all.at[mine], REDUCED, target)

    def longitude_solve(source):
        def one(part_, carry):
            base = pl.multiple_of(part_ * 64, 64)
            r = [source[pl.ds(base + 8 * j, 8), :] for j in range(TILES)]
            for i, stride in enumerate(STRIDES):
                west = from_west([x_factor[i, 0, pl.ds(base + 8 * j, 8), :] * r[j] for j in range(TILES)], stride, lane)
                east = from_east([x_factor[i, 1, pl.ds(base + 8 * j, 8), :] * r[j] for j in range(TILES)], stride, lane)
                r = [a + (b + c) for a, b, c in zip(r, west, east)]
            for j in range(TILES):
                grid[pl.ds(base + 8 * j, 8), :] = r[j] * x_last[pl.ds(base + 8 * j, 8), :]
            return carry

        lax.fori_loop(0, 4, one, 0)

    def reduced_inverse():
        for half in range(2):
            spot = pl.ds(8 * half, 8)
            ground = [r_all[b, 0, spot, :] for b in range(8)]
            for b in range(1, 8):
                ground[b] = ground[b] + r_all[b - 1, 1, spot, :]
            link = [r_all[b, 2, spot, :] for b in range(7)]
            below, above = [ground[0]], [None] * 7 + [jnp.zeros((8, 128), F32)]
            north, south = [None] * 8, [None] * 8
            for b in range(7):
                north[b] = link[b] / (below[b] + link[b])
                below.append(ground[b + 1] + north[b] * below[b])
            for b in range(7, 0, -1):
                total = ground[b] + above[b]
                south[b] = link[b - 1] / (total + link[b - 1])
                above[b - 1] = south[b] * total
            for which in range(2):
                spike = mine + which
                row = [None] * 8
                here = jnp.zeros((8, 128), F32)
                for b in range(7, -1, -1):
                    moved = here if b == 7 else north[b] * here
                    here = jnp.where(spike == b, 1.0 / (below[b] + above[b]), moved)
                    row[b] = here
                here = jnp.zeros((8, 128), F32)
                for b in range(8):
                    moved = here if b == 0 else south[b] * here
                    here = jnp.where(spike < b, moved, row[b])
                    inverse[which, b, spot, :] = here

    def latitude_solve(rows, step, between=None):
        held = []
        for half in range(2):
            spot = pl.ds(8 * half, 8)
            own, here = rows(0, half), rows(1, half)
            mid = [None]
            for i in range(1, BLOCK):
                mid.append(y_factor[2, i, spot, :] * here)
                own = own + y_factor[0, i, spot, :] * here
                here = y_factor[1, i, spot, :] * here
                if i + 1 < BLOCK:
                    here = rows(i + 1, half) + here
            y_all[step, mine, spot, :] = own
            y_all[step, mine, pl.ds(16 + 8 * half, 8), :] = here
            held.append(mid)
        for target in ring:
            send(y_all.at[step, mine], y_all.at[step, mine], LATITUDE + step, target)
        for half in range(2):
            spot = pl.ds(8 * half, 8)
            for i in range(BLOCK - 2, 0, -1):
                held[half][i] = held[half][i] + y_factor[1, i, spot, :] * held[half][i + 1]
        if between is not None:
            between()
        wait(y_all.at[step, pl.ds(0, 7)], recv_sem.at[LATITUDE + step])
        result = []
        for half in range(2):
            spot = pl.ds(8 * half, 8)
            ends = []
            right = []
            for b in range(8):
                value = y_all[step, b, spot, :]
                if b > 0:
                    value = value + y_all[step, b - 1, pl.ds(16 + 8 * half, 8), :]
                right.append(value)
            for which in range(2):
                terms = [inverse[which, b, spot, :] * right[b] for b in range(8)]
                while len(terms) > 1:
                    terms = [a + b for a, b in zip(terms[::2], terms[1::2])]
                ends.append(terms[0])
            result.append(
                [ends[0]]
                + [
                    held[half][i] + (y_factor[3, i, spot, :] * ends[0] + y_factor[4, i, spot, :] * ends[1])
                    for i in range(1, BLOCK)
                ]
            )
        return result

    def from_grid(i, half):
        return grid[row_at(i, half), :]

    def to_grid(result):
        for half in range(2):
            for i in range(BLOCK):
                grid[row_at(i, half), :] = result[half][i]

    def first_between():
        wait(r_all.at[pl.ds(0, 7)], recv_sem.at[REDUCED])
        reduced_inverse()

    row = (mine * BLOCK + lax.broadcasted_iota(jnp.int32, (BLOCK, 128), 0)).astype(F32)
    weight = jnp.cos((-78.0 + 166.0 * (row + 0.5) / ROWS) * (math.pi / 180.0))

    wait(g_recv, recv_sem.at[TO_LINES])
    longitude_solve(g_recv)
    to_grid(latitude_solve(from_grid, 0, first_between))
    longitude_solve(grid)
    forward = latitude_solve(from_grid, 1)
    weighted = [[forward[half][i] * weight[i : i + 1, :] for i in range(BLOCK)] for half in range(2)]
    to_grid(latitude_solve(lambda i, half: weighted[half][i], 2))
    longitude_solve(grid)
    to_grid(latitude_solve(from_grid, 3))
    longitude_solve(grid)

    level = x * 4 + zl
    for a in (2, 1, 3, 0):
        x_ = (x + a) % 4
        for b in range(4):
            zl_, core_ = (2 * core + b // 2 + 2) % 4, b % 2
            src = grid.at[pl.ds(pl.multiple_of(b * 64 + x_ * 16, 16), 16)]
            target = at(y, zl_, core_, x_, zh)
            if a == 0:
                send_or_keep(src, zb_recv.at[level], BACK_COLUMNS, target, (zl_ == zl) & (core_ == core))
            else:
                send(src, zb_recv.at[level], BACK_COLUMNS, target)
    wait(zb_recv, recv_sem.at[BACK_COLUMNS])

    def put_last(k, value):
        zb_out[k] = value

    solve_levels(lambda k: zb_recv[k], put_last)
    for a in (2, 1, 3, 0):
        for b in range(2):
            x_ = (x + a) % 4
            src = zb_out.at[pl.ds(x_ * 4 + b * 2, 2)]
            dst = r_recv.at[zh, :, pl.ds(pl.multiple_of(x * 16, 16), 16)]
            send(src, dst, BACK_ROWS, at(y, zf, core, x_, b))
    wait(r_recv, recv_sem.at[BACK_ROWS])
    for t in range(2):
        for l in range(2):
            for j in range(TILES):
                spot = pl.ds(8 * j, 8)
                tile = scale[t, l, spot, :] * r_recv[t, l, spot, :]
                out_ref[t, l, :, 128 * j : 128 * j + 128] = tile[:4]
                out_ref[t, l, :, HALF + 128 * j : HALF + 128 * j + 128] = tile[4:]

    wait(z_send.at[:, :, :, :], send_sem.at[TO_COLUMNS])
    for l in range(2):
        wait(c_send.at[l], send_sem.at[COUPLINGS])
        kept = (zl == 2 * zh + l) & (core == lines_core)

        @pl.when(jnp.logical_not(kept))
        def _():
            wait(c_send.at[l], send_sem.at[COUPLINGS])

    wait(z_out.at[pl.ds(0, 15)], send_sem.at[TO_LINES])

    @pl.when(from_core != core)
    def _():
        wait(z_out.at[15], send_sem.at[TO_LINES])

    wait(n_send, send_sem.at[NEXT_ROW])
    wait(r_all.at[pl.ds(0, 7)], send_sem.at[REDUCED])
    for step in range(4):
        wait(y_all.at[step, pl.ds(0, 7)], send_sem.at[LATITUDE + step])
    wait(zb_recv.at[pl.ds(0, 15)], send_sem.at[BACK_COLUMNS])
    base = (zl - 2 * core + 2) % 4

    @pl.when(base >= 2)
    def _():
        wait(zb_recv.at[15], send_sem.at[BACK_COLUMNS])

    wait(r_recv, send_sem.at[BACK_ROWS])


def per_device(increment, deviations, diffuse_x, diffuse_y, diffuse_z, sea_mask):
    vmem = lambda *shape: pltpu.VMEM(shape, F32)
    shape = increment.shape
    plane = diffuse_x.shape
    return pl.pallas_call(
        kernel,
        out_shape=jax.ShapeDtypeStruct(shape, F32),
        in_specs=[pl.BlockSpec(memory_space=pl.ANY)] * 6,
        out_specs=pl.BlockSpec(memory_space=pltpu.VMEM),
        scratch_shapes=[
            vmem(*shape), vmem(*shape), vmem(*plane), vmem(*plane), vmem(*plane), pltpu.VMEM(plane, jnp.int32),
            vmem(2, 2, 64, 128),
            vmem(2, 4, 2, 2, 16, 128), vmem(8, 2, 2, 16, 128), vmem(2, 16, 16, 128), vmem(16, 16, 128),
            vmem(256, 128), vmem(2, 2, 64, 128), vmem(2, 256, 128), vmem(16, 128), vmem(16, 128),
            vmem(11, 2, 256, 128), vmem(256, 128), vmem(5, 16, 16, 128), vmem(8, 3, 16, 128), vmem(2, 8, 16, 128),
            vmem(4, 8, 32, 128), vmem(256, 128), vmem(16, 16, 128), vmem(16, 16, 128), vmem(2, 2, 64, 128),
            pltpu.SemaphoreType.DMA((6,)), pltpu.SemaphoreType.DMA((11,)), pltpu.SemaphoreType.DMA((11,)),
        ],
        compiler_params=pltpu.CompilerParams(
            collective_id=0, has_side_effects=True, vmem_limit_bytes=32 * 1024 * 1024
        ),
        name="covariance",
    )(increment, deviations, diffuse_x, diffuse_y, diffuse_z, sea_mask)


def solution(mesh):
    in_specs = (
        P(None, "lev", "lat", None),
        P(None, "lev", "lat", None),
        P("lev", "lat", None),
        P("lev", "lat", None),
        P("lev", "lat", None),
        P("lev", "lat", None),
    )
    out_specs = P(None, "lev", "lat", None)
    return jax.shard_map(
        per_device, mesh=mesh, in_specs=in_specs, out_specs=out_specs, check_vma=False
    )
```

```python
import math

import jax
import jax.numpy as jnp
from jax import lax
from jax.experimental import pallas as pl
from jax.experimental.pallas import tpu as pltpu
from jax.sharding import PartitionSpec as P

MESH = pl.DeviceIdType.MESH
F32 = jnp.float32
LEVELS, HALF, TILES, BLOCK, ROWS = 16, 1024, 8, 16, 128
GROUP = 4
STRIDES = (1, 2, 4, 8, 16, 32, 64, 128, 256, 512, 1024)
TO_COLUMNS, TO_LINES, COUPLINGS, NEXT_ROW, REDUCED, LATITUDE, BACK_COLUMNS, BACK_ROWS = 0, 1, 2, 3, 4, 5, 9, 10


def swap_halves(tile):
    return pltpu.roll(tile, 4, 0)


def from_west(tiles, stride, lane):
    if stride >= 128:
        k = stride // 128
        return [tiles[j - k] if j >= k else swap_halves(tiles[TILES + j - k]) for j in range(TILES)]
    turned = [pltpu.roll(tile, stride, 1) for tile in tiles]
    carry = [swap_halves(turned[-1])] + turned[:-1]
    return [jnp.where(lane < stride, c, t) for c, t in zip(carry, turned)]


def from_east(tiles, stride, lane):
    if stride >= 128:
        k = stride // 128
        return [tiles[j + k] if j + k < TILES else swap_halves(tiles[j + k - TILES]) for j in range(TILES)]
    turned = [pltpu.roll(tile, 128 - stride, 1) for tile in tiles]
    carry = turned[1:] + [swap_halves(turned[0])]
    return [jnp.where(lane >= 128 - stride, c, t) for c, t in zip(carry, turned)]


def paired(rows):
    return jnp.concatenate([rows[:, :HALF], rows[:, HALF:]], axis=0)


def tiles_of(wide):
    return [wide[:, 128 * j : 128 * (j + 1)] for j in range(TILES)]


def kernel(
    inc_hbm, dev_hbm, dx_hbm, dy_hbm, dz_hbm, sea_hbm, out_ref,
    inc, dev, dx, dy, dz, mask, scale,
    z_send, z_recv, z_factor, z_out, g_recv, c_send, c_recv, n_send, n_recv,
    x_factor, x_last, y_factor, r_all, inverse, y_all, grid, zb_recv, zb_out, r_recv,
    in_sem, send_sem, recv_sem,
):
    lat, lev = lax.axis_index("lat"), lax.axis_index("lev")
    y, zl, core = lat // 8, (lat // 2) % 4, lat % 2
    x, zh = lev // 2, lev % 2
    mine = y * 2 + core
    lane = lax.broadcasted_iota(jnp.int32, (8, 128), 1)
    sublane = lax.broadcasted_iota(jnp.int32, (8, 128), 0)

    def at(y_, zl_, core_, x_, zh_):
        return {"lat": y_ * 8 + zl_ * 2 + core_, "lev": x_ * 2 + zh_}

    def send(src, dst, phase, target):
        pltpu.make_async_remote_copy(
            src_ref=src, dst_ref=dst, send_sem=send_sem.at[phase], recv_sem=recv_sem.at[phase],
            device_id=target, device_id_type=MESH,
        ).start()

    def send_or_keep(src, dst, phase, target, here):
        @pl.when(here)
        def _():
            pltpu.make_async_copy(src, dst, recv_sem.at[phase]).start()

        @pl.when(jnp.logical_not(here))
        def _():
            send(src, dst, phase, target)

    def wait(ref, sem):
        pltpu.make_async_copy(ref, ref, sem).wait()

    loads = [
        pltpu.make_async_copy(src, dst, in_sem.at[i])
        for i, (src, dst) in enumerate(
            [(sea_hbm, mask), (dev_hbm, dev), (inc_hbm, inc), (dz_hbm, dz), (dx_hbm, dx), (dy_hbm, dy)]
        )
    ]
    for load in loads:
        load.start()

    zf = (zl + 2) % 4
    greeted = [at(y, zf, core, (x + a) % 4, (zh + b) % 2) for a in (2, 1, 3, 0) for b in (0, 1)]
    greeted += [
        at(y, (zl + a) % 4, (core + d) % 2, x, (zh + b) % 2)
        for a in range(4) for b in range(2) for d in range(2)
        if (a, b, d) != (0, 0, 0) and (a, d) != (2, 0)
    ]
    greeted += [at((y + a) % 4, zl, d, x, zh) for a in (2, 1, 3) for d in range(2)]
    barrier = pltpu.get_barrier_semaphore()
    for target in greeted:
        pl.semaphore_signal(barrier, inc=1, device_id=target, device_id_type=MESH)

    for load in loads[:4]:
        load.wait()
    sea = [paired(mask[l]).astype(F32) for l in range(2)]
    for l in range(2):
        couple = tiles_of(paired(dz[l]) * sea[l])
        for t in range(2):
            factor = paired(dev[t, l]) * sea[l]
            state = tiles_of(factor * paired(inc[t, l]))
            factor = tiles_of(factor)
            for j in range(TILES):
                scale[t, l, 8 * j : 8 * j + 8, :] = factor[j]
                spot = pl.ds(8 * (j % 2), 8)
                z_send[t, j // 2, 0, l, spot, :] = state[j]
                z_send[t, j // 2, 1, l, spot, :] = couple[j]
    for load in loads[4:]:
        load.wait()
    for l in range(2):
        sea_tiles = tiles_of(sea[l])
        west = from_west(sea_tiles, 1, lane)
        west[0] = jnp.where((lane == 0) & (sublane < 4), 0.0, west[0])
        couple_x, couple_y = tiles_of(paired(dx[l])), tiles_of(paired(dy[l]))
        for j in range(TILES):
            c_send[l, 0, 8 * j : 8 * j + 8, :] = couple_x[j] * sea_tiles[j] * west[j]
            c_send[l, 1, 8 * j : 8 * j + 8, :] = couple_y[j] * sea_tiles[j]

    pl.semaphore_wait(barrier, len(greeted))

    for a in (2, 1, 3, 0):
        j = (x + a) % 4
        for t in range(2):
            send(z_send.at[t, j], z_recv.at[lev], TO_COLUMNS, at(y, zf, core, j, t))
    part = (zl % 2) * 2 + core
    lines_core = zl // 2
    for l in range(2):
        zt = 2 * zh + l
        for b in (1, 0):
            target = at(y, zt, lines_core, x, (zh + b) % 2)
            src, dst = c_send.at[l], c_recv.at[:, pl.ds(pl.multiple_of(part * 64, 64), 64)]
            if b == 0:
                send_or_keep(src, dst, COUPLINGS, target, (zl == zt) & (core == lines_core))
            else:
                send(src, dst, COUPLINGS, target)

    def solve_levels(take, put):
        upper, lower = take(0), take(15)
        held = {0: upper, 15: lower}
        for k in range(7):
            held[k + 1] = take(k + 1) + z_factor[0, k] * held[k]
            held[14 - k] = take(14 - k) + z_factor[0, 15 - k] * held[15 - k]
        solved = z_factor[1, 8] * (held[8] + z_factor[0, 7] * held[7])
        put(8, solved)
        up = down = solved
        for k in range(8):
            up = z_factor[1, 7 - k] * held[7 - k] + z_factor[0, 7 - k] * up
            put(7 - k, up)
            if k < 7:
                down = z_factor[1, 9 + k] * held[9 + k] + z_factor[0, 9 + k] * down
                put(9 + k, down)

    wait(z_recv, recv_sem.at[TO_COLUMNS])
    upper = lower = jnp.ones((16, 128), F32)
    for k in range(8):
        c_up = z_recv[(k + 1) // 2, 1, (k + 1) % 2]
        inv = 1.0 / (upper + c_up)
        z_factor[0, k] = c_up * inv
        z_factor[1, k] = inv
        upper = 1.0 + c_up * inv * upper
        if k < 7:
            c_low = z_recv[(15 - k) // 2, 1, (15 - k) % 2]
            inv = 1.0 / (lower + c_low)
            z_factor[0, 15 - k] = c_low * inv
            z_factor[1, 15 - k] = inv
            lower = 1.0 + c_low * inv * lower
    z_factor[1, 8] = 1.0 / (upper + (lower - 1.0))

    def put_first(k, value):
        z_out[k] = value

    solve_levels(lambda k: z_recv[k // 2, 0, k % 2], put_first)

    from_core = zf // 2
    from_part = (zf % 2) * 2 + core
    for a in (2, 1, 3, 0):
        for b in (3, 1, 2, 0):
            x_, zl_ = (x + a) % 4, (zl + b) % 4
            src = z_out.at[x_ * 4 + zl_]
            dst = g_recv.at[pl.ds(pl.multiple_of(from_part * 64 + x * 16, 16), 16)]
            target = at(y, zl_, from_core, x_, zh)
            if a == 0 and b == 0:
                send_or_keep(src, dst, TO_LINES, target, from_core == core)
            else:
                send(src, dst, TO_LINES, target)

    wait(c_recv, recv_sem.at[COUPLINGS])

    def row_at(i, half):
        return pl.ds((i // 4) * 64 + (i % 4) + 32 * half, 8, stride=4)

    for half in range(2):
        n_send[8 * half : 8 * half + 8, :] = c_recv[1, row_at(0, half), :]
    before = (mine + 7) % 8
    send(n_send, n_recv, NEXT_ROW, at(before // 2, zl, before % 2, x, zh))

    def longitude_factor(step, carry):
        bases = [pl.multiple_of(step * (64 * GROUP), 64) + 64 * g for g in range(GROUP)]
        k = [[c_recv[0, pl.ds(base + 8 * j, 8), :] for j in range(TILES)] for base in bases]
        e = [[jnp.ones((8, 128), F32)] * TILES for _ in bases]
        for i, stride in enumerate(STRIDES):
            for g, base in enumerate(bases):
                k_east = from_east(k[g], stride, lane)
                inv = [1.0 / (a + (b + c)) for a, b, c in zip(e[g], k[g], k_east)]
                plus = [a * b for a, b in zip(k_east, inv)]
                minus = [a * b for a, b in zip(k[g], inv)]
                for j in range(TILES):
                    x_factor[i, 0, pl.ds(base + 8 * j, 8), :] = plus[j]
                    x_factor[i, 1, pl.ds(base + 8 * j, 8), :] = minus[j]
                west = from_west([a * b for a, b in zip(plus, e[g])], stride, lane)
                east = from_east([a * b for a, b in zip(minus, e[g])], stride, lane)
                k[g] = from_west([a * b for a, b in zip(plus, k[g])], stride, lane)
                e[g] = [a + (b + c) for a, b, c in zip(e[g], west, east)]
        for g, base in enumerate(bases):
            for j in range(TILES):
                x_last[pl.ds(base + 8 * j, 8), :] = 1.0 / e[g][j]
        return carry

    lax.fori_loop(0, 4 // GROUP, longitude_factor, 0)

    wait(n_recv, recv_sem.at[NEXT_ROW])
    for half in range(2):
        spot = pl.ds(8 * half, 8)
        faces = [c_recv[1, row_at(i, half), :] for i in range(BLOCK)]
        north = jnp.where(mine < 7, n_recv[spot, :], 0.0)
        couple = [None] + [
            jnp.where(faces[i - 1] > 0.0, faces[i] if i < BLOCK else north, 0.0) for i in range(1, BLOCK + 1)
        ]
        ground = jnp.ones((8, 128), F32)
        own, link = jnp.ones((8, 128), F32), couple[1]
        to_own, to_next = [None] * BLOCK, [None] * BLOCK
        for i in range(1, BLOCK):
            inv = 1.0 / (ground + (link + couple[i + 1]))
            to_own[i], to_next[i] = link * inv, couple[i + 1] * inv
            y_factor[0, i, spot, :] = to_own[i]
            y_factor[1, i, spot, :] = to_next[i]
            y_factor[2, i, spot, :] = inv
            own = own + to_own[i] * ground
            link = to_own[i] * couple[i + 1]
            beyond = to_next[i] * ground
            ground = 1.0 + beyond
        r_all[mine, 0, spot, :] = own
        r_all[mine, 1, spot, :] = beyond
        r_all[mine, 2, spot, :] = link
        left, right = to_own[15], to_next[15]
        y_factor[3, 15, spot, :] = left
        y_factor[4, 15, spot, :] = right
        for i in range(BLOCK - 2, 0, -1):
            left = to_own[i] + to_next[i] * left
            right = to_next[i] * right
            y_factor[3, i, spot, :] = left
            y_factor[4, i, spot, :] = right

    ring = []
    for k in (4, 5, 3, 2, 6, 7, 1):
        block = (mine + k) % 8
        ring.append(at(block // 2, zl, block % 2, x, zh))
    for target in ring:
        send(r_all.at[mine], r_all.at[mine], REDUCED, target)

    def longitude_solve(source):
        def one(step, carry):
            bases = [pl.multiple_of(step * (64 * GROUP), 64) + 64 * g for g in range(GROUP)]
            r = [[source[pl.ds(base + 8 * j, 8), :] for j in range(TILES)] for base in bases]
            for i, stride in enumerate(STRIDES):
                for g, base in enumerate(bases):
                    plus = [x_factor[i, 0, pl.ds(base + 8 * j, 8), :] * r[g][j] for j in range(TILES)]
                    minus = [x_factor[i, 1, pl.ds(base + 8 * j, 8), :] * r[g][j] for j in range(TILES)]
                    west, east = from_west(plus, stride, lane), from_east(minus, stride, lane)
                    r[g] = [a + (b + c) for a, b, c in zip(r[g], west, east)]
            for g, base in enumerate(bases):
                for j in range(TILES):
                    grid[pl.ds(base + 8 * j, 8), :] = r[g][j] * x_last[pl.ds(base + 8 * j, 8), :]
            return carry

        lax.fori_loop(0, 4 // GROUP, one, 0)

    def reduced_inverse():
        for half in range(2):
            spot = pl.ds(8 * half, 8)
            ground = [r_all[b, 0, spot, :] for b in range(8)]
            for b in range(1, 8):
                ground[b] = ground[b] + r_all[b - 1, 1, spot, :]
            link = [r_all[b, 2, spot, :] for b in range(7)]
            below, above = [ground[0]], [None] * 7 + [jnp.zeros((8, 128), F32)]
            north, south = [None] * 8, [None] * 8
            for b in range(7):
                north[b] = link[b] / (below[b] + link[b])
                below.append(ground[b + 1] + north[b] * below[b])
            for b in range(7, 0, -1):
                total = ground[b] + above[b]
                south[b] = link[b - 1] / (total + link[b - 1])
                above[b - 1] = south[b] * total
            for which in range(2):
                spike = mine + which
                row = [None] * 8
                here = jnp.zeros((8, 128), F32)
                for b in range(7, -1, -1):
                    moved = here if b == 7 else north[b] * here
                    here = jnp.where(spike == b, 1.0 / (below[b] + above[b]), moved)
                    row[b] = here
                here = jnp.zeros((8, 128), F32)
                for b in range(8):
                    moved = here if b == 0 else south[b] * here
                    here = jnp.where(spike < b, moved, row[b])
                    inverse[which, b, spot, :] = here

    def latitude_solve(rows, step, between=None):
        held = []
        for half in range(2):
            spot = pl.ds(8 * half, 8)
            own, here = rows(0, half), rows(1, half)
            mid = [None]
            for i in range(1, BLOCK):
                mid.append(y_factor[2, i, spot, :] * here)
                own = own + y_factor[0, i, spot, :] * here
                here = y_factor[1, i, spot, :] * here
                if i + 1 < BLOCK:
                    here = rows(i + 1, half) + here
            y_all[step, mine, spot, :] = own
            y_all[step, mine, pl.ds(16 + 8 * half, 8), :] = here
            held.append(mid)
        for target in ring:
            send(y_all.at[step, mine], y_all.at[step, mine], LATITUDE + step, target)
        for half in range(2):
            spot = pl.ds(8 * half, 8)
            for i in range(BLOCK - 2, 0, -1):
                held[half][i] = held[half][i] + y_factor[1, i, spot, :] * held[half][i + 1]
        if between is not None:
            between()
        wait(y_all.at[step, pl.ds(0, 7)], recv_sem.at[LATITUDE + step])
        result = []
        for half in range(2):
            spot = pl.ds(8 * half, 8)
            ends = []
            right = []
            for b in range(8):
                value = y_all[step, b, spot, :]
                if b > 0:
                    value = value + y_all[step, b - 1, pl.ds(16 + 8 * half, 8), :]
                right.append(value)
            for which in range(2):
                terms = [inverse[which, b, spot, :] * right[b] for b in range(8)]
                while len(terms) > 1:
                    terms = [a + b for a, b in zip(terms[::2], terms[1::2])]
                ends.append(terms[0])
            result.append(
                [ends[0]]
                + [
                    held[half][i] + (y_factor[3, i, spot, :] * ends[0] + y_factor[4, i, spot, :] * ends[1])
                    for i in range(1, BLOCK)
                ]
            )
        return result

    def from_grid(i, half):
        return grid[row_at(i, half), :]

    def to_grid(result):
        for half in range(2):
            for i in range(BLOCK):
                grid[row_at(i, half), :] = result[half][i]

    def first_between():
        wait(r_all.at[pl.ds(0, 7)], recv_sem.at[REDUCED])
        reduced_inverse()

    row = (mine * BLOCK + lax.broadcasted_iota(jnp.int32, (BLOCK, 128), 0)).astype(F32)
    weight = jnp.cos((-78.0 + 166.0 * (row + 0.5) / ROWS) * (math.pi / 180.0))

    wait(g_recv, recv_sem.at[TO_LINES])
    longitude_solve(g_recv)
    to_grid(latitude_solve(from_grid, 0, first_between))
    longitude_solve(grid)
    forward = latitude_solve(from_grid, 1)
    weighted = [[forward[half][i] * weight[i : i + 1, :] for i in range(BLOCK)] for half in range(2)]
    to_grid(latitude_solve(lambda i, half: weighted[half][i], 2))
    longitude_solve(grid)
    to_grid(latitude_solve(from_grid, 3))
    longitude_solve(grid)

    level = x * 4 + zl
    for a in (2, 1, 3, 0):
        x_ = (x + a) % 4
        for b in range(4):
            zl_, core_ = (2 * core + b // 2 + 2) % 4, b % 2
            src = grid.at[pl.ds(pl.multiple_of(b * 64 + x_ * 16, 16), 16)]
            target = at(y, zl_, core_, x_, zh)
            if a == 0:
                send_or_keep(src, zb_recv.at[level], BACK_COLUMNS, target, (zl_ == zl) & (core_ == core))
            else:
                send(src, zb_recv.at[level], BACK_COLUMNS, target)
    wait(zb_recv, recv_sem.at[BACK_COLUMNS])

    def put_last(k, value):
        zb_out[k] = value

    solve_levels(lambda k: zb_recv[k], put_last)
    for a in (2, 1, 3, 0):
        for b in range(2):
            x_ = (x + a) % 4
            src = zb_out.at[pl.ds(x_ * 4 + b * 2, 2)]
            dst = r_recv.at[zh, :, pl.ds(pl.multiple_of(x * 16, 16), 16)]
            send(src, dst, BACK_ROWS, at(y, zf, core, x_, b))
    wait(r_recv, recv_sem.at[BACK_ROWS])
    for t in range(2):
        for l in range(2):
            for j in range(TILES):
                spot = pl.ds(8 * j, 8)
                tile = scale[t, l, spot, :] * r_recv[t, l, spot, :]
                out_ref[t, l, :, 128 * j : 128 * j + 128] = tile[:4]
                out_ref[t, l, :, HALF + 128 * j : HALF + 128 * j + 128] = tile[4:]

    wait(z_send.at[:, :, :, :], send_sem.at[TO_COLUMNS])
    for l in range(2):
        wait(c_send.at[l], send_sem.at[COUPLINGS])
        kept = (zl == 2 * zh + l) & (core == lines_core)

        @pl.when(jnp.logical_not(kept))
        def _():
            wait(c_send.at[l], send_sem.at[COUPLINGS])

    wait(z_out.at[pl.ds(0, 15)], send_sem.at[TO_LINES])

    @pl.when(from_core != core)
    def _():
        wait(z_out.at[15], send_sem.at[TO_LINES])

    wait(n_send, send_sem.at[NEXT_ROW])
    wait(r_all.at[pl.ds(0, 7)], send_sem.at[REDUCED])
    for step in range(4):
        wait(y_all.at[step, pl.ds(0, 7)], send_sem.at[LATITUDE + step])
    wait(zb_recv.at[pl.ds(0, 15)], send_sem.at[BACK_COLUMNS])
    base = (zl - 2 * core + 2) % 4

    @pl.when(base >= 2)
    def _():
        wait(zb_recv.at[15], send_sem.at[BACK_COLUMNS])

    wait(r_recv, send_sem.at[BACK_ROWS])


def per_device(increment, deviations, diffuse_x, diffuse_y, diffuse_z, sea_mask):
    vmem = lambda *shape: pltpu.VMEM(shape, F32)
    shape = increment.shape
    plane = diffuse_x.shape
    return pl.pallas_call(
        kernel,
        out_shape=jax.ShapeDtypeStruct(shape, F32),
        in_specs=[pl.BlockSpec(memory_space=pl.ANY)] * 6,
        out_specs=pl.BlockSpec(memory_space=pltpu.VMEM),
        scratch_shapes=[
            vmem(*shape), vmem(*shape), vmem(*plane), vmem(*plane), vmem(*plane), pltpu.VMEM(plane, jnp.int32),
            vmem(2, 2, 64, 128),
            vmem(2, 4, 2, 2, 16, 128), vmem(8, 2, 2, 16, 128), vmem(2, 16, 16, 128), vmem(16, 16, 128),
            vmem(256, 128), vmem(2, 2, 64, 128), vmem(2, 256, 128), vmem(16, 128), vmem(16, 128),
            vmem(11, 2, 256, 128), vmem(256, 128), vmem(5, 16, 16, 128), vmem(8, 3, 16, 128), vmem(2, 8, 16, 128),
            vmem(4, 8, 32, 128), vmem(256, 128), vmem(16, 16, 128), vmem(16, 16, 128), vmem(2, 2, 64, 128),
            pltpu.SemaphoreType.DMA((6,)), pltpu.SemaphoreType.DMA((11,)), pltpu.SemaphoreType.DMA((11,)),
        ],
        compiler_params=pltpu.CompilerParams(
            collective_id=0, has_side_effects=True, vmem_limit_bytes=60 * 1024 * 1024
        ),
        name="covariance",
    )(increment, deviations, diffuse_x, diffuse_y, diffuse_z, sea_mask)


def solution(mesh):
    in_specs = (
        P(None, "lev", "lat", None),
        P(None, "lev", "lat", None),
        P("lev", "lat", None),
        P("lev", "lat", None),
        P("lev", "lat", None),
        P("lev", "lat", None),
    )
    out_specs = P(None, "lev", "lat", None)
    return jax.shard_map(
        per_device, mesh=mesh, in_specs=in_specs, out_specs=out_specs, check_vma=False
    )
```

```python
import math

import jax
import jax.numpy as jnp
from jax import lax
from jax.experimental import pallas as pl
from jax.experimental.pallas import tpu as pltpu
from jax.sharding import PartitionSpec as P

MESH = pl.DeviceIdType.MESH
F32 = jnp.float32
LEVELS, HALF, TILES, BLOCK, ROWS = 16, 1024, 8, 16, 128
STRIDES = (1, 2, 4, 8, 16, 32, 64, 128, 256, 512, 1024)
TO_COLUMNS, TO_LINES, COUPLE_X, COUPLE_Y, NEXT_ROW, REDUCED, WEIGHTED = range(7)
LATITUDE_A, LATITUDE_B, LATITUDE_C, BACK_COLUMNS, BACK_ROWS = range(7, 12)


def swap_halves(tile):
    return pltpu.roll(tile, 4, 0)


def from_west(tiles, stride, lane):
    if stride >= 128:
        k = stride // 128
        return [tiles[j - k] if j >= k else swap_halves(tiles[TILES + j - k]) for j in range(TILES)]
    turned = [pltpu.roll(tile, stride, 1) for tile in tiles]
    carry = [swap_halves(turned[-1])] + turned[:-1]
    return [jnp.where(lane < stride, c, t) for c, t in zip(carry, turned)]


def from_east(tiles, stride, lane):
    if stride >= 128:
        k = stride // 128
        return [tiles[j + k] if j + k < TILES else swap_halves(tiles[j + k - TILES]) for j in range(TILES)]
    turned = [pltpu.roll(tile, 128 - stride, 1) for tile in tiles]
    carry = turned[1:] + [swap_halves(turned[0])]
    return [jnp.where(lane >= 128 - stride, c, t) for c, t in zip(carry, turned)]


def paired(rows):
    return jnp.concatenate([rows[:, :HALF], rows[:, HALF:]], axis=0)


def tiles_of(wide):
    return [wide[:, 128 * j : 128 * (j + 1)] for j in range(TILES)]


def kernel(
    inc_hbm, dev_hbm, dx_hbm, dy_hbm, dz_hbm, sea_hbm, out_ref,
    inc, dev, dx, dy, dz, mask, scale,
    z_send, z_recv, z_factor, z_out, g_recv, cx_send, cx_recv, cy_send, cy_recv, n_send, n_recv,
    x_factor, x_last, y_factor, r_all, w_all, inverse, y_all, f_all, grid, zb_recv, zb_out, r_recv,
    in_sem, send_sem, recv_sem,
):
    lat, lev = lax.axis_index("lat"), lax.axis_index("lev")
    y, zl, core = lat // 8, (lat // 2) % 4, lat % 2
    x, zh = lev // 2, lev % 2
    mine = y * 2 + core
    lane = lax.broadcasted_iota(jnp.int32, (8, 128), 1)
    sublane = lax.broadcasted_iota(jnp.int32, (8, 128), 0)

    def at(y_, zl_, core_, x_, zh_):
        return {"lat": y_ * 8 + zl_ * 2 + core_, "lev": x_ * 2 + zh_}

    def send(src, dst, phase, target):
        pltpu.make_async_remote_copy(
            src_ref=src, dst_ref=dst, send_sem=send_sem.at[phase], recv_sem=recv_sem.at[phase],
            device_id=target, device_id_type=MESH,
        ).start()

    def send_or_keep(src, dst, phase, target, here):
        @pl.when(here)
        def _():
            pltpu.make_async_copy(src, dst, recv_sem.at[phase]).start()

        @pl.when(jnp.logical_not(here))
        def _():
            send(src, dst, phase, target)

    def wait(ref, sem):
        pltpu.make_async_copy(ref, ref, sem).wait()

    loads = [
        pltpu.make_async_copy(src, dst, in_sem.at[i])
        for i, (src, dst) in enumerate(
            [(sea_hbm, mask), (dev_hbm, dev), (inc_hbm, inc), (dz_hbm, dz), (dx_hbm, dx), (dy_hbm, dy)]
        )
    ]
    for load in loads:
        load.start()

    zf = (zl + 2) % 4
    greeted = [at(y, zf, core, (x + a) % 4, (zh + b) % 2) for a in (2, 1, 3, 0) for b in (0, 1)]
    greeted += [
        at(y, (zl + a) % 4, (core + d) % 2, x, (zh + b) % 2)
        for a in range(4) for b in range(2) for d in range(2)
        if (a, b, d) != (0, 0, 0) and (a, d) != (2, 0)
    ]
    greeted += [at((y + a) % 4, zl, d, x, zh) for a in (2, 1, 3) for d in range(2)]
    barrier = pltpu.get_barrier_semaphore()
    for target in greeted:
        pl.semaphore_signal(barrier, inc=1, device_id=target, device_id_type=MESH)

    for load in loads[:4]:
        load.wait()
    sea = [paired(mask[l]).astype(F32) for l in range(2)]
    for l in range(2):
        couple = tiles_of(paired(dz[l]) * sea[l])
        for t in range(2):
            factor = paired(dev[t, l]) * sea[l]
            state = tiles_of(factor * paired(inc[t, l]))
            factor = tiles_of(factor)
            for j in range(TILES):
                scale[t, l, 8 * j : 8 * j + 8, :] = factor[j]
                spot = pl.ds(8 * (j % 2), 8)
                z_send[t, j // 2, 0, l, spot, :] = state[j]
                z_send[t, j // 2, 1, l, spot, :] = couple[j]
    for load in loads[4:]:
        load.wait()
    for l in range(2):
        sea_tiles = tiles_of(sea[l])
        west = from_west(sea_tiles, 1, lane)
        west[0] = jnp.where((lane == 0) & (sublane < 4), 0.0, west[0])
        couple_x, couple_y = tiles_of(paired(dx[l])), tiles_of(paired(dy[l]))
        for j in range(TILES):
            cx_send[l, 8 * j : 8 * j + 8, :] = couple_x[j] * sea_tiles[j] * west[j]
            cy_send[l, 8 * j : 8 * j + 8, :] = couple_y[j] * sea_tiles[j]

    pl.semaphore_wait(barrier, len(greeted))

    for a in (2, 1, 3, 0):
        j = (x + a) % 4
        for t in range(2):
            send(z_send.at[t, j], z_recv.at[lev], TO_COLUMNS, at(y, zf, core, j, t))
    part = (zl % 2) * 2 + core
    lines_core = zl // 2
    for c_send, c_recv, phase in ((cy_send, cy_recv, COUPLE_Y), (cx_send, cx_recv, COUPLE_X)):
        for l in range(2):
            zt = 2 * zh + l
            for b in (1, 0):
                target = at(y, zt, lines_core, x, (zh + b) % 2)
                src, dst = c_send.at[l], c_recv.at[pl.ds(pl.multiple_of(part * 64, 64), 64)]
                if b == 0:
                    send_or_keep(src, dst, phase, target, (zl == zt) & (core == lines_core))
                else:
                    send(src, dst, phase, target)

    def solve_levels(take, put):
        upper, lower = take(0), take(15)
        held = {0: upper, 15: lower}
        for k in range(7):
            held[k + 1] = take(k + 1) + z_factor[0, k] * held[k]
            held[14 - k] = take(14 - k) + z_factor[0, 15 - k] * held[15 - k]
        solved = z_factor[1, 8] * (held[8] + z_factor[0, 7] * held[7])
        put(8, solved)
        up = down = solved
        for k in range(8):
            up = z_factor[1, 7 - k] * held[7 - k] + z_factor[0, 7 - k] * up
            put(7 - k, up)
            if k < 7:
                down = z_factor[1, 9 + k] * held[9 + k] + z_factor[0, 9 + k] * down
                put(9 + k, down)

    wait(z_recv, recv_sem.at[TO_COLUMNS])
    upper = lower = jnp.ones((16, 128), F32)
    for k in range(8):
        c_up = z_recv[(k + 1) // 2, 1, (k + 1) % 2]
        inv = 1.0 / (upper + c_up)
        z_factor[0, k] = c_up * inv
        z_factor[1, k] = inv
        upper = 1.0 + c_up * inv * upper
        if k < 7:
            c_low = z_recv[(15 - k) // 2, 1, (15 - k) % 2]
            inv = 1.0 / (lower + c_low)
            z_factor[0, 15 - k] = c_low * inv
            z_factor[1, 15 - k] = inv
            lower = 1.0 + c_low * inv * lower
    z_factor[1, 8] = 1.0 / (upper + (lower - 1.0))

    def put_first(k, value):
        z_out[k] = value

    solve_levels(lambda k: z_recv[k // 2, 0, k % 2], put_first)

    from_core = zf // 2
    from_part = (zf % 2) * 2 + core
    for a in (2, 1, 3, 0):
        for b in (3, 1, 2, 0):
            x_, zl_ = (x + a) % 4, (zl + b) % 4
            src = z_out.at[x_ * 4 + zl_]
            dst = g_recv.at[pl.ds(pl.multiple_of(from_part * 64 + x * 16, 16), 16)]
            target = at(y, zl_, from_core, x_, zh)
            if a == 0 and b == 0:
                send_or_keep(src, dst, TO_LINES, target, from_core == core)
            else:
                send(src, dst, TO_LINES, target)

    wait(cy_recv, recv_sem.at[COUPLE_Y])

    def row_at(i, half):
        return pl.ds((i // 4) * 64 + (i % 4) + 32 * half, 8, stride=4)

    for half in range(2):
        n_send[8 * half : 8 * half + 8, :] = cy_recv[row_at(0, half), :]
    before = (mine + 7) % 8
    send(n_send, n_recv, NEXT_ROW, at(before // 2, zl, before % 2, x, zh))

    ring = []
    for k in (4, 5, 3, 2, 6, 7, 1):
        block = (mine + k) % 8
        ring.append(at(block // 2, zl, block % 2, x, zh))

    row = (mine * BLOCK + lax.broadcasted_iota(jnp.int32, (BLOCK, 128), 0)).astype(F32)
    weight = jnp.cos((-78.0 + 166.0 * (row + 0.5) / ROWS) * (math.pi / 180.0))
    inner = range(1, BLOCK)

    def total(terms):
        while len(terms) > 1:
            terms = [sum(terms[i : i + 2][1:], terms[i]) for i in range(0, len(terms), 2)]
        return terms[0]

    def solve_inner(rows, spot):
        here, held = None, [None] * BLOCK
        for i in inner:
            here = rows[i] if i == 1 else rows[i] + y_factor[0, i - 1, spot, :] * here
            held[i] = y_factor[1, i, spot, :] * here
        for i in range(BLOCK - 2, 0, -1):
            held[i] = held[i] + y_factor[0, i, spot, :] * held[i + 1]
        return held

    wait(n_recv, recv_sem.at[NEXT_ROW])
    for half in range(2):
        spot = pl.ds(8 * half, 8)
        faces = [cy_recv[row_at(i, half), :] for i in range(BLOCK)]
        north = jnp.where(mine < 7, n_recv[spot, :], 0.0)
        couple = [None] + [
            jnp.where(faces[i - 1] > 0.0, faces[i] if i < BLOCK else north, 0.0) for i in range(1, BLOCK + 1)
        ]
        ground = jnp.ones((8, 128), F32)
        own, link = jnp.ones((8, 128), F32), couple[1]
        to_own, to_next = [None] * BLOCK, [None] * BLOCK
        for i in inner:
            inv = 1.0 / (ground + (link + couple[i + 1]))
            to_own[i], to_next[i] = link * inv, couple[i + 1] * inv
            y_factor[0, i, spot, :] = to_next[i]
            y_factor[1, i, spot, :] = inv
            own = own + to_own[i] * ground
            link = to_own[i] * couple[i + 1]
            beyond = to_next[i] * ground
            ground = 1.0 + beyond
        r_all[mine, 0, spot, :] = own
        r_all[mine, 1, spot, :] = beyond
        r_all[mine, 2, spot, :] = link
        left, right = to_own[15], to_next[15]
        y_factor[2, 15, spot, :] = left
        y_factor[3, 15, spot, :] = right
        for i in range(BLOCK - 2, 0, -1):
            left = to_own[i] + to_next[i] * left
            right = to_next[i] * right
            y_factor[2, i, spot, :] = left
            y_factor[3, i, spot, :] = right
    for target in ring:
        send(r_all.at[mine], r_all.at[mine], REDUCED, target)

    for half in range(2):
        spot = pl.ds(8 * half, 8)
        sides = [[None] + [y_factor[2 + k, i, spot, :] for i in inner] for k in range(2)]
        loaded = [[None] + [side[i] * weight[i : i + 1, :] for i in inner] for side in sides]
        w_all[mine, 0, spot, :] = weight[0:1, :] + total([sides[0][i] * loaded[0][i] for i in inner])
        w_all[mine, 1, spot, :] = total([sides[0][i] * loaded[1][i] for i in inner])
        w_all[mine, 2, spot, :] = total([sides[1][i] * loaded[1][i] for i in inner])
        for k in range(2):
            twice = solve_inner(loaded[k], spot)
            for i in inner:
                y_factor[4 + k, i, spot, :] = twice[i]

    wait(cx_recv, recv_sem.at[COUPLE_X])

    def bases():
        return [64 * part_ for part_ in range(4)]

    k = [[cx_recv[base + 8 * j : base + 8 * j + 8, :] for j in range(TILES)] for base in bases()]
    e = [[jnp.ones((8, 128), F32)] * TILES for _ in bases()]
    for i, stride in enumerate(STRIDES):
        for g, base in enumerate(bases()):
            k_east = from_east(k[g], stride, lane)
            inv = [1.0 / (a + (b + c)) for a, b, c in zip(e[g], k[g], k_east)]
            plus = [a * b for a, b in zip(k_east, inv)]
            minus = [a * b for a, b in zip(k[g], inv)]
            for j in range(TILES):
                x_factor[i, 0, base + 8 * j : base + 8 * j + 8, :] = plus[j]
                x_factor[i, 1, base + 8 * j : base + 8 * j + 8, :] = minus[j]
            west = from_west([a * b for a, b in zip(plus, e[g])], stride, lane)
            east = from_east([a * b for a, b in zip(minus, e[g])], stride, lane)
            k[g] = from_west([a * b for a, b in zip(plus, k[g])], stride, lane)
            e[g] = [a + (b + c) for a, b, c in zip(e[g], west, east)]
    for g, base in enumerate(bases()):
        for j in range(TILES):
            x_last[base + 8 * j : base + 8 * j + 8, :] = 1.0 / e[g][j]

    def longitude_solve(source):
        r = [[source[base + 8 * j : base + 8 * j + 8, :] for j in range(TILES)] for base in bases()]
        for i, stride in enumerate(STRIDES):
            for g, base in enumerate(bases()):
                plus = [x_factor[i, 0, base + 8 * j : base + 8 * j + 8, :] * r[g][j] for j in range(TILES)]
                minus = [x_factor[i, 1, base + 8 * j : base + 8 * j + 8, :] * r[g][j] for j in range(TILES)]
                west, east = from_west(plus, stride, lane), from_east(minus, stride, lane)
                r[g] = [a + (b + c) for a, b, c in zip(r[g], west, east)]
        for g, base in enumerate(bases()):
            for j in range(TILES):
                grid[base + 8 * j : base + 8 * j + 8, :] = r[g][j] * x_last[base + 8 * j : base + 8 * j + 8, :]

    def reduced_inverse():
        for half in range(2):
            spot = pl.ds(8 * half, 8)
            ground = [r_all[b, 0, spot, :] for b in range(8)]
            for b in range(1, 8):
                ground[b] = ground[b] + r_all[b - 1, 1, spot, :]
            link = [r_all[b, 2, spot, :] for b in range(7)]
            below, above = [ground[0]], [None] * 7 + [jnp.zeros((8, 128), F32)]
            north, south = [None] * 8, [None] * 8
            for b in range(7):
                inv = 1.0 / (below[b] + link[b])
                north[b] = link[b] * inv
                inverse[4, b, spot, :] = north[b]
                inverse[5, b, spot, :] = inv
                below.append(ground[b + 1] + north[b] * below[b])
            inverse[5, 7, spot, :] = 1.0 / below[7]
            for b in range(7, 0, -1):
                whole = ground[b] + above[b]
                south[b] = link[b - 1] / (whole + link[b - 1])
                above[b - 1] = south[b] * whole
            for which in range(2):
                spike = mine + which
                row_ = [None] * 8
                here = jnp.zeros((8, 128), F32)
                for b in range(7, -1, -1):
                    moved = here if b == 7 else north[b] * here
                    here = jnp.where(spike == b, 1.0 / (below[b] + above[b]), moved)
                    row_[b] = here
                here = jnp.zeros((8, 128), F32)
                for b in range(8):
                    moved = here if b == 0 else south[b] * here
                    here = jnp.where(spike < b, moved, row_[b])
                    inverse[which, b, spot, :] = here

    def weighted_inverse():
        for half in range(2):
            spot = pl.ds(8 * half, 8)
            middle = [w_all[b, 0, spot, :] for b in range(8)]
            for b in range(1, 8):
                middle[b] = middle[b] + w_all[b - 1, 2, spot, :]
            beside = [w_all[b, 1, spot, :] for b in range(7)]
            for which in range(2):
                g = [inverse[which, b, spot, :] for b in range(8)]
                right = [middle[b] * g[b] for b in range(8)]
                for b in range(7):
                    right[b] = right[b] + beside[b] * g[b + 1]
                    right[b + 1] = right[b + 1] + beside[b] * g[b]
                for b in range(7):
                    right[b + 1] = right[b + 1] + inverse[4, b, spot, :] * right[b]
                here = inverse[5, 7, spot, :] * right[7]
                inverse[2 + which, 7, spot, :] = here
                for b in range(6, -1, -1):
                    here = inverse[5, b, spot, :] * right[b] + inverse[4, b, spot, :] * here
                    inverse[2 + which, b, spot, :] = here

    def rows_of(half):
        return [grid[row_at(i, half), :] for i in range(BLOCK)]

    def put_rows(half, rows):
        for i in range(BLOCK):
            grid[row_at(i, half), :] = rows[i]

    def gathered(everyone, first, half):
        values = [everyone[b, pl.ds(16 * first + 8 * half, 8), :] for b in range(8)]
        for b in range(1, 8):
            values[b] = values[b] + everyone[b - 1, pl.ds(16 * (first + 1) + 8 * half, 8), :]
        return values

    def applied(which, values, spot):
        return [inverse[which, b, spot, :] * values[b] for b in range(8)]

    def tell(everyone, phase):
        for target in ring:
            send(everyone.at[mine], everyone.at[mine], phase, target)

    def latitude_solve(everyone, phase, behind=None, between=None):
        inside = []
        for half in range(2):
            spot = pl.ds(8 * half, 8)
            rows = rows_of(half)
            own = total([rows[0]] + [y_factor[2, i, spot, :] * rows[i] for i in inner])
            beyond = total([y_factor[3, i, spot, :] * rows[i] for i in inner])
            everyone[mine, spot, :] = own
            everyone[mine, pl.ds(16 + 8 * half, 8), :] = beyond
        tell(everyone, phase)
        if behind is not None:
            behind()
        for half in range(2):
            inside.append(solve_inner(rows_of(half), pl.ds(8 * half, 8)))
        if between is not None:
            between()
        wait(everyone.at[pl.ds(0, 7)], recv_sem.at[phase])
        for half in range(2):
            spot = pl.ds(8 * half, 8)
            right = gathered(everyone, 0, half)
            first, last = (total(applied(which, right, spot)) for which in range(2))
            put_rows(half, [first] + [
                inside[half][i] + (y_factor[2, i, spot, :] * first + y_factor[3, i, spot, :] * last) for i in inner
            ])

    def latitude_pair(everyone, phase):
        inside = []
        for half in range(2):
            spot = pl.ds(8 * half, 8)
            rows = rows_of(half)
            for k in range(4):
                terms = [y_factor[2 + k, i, spot, :] * rows[i] for i in inner]
                everyone[mine, pl.ds(16 * k + 8 * half, 8), :] = total(([rows[0]] if k == 0 else []) + terms)
        tell(everyone, phase)
        for half in range(2):
            spot = pl.ds(8 * half, 8)
            once = solve_inner(rows_of(half), spot)
            inside.append(solve_inner([None] + [once[i] * weight[i : i + 1, :] for i in inner], spot))
        wait(w_all.at[pl.ds(0, 7)], recv_sem.at[WEIGHTED])
        weighted_inverse()
        wait(everyone.at[pl.ds(0, 7)], recv_sem.at[phase])
        for half in range(2):
            spot = pl.ds(8 * half, 8)
            right, more = gathered(everyone, 0, half), gathered(everyone, 2, half)
            ends = [total(applied(which, right, spot)) for which in range(2)]
            ends += [total(applied(2 + k, right, spot) + applied(k, more, spot)) for k in range(2)]
            put_rows(half, [ends[2]] + [
                inside[half][i]
                + (y_factor[4, i, spot, :] * ends[0] + y_factor[5, i, spot, :] * ends[1])
                + (y_factor[2, i, spot, :] * ends[2] + y_factor[3, i, spot, :] * ends[3])
                for i in inner
            ])

    def first_between():
        wait(r_all.at[pl.ds(0, 7)], recv_sem.at[REDUCED])
        reduced_inverse()

    wait(g_recv, recv_sem.at[TO_LINES])
    longitude_solve(g_recv)
    latitude_solve(y_all.at[0], LATITUDE_A, lambda: tell(w_all, WEIGHTED), first_between)
    longitude_solve(grid)
    latitude_pair(f_all, LATITUDE_B)
    longitude_solve(grid)
    latitude_solve(y_all.at[1], LATITUDE_C)
    longitude_solve(grid)

    level = x * 4 + zl
    for a in (2, 1, 3, 0):
        x_ = (x + a) % 4
        for b in range(4):
            zl_, core_ = (2 * core + b // 2 + 2) % 4, b % 2
            src = grid.at[pl.ds(pl.multiple_of(b * 64 + x_ * 16, 16), 16)]
            target = at(y, zl_, core_, x_, zh)
            if a == 0:
                send_or_keep(src, zb_recv.at[level], BACK_COLUMNS, target, (zl_ == zl) & (core_ == core))
            else:
                send(src, zb_recv.at[level], BACK_COLUMNS, target)
    wait(zb_recv, recv_sem.at[BACK_COLUMNS])

    def put_last(k, value):
        zb_out[k] = value

    solve_levels(lambda k: zb_recv[k], put_last)
    for a in (2, 1, 3, 0):
        for b in range(2):
            x_ = (x + a) % 4
            src = zb_out.at[pl.ds(x_ * 4 + b * 2, 2)]
            dst = r_recv.at[zh, :, pl.ds(pl.multiple_of(x * 16, 16), 16)]
            send(src, dst, BACK_ROWS, at(y, zf, core, x_, b))
    wait(r_recv, recv_sem.at[BACK_ROWS])
    for t in range(2):
        for l in range(2):
            for j in range(TILES):
                spot = pl.ds(8 * j, 8)
                tile = scale[t, l, spot, :] * r_recv[t, l, spot, :]
                out_ref[t, l, :, 128 * j : 128 * j + 128] = tile[:4]
                out_ref[t, l, :, HALF + 128 * j : HALF + 128 * j + 128] = tile[4:]

    wait(z_send.at[:, :, :, :], send_sem.at[TO_COLUMNS])
    for c_send, phase in ((cy_send, COUPLE_Y), (cx_send, COUPLE_X)):
        for l in range(2):
            wait(c_send.at[l], send_sem.at[phase])

            @pl.when(jnp.logical_not((zl == 2 * zh + l) & (core == lines_core)))
            def _():
                wait(c_send.at[l], send_sem.at[phase])

    wait(z_out.at[pl.ds(0, 15)], send_sem.at[TO_LINES])

    @pl.when(from_core != core)
    def _():
        wait(z_out.at[15], send_sem.at[TO_LINES])

    wait(n_send, send_sem.at[NEXT_ROW])
    wait(r_all.at[pl.ds(0, 7)], send_sem.at[REDUCED])
    wait(w_all.at[pl.ds(0, 7)], send_sem.at[WEIGHTED])
    wait(y_all.at[0, pl.ds(0, 7)], send_sem.at[LATITUDE_A])
    wait(f_all.at[pl.ds(0, 7)], send_sem.at[LATITUDE_B])
    wait(y_all.at[1, pl.ds(0, 7)], send_sem.at[LATITUDE_C])
    wait(zb_recv.at[pl.ds(0, 15)], send_sem.at[BACK_COLUMNS])
    base = (zl - 2 * core + 2) % 4

    @pl.when(base >= 2)
    def _():
        wait(zb_recv.at[15], send_sem.at[BACK_COLUMNS])

    wait(r_recv, send_sem.at[BACK_ROWS])


def per_device(increment, deviations, diffuse_x, diffuse_y, diffuse_z, sea_mask):
    vmem = lambda *shape: pltpu.VMEM(shape, F32)
    shape = increment.shape
    plane = diffuse_x.shape
    return pl.pallas_call(
        kernel,
        out_shape=jax.ShapeDtypeStruct(shape, F32),
        in_specs=[pl.BlockSpec(memory_space=pl.ANY)] * 6,
        out_specs=pl.BlockSpec(memory_space=pltpu.VMEM),
        scratch_shapes=[
            vmem(*shape), vmem(*shape), vmem(*plane), vmem(*plane), vmem(*plane), pltpu.VMEM(plane, jnp.int32),
            vmem(2, 2, 64, 128),
            vmem(2, 4, 2, 2, 16, 128), vmem(8, 2, 2, 16, 128), vmem(2, 16, 16, 128), vmem(16, 16, 128),
            vmem(256, 128), vmem(2, 64, 128), vmem(256, 128), vmem(2, 64, 128), vmem(256, 128), vmem(16, 128), vmem(16, 128),
            vmem(11, 2, 256, 128), vmem(256, 128), vmem(6, 16, 16, 128), vmem(8, 3, 16, 128), vmem(8, 3, 16, 128),
            vmem(6, 8, 16, 128), vmem(2, 8, 32, 128), vmem(8, 64, 128), vmem(256, 128), vmem(16, 16, 128), vmem(16, 16, 128), vmem(2, 2, 64, 128),
            pltpu.SemaphoreType.DMA((6,)), pltpu.SemaphoreType.DMA((12,)), pltpu.SemaphoreType.DMA((12,)),
        ],
        compiler_params=pltpu.CompilerParams(
            collective_id=0, has_side_effects=True, vmem_limit_bytes=60 * 1024 * 1024
        ),
        name="covariance",
    )(increment, deviations, diffuse_x, diffuse_y, diffuse_z, sea_mask)


def solution(mesh):
    in_specs = (
        P(None, "lev", "lat", None),
        P(None, "lev", "lat", None),
        P("lev", "lat", None),
        P("lev", "lat", None),
        P("lev", "lat", None),
        P("lev", "lat", None),
    )
    out_specs = P(None, "lev", "lat", None)
    return jax.shard_map(
        per_device, mesh=mesh, in_specs=in_specs, out_specs=out_specs, check_vma=False
    )
```

```python
import math

import jax
import jax.numpy as jnp
from jax import lax
from jax.experimental import pallas as pl
from jax.experimental.pallas import tpu as pltpu
from jax.sharding import PartitionSpec as P

MESH = pl.DeviceIdType.MESH
F32 = jnp.float32
LEVELS, HALF, TILES, BLOCK, ROWS = 16, 1024, 8, 16, 128
STRIDES = (1, 2, 4, 8, 16, 32, 64, 128, 256, 512, 1024)
TO_COLUMNS, TO_LINES, COUPLE_X, COUPLE_Y, NEXT_ROW, REDUCED, WEIGHTED = range(7)
LATITUDE_A, LATITUDE_B, LATITUDE_C, BACK_COLUMNS, BACK_ROWS = range(7, 12)


def swap_halves(tile):
    return pltpu.roll(tile, 4, 0)


def from_west(tiles, stride, lane):
    if stride >= 128:
        k = stride // 128
        return [tiles[j - k] if j >= k else swap_halves(tiles[TILES + j - k]) for j in range(TILES)]
    turned = [pltpu.roll(tile, stride, 1) for tile in tiles]
    carry = [swap_halves(turned[-1])] + turned[:-1]
    return [jnp.where(lane < stride, c, t) for c, t in zip(carry, turned)]


def from_east(tiles, stride, lane):
    if stride >= 128:
        k = stride // 128
        return [tiles[j + k] if j + k < TILES else swap_halves(tiles[j + k - TILES]) for j in range(TILES)]
    turned = [pltpu.roll(tile, 128 - stride, 1) for tile in tiles]
    carry = turned[1:] + [swap_halves(turned[0])]
    return [jnp.where(lane >= 128 - stride, c, t) for c, t in zip(carry, turned)]


def paired(rows):
    return jnp.concatenate([rows[:, :HALF], rows[:, HALF:]], axis=0)


def tiles_of(wide):
    return [wide[:, 128 * j : 128 * (j + 1)] for j in range(TILES)]


def kernel(
    inc_hbm, dev_hbm, dx_hbm, dy_hbm, dz_hbm, sea_hbm, out_ref,
    inc, dev, dx, dy, dz, mask, scale,
    z_send, z_recv, z_factor, z_out, g_recv, cx_send, cx_recv, cy_send, cy_recv, n_send, n_recv,
    x_factor, x_last, y_factor, r_all, w_all, inverse, y_all, f_all, grid, zb_recv, zb_out, r_recv,
    in_sem, send_sem, recv_sem,
):
    lat, lev = lax.axis_index("lat"), lax.axis_index("lev")
    y, zl, core = lat // 8, (lat // 2) % 4, lat % 2
    x, zh = lev // 2, lev % 2
    mine = y * 2 + core
    lane = lax.broadcasted_iota(jnp.int32, (8, 128), 1)
    sublane = lax.broadcasted_iota(jnp.int32, (8, 128), 0)

    def at(y_, zl_, core_, x_, zh_):
        return {"lat": y_ * 8 + zl_ * 2 + core_, "lev": x_ * 2 + zh_}

    def level_at(x_, zl_):
        inner = ((zl_ + 1) // 2) % 2
        return x_ * 4 + 2 * ((zh + 1 + inner) % 2) + zl_ // 2

    def send(src, dst, phase, target):
        pltpu.make_async_remote_copy(
            src_ref=src, dst_ref=dst, send_sem=send_sem.at[phase], recv_sem=recv_sem.at[phase],
            device_id=target, device_id_type=MESH,
        ).start()

    def send_or_keep(src, dst, phase, target, here):
        @pl.when(here)
        def _():
            pltpu.make_async_copy(src, dst, recv_sem.at[phase]).start()

        @pl.when(jnp.logical_not(here))
        def _():
            send(src, dst, phase, target)

    def wait(ref, sem):
        pltpu.make_async_copy(ref, ref, sem).wait()

    loads = [
        pltpu.make_async_copy(src, dst, in_sem.at[i])
        for i, (src, dst) in enumerate(
            [(sea_hbm, mask), (dev_hbm, dev), (inc_hbm, inc), (dz_hbm, dz), (dx_hbm, dx), (dy_hbm, dy)]
        )
    ]
    for load in loads:
        load.start()

    zf = (zl + 2) % 4
    greeted = [at(y, zf, core, (x + a) % 4, (zh + b) % 2) for a in (2, 1, 3, 0) for b in (0, 1)]
    greeted += [
        at(y, (zl + a) % 4, (core + d) % 2, x, (zh + b) % 2)
        for a in range(4) for b in range(2) for d in range(2)
        if (a, b, d) != (0, 0, 0) and (a, d) != (2, 0)
    ]
    greeted += [at((y + a) % 4, zl, d, x, zh) for a in (2, 1, 3) for d in range(2)]
    barrier = pltpu.get_barrier_semaphore()
    for target in greeted:
        pl.semaphore_signal(barrier, inc=1, device_id=target, device_id_type=MESH)

    for load in loads[:4]:
        load.wait()
    sea = [paired(mask[l]).astype(F32) for l in range(2)]
    for l in range(2):
        couple = tiles_of(paired(dz[l]) * sea[l])
        for t in range(2):
            factor = paired(dev[t, l]) * sea[l]
            state = tiles_of(factor * paired(inc[t, l]))
            factor = tiles_of(factor)
            for j in range(TILES):
                scale[t, l, 8 * j : 8 * j + 8, :] = factor[j]
                spot = pl.ds(8 * (j % 2), 8)
                z_send[t, j // 2, 0, l, spot, :] = state[j]
                z_send[t, j // 2, 1, l, spot, :] = couple[j]
    for load in loads[4:]:
        load.wait()
    for l in range(2):
        sea_tiles = tiles_of(sea[l])
        west = from_west(sea_tiles, 1, lane)
        west[0] = jnp.where((lane == 0) & (sublane < 4), 0.0, west[0])
        couple_x, couple_y = tiles_of(paired(dx[l])), tiles_of(paired(dy[l]))
        for j in range(TILES):
            cx_send[l, 8 * j : 8 * j + 8, :] = couple_x[j] * sea_tiles[j] * west[j]
            cy_send[l, 8 * j : 8 * j + 8, :] = couple_y[j] * sea_tiles[j]

    pl.semaphore_wait(barrier, len(greeted))

    for a in (2, 1, 3, 0):
        j = (x + a) % 4
        for t in range(2):
            send(z_send.at[t, j], z_recv.at[lev], TO_COLUMNS, at(y, zf, core, j, t))
    part = (zl % 2) * 2 + core
    lines_core = zl // 2
    for c_send, c_recv, phase in ((cy_send, cy_recv, COUPLE_Y), (cx_send, cx_recv, COUPLE_X)):
        for l in range(2):
            for b in (1, 0):
                zt = 3 * l if b else 1 + l
                target = at(y, zt, lines_core, x, (zh + b) % 2)
                src, dst = c_send.at[l], c_recv.at[pl.ds(pl.multiple_of(part * 64, 64), 64)]
                if b == 0:
                    send_or_keep(src, dst, phase, target, (zl == zt) & (core == lines_core))
                else:
                    send(src, dst, phase, target)

    def solve_levels(take, put):
        upper, lower = take(0), take(15)
        held = {0: upper, 15: lower}
        for k in range(7):
            held[k + 1] = take(k + 1) + z_factor[0, k] * held[k]
            held[14 - k] = take(14 - k) + z_factor[0, 15 - k] * held[15 - k]
        solved = z_factor[1, 8] * (held[8] + z_factor[0, 7] * held[7])
        put(8, solved)
        up = down = solved
        for k in range(8):
            up = z_factor[1, 7 - k] * held[7 - k] + z_factor[0, 7 - k] * up
            put(7 - k, up)
            if k < 7:
                down = z_factor[1, 9 + k] * held[9 + k] + z_factor[0, 9 + k] * down
                put(9 + k, down)

    wait(z_recv, recv_sem.at[TO_COLUMNS])
    upper = lower = jnp.ones((16, 128), F32)
    for k in range(8):
        c_up = z_recv[(k + 1) // 2, 1, (k + 1) % 2]
        inv = 1.0 / (upper + c_up)
        z_factor[0, k] = c_up * inv
        z_factor[1, k] = inv
        upper = 1.0 + c_up * inv * upper
        if k < 7:
            c_low = z_recv[(15 - k) // 2, 1, (15 - k) % 2]
            inv = 1.0 / (lower + c_low)
            z_factor[0, 15 - k] = c_low * inv
            z_factor[1, 15 - k] = inv
            lower = 1.0 + c_low * inv * lower
    z_factor[1, 8] = 1.0 / (upper + (lower - 1.0))

    def put_first(k, value):
        z_out[k] = value

    solve_levels(lambda k: z_recv[k // 2, 0, k % 2], put_first)

    from_core = zf // 2
    from_part = (zf % 2) * 2 + core
    for a in (2, 1, 3, 0):
        for b in (3, 1, 2, 0):
            x_, zl_ = (x + a) % 4, (zl + b) % 4
            src = z_out.at[level_at(x_, zl_)]
            dst = g_recv.at[pl.ds(pl.multiple_of(from_part * 64 + x * 16, 16), 16)]
            target = at(y, zl_, from_core, x_, zh)
            if a == 0 and b == 0:
                send_or_keep(src, dst, TO_LINES, target, from_core == core)
            else:
                send(src, dst, TO_LINES, target)

    wait(cy_recv, recv_sem.at[COUPLE_Y])

    def row_at(i, half):
        return pl.ds((i // 4) * 64 + (i % 4) + 32 * half, 8, stride=4)

    for half in range(2):
        n_send[8 * half : 8 * half + 8, :] = cy_recv[row_at(0, half), :]
    before = (mine + 7) % 8
    send(n_send, n_recv, NEXT_ROW, at(before // 2, zl, before % 2, x, zh))

    ring = []
    for k in (4, 5, 3, 2, 6, 7, 1):
        block = (mine + k) % 8
        ring.append(at(block // 2, zl, block % 2, x, zh))

    row = (mine * BLOCK + lax.broadcasted_iota(jnp.int32, (BLOCK, 128), 0)).astype(F32)
    weight = jnp.cos((-78.0 + 166.0 * (row + 0.5) / ROWS) * (math.pi / 180.0))
    inner = range(1, BLOCK)

    def total(terms):
        while len(terms) > 1:
            terms = [sum(terms[i : i + 2][1:], terms[i]) for i in range(0, len(terms), 2)]
        return terms[0]

    def solve_inner(rows, spot):
        here, held = None, [None] * BLOCK
        for i in inner:
            here = rows[i] if i == 1 else rows[i] + y_factor[0, i - 1, spot, :] * here
            held[i] = y_factor[1, i, spot, :] * here
        for i in range(BLOCK - 2, 0, -1):
            held[i] = held[i] + y_factor[0, i, spot, :] * held[i + 1]
        return held

    wait(n_recv, recv_sem.at[NEXT_ROW])
    for half in range(2):
        spot = pl.ds(8 * half, 8)
        faces = [cy_recv[row_at(i, half), :] for i in range(BLOCK)]
        north = jnp.where(mine < 7, n_recv[spot, :], 0.0)
        couple = [None] + [
            jnp.where(faces[i - 1] > 0.0, faces[i] if i < BLOCK else north, 0.0) for i in range(1, BLOCK + 1)
        ]
        ground = jnp.ones((8, 128), F32)
        own, link = jnp.ones((8, 128), F32), couple[1]
        to_own, to_next = [None] * BLOCK, [None] * BLOCK
        for i in inner:
            inv = 1.0 / (ground + (link + couple[i + 1]))
            to_own[i], to_next[i] = link * inv, couple[i + 1] * inv
            y_factor[0, i, spot, :] = to_next[i]
            y_factor[1, i, spot, :] = inv
            own = own + to_own[i] * ground
            link = to_own[i] * couple[i + 1]
            beyond = to_next[i] * ground
            ground = 1.0 + beyond
        r_all[mine, 0, spot, :] = own
        r_all[mine, 1, spot, :] = beyond
        r_all[mine, 2, spot, :] = link
        left, right = to_own[15], to_next[15]
        y_factor[2, 15, spot, :] = left
        y_factor[3, 15, spot, :] = right
        for i in range(BLOCK - 2, 0, -1):
            left = to_own[i] + to_next[i] * left
            right = to_next[i] * right
            y_factor[2, i, spot, :] = left
            y_factor[3, i, spot, :] = right
    for target in ring:
        send(r_all.at[mine], r_all.at[mine], REDUCED, target)

    wait(cx_recv, recv_sem.at[COUPLE_X])

    def bases():
        return [64 * part_ for part_ in range(4)]

    k = [[cx_recv[base + 8 * j : base + 8 * j + 8, :] for j in range(TILES)] for base in bases()]
    e = [[jnp.ones((8, 128), F32)] * TILES for _ in bases()]
    for i, stride in enumerate(STRIDES):
        for g, base in enumerate(bases()):
            k_east = from_east(k[g], stride, lane)
            inv = [1.0 / (a + (b + c)) for a, b, c in zip(e[g], k[g], k_east)]
            plus = [a * b for a, b in zip(k_east, inv)]
            minus = [a * b for a, b in zip(k[g], inv)]
            for j in range(TILES):
                x_factor[i, 0, base + 8 * j : base + 8 * j + 8, :] = plus[j]
                x_factor[i, 1, base + 8 * j : base + 8 * j + 8, :] = minus[j]
            west = from_west([a * b for a, b in zip(plus, e[g])], stride, lane)
            east = from_east([a * b for a, b in zip(minus, e[g])], stride, lane)
            k[g] = from_west([a * b for a, b in zip(plus, k[g])], stride, lane)
            e[g] = [a + (b + c) for a, b, c in zip(e[g], west, east)]
    for g, base in enumerate(bases()):
        for j in range(TILES):
            x_last[base + 8 * j : base + 8 * j + 8, :] = 1.0 / e[g][j]

    def longitude_solve(source):
        r = [[source[base + 8 * j : base + 8 * j + 8, :] for j in range(TILES)] for base in bases()]
        for i, stride in enumerate(STRIDES):
            for g, base in enumerate(bases()):
                plus = [x_factor[i, 0, base + 8 * j : base + 8 * j + 8, :] * r[g][j] for j in range(TILES)]
                minus = [x_factor[i, 1, base + 8 * j : base + 8 * j + 8, :] * r[g][j] for j in range(TILES)]
                west, east = from_west(plus, stride, lane), from_east(minus, stride, lane)
                r[g] = [a + (b + c) for a, b, c in zip(r[g], west, east)]
        for g, base in enumerate(bases()):
            for j in range(TILES):
                grid[base + 8 * j : base + 8 * j + 8, :] = r[g][j] * x_last[base + 8 * j : base + 8 * j + 8, :]

    def reduced_inverse():
        for half in range(2):
            spot = pl.ds(8 * half, 8)
            ground = [r_all[b, 0, spot, :] for b in range(8)]
            for b in range(1, 8):
                ground[b] = ground[b] + r_all[b - 1, 1, spot, :]
            link = [r_all[b, 2, spot, :] for b in range(7)]
            below, above = [ground[0]], [None] * 7 + [jnp.zeros((8, 128), F32)]
            north, south = [None] * 8, [None] * 8
            for b in range(7):
                inv = 1.0 / (below[b] + link[b])
                north[b] = link[b] * inv
                inverse[4, b, spot, :] = north[b]
                inverse[5, b, spot, :] = inv
                below.append(ground[b + 1] + north[b] * below[b])
            inverse[5, 7, spot, :] = 1.0 / below[7]
            for b in range(7, 0, -1):
                whole = ground[b] + above[b]
                south[b] = link[b - 1] / (whole + link[b - 1])
                above[b - 1] = south[b] * whole
            for which in range(2):
                spike = mine + which
                row_ = [None] * 8
                here = jnp.zeros((8, 128), F32)
                for b in range(7, -1, -1):
                    moved = here if b == 7 else north[b] * here
                    here = jnp.where(spike == b, 1.0 / (below[b] + above[b]), moved)
                    row_[b] = here
                here = jnp.zeros((8, 128), F32)
                for b in range(8):
                    moved = here if b == 0 else south[b] * here
                    here = jnp.where(spike < b, moved, row_[b])
                    inverse[which, b, spot, :] = here

    def weighted_inverse():
        for half in range(2):
            spot = pl.ds(8 * half, 8)
            middle = [w_all[b, 0, spot, :] for b in range(8)]
            for b in range(1, 8):
                middle[b] = middle[b] + w_all[b - 1, 2, spot, :]
            beside = [w_all[b, 1, spot, :] for b in range(7)]
            for which in range(2):
                g = [inverse[which, b, spot, :] for b in range(8)]
                right = [middle[b] * g[b] for b in range(8)]
                for b in range(7):
                    right[b] = right[b] + beside[b] * g[b + 1]
                    right[b + 1] = right[b + 1] + beside[b] * g[b]
                for b in range(7):
                    right[b + 1] = right[b + 1] + inverse[4, b, spot, :] * right[b]
                here = inverse[5, 7, spot, :] * right[7]
                inverse[2 + which, 7, spot, :] = here
                for b in range(6, -1, -1):
                    here = inverse[5, b, spot, :] * right[b] + inverse[4, b, spot, :] * here
                    inverse[2 + which, b, spot, :] = here

    def rows_of(half):
        return [grid[row_at(i, half), :] for i in range(BLOCK)]

    def put_rows(half, rows):
        for i in range(BLOCK):
            grid[row_at(i, half), :] = rows[i]

    def gathered(everyone, first, half):
        values = [everyone[b, pl.ds(16 * first + 8 * half, 8), :] for b in range(8)]
        for b in range(1, 8):
            values[b] = values[b] + everyone[b - 1, pl.ds(16 * (first + 1) + 8 * half, 8), :]
        return values

    def applied(which, values, spot):
        return [inverse[which, b, spot, :] * values[b] for b in range(8)]

    def tell(everyone, phase):
        for target in ring:
            send(everyone.at[mine], everyone.at[mine], phase, target)

    def latitude_solve(everyone, phase, behind=None, between=None):
        inside = []
        for half in range(2):
            spot = pl.ds(8 * half, 8)
            rows = rows_of(half)
            own = total([rows[0]] + [y_factor[2, i, spot, :] * rows[i] for i in inner])
            beyond = total([y_factor[3, i, spot, :] * rows[i] for i in inner])
            everyone[mine, spot, :] = own
            everyone[mine, pl.ds(16 + 8 * half, 8), :] = beyond
        tell(everyone, phase)
        if behind is not None:
            behind()
        for half in range(2):
            inside.append(solve_inner(rows_of(half), pl.ds(8 * half, 8)))
        if between is not None:
            between()
        wait(everyone.at[pl.ds(0, 7)], recv_sem.at[phase])
        for half in range(2):
            spot = pl.ds(8 * half, 8)
            right = gathered(everyone, 0, half)
            first, last = (total(applied(which, right, spot)) for which in range(2))
            put_rows(half, [first] + [
                inside[half][i] + (y_factor[2, i, spot, :] * first + y_factor[3, i, spot, :] * last) for i in inner
            ])

    def latitude_pair(everyone, phase):
        inside = []
        for half in range(2):
            spot = pl.ds(8 * half, 8)
            rows = rows_of(half)
            for k in range(4):
                terms = [y_factor[2 + k, i, spot, :] * rows[i] for i in inner]
                everyone[mine, pl.ds(16 * k + 8 * half, 8), :] = total(([rows[0]] if k == 0 else []) + terms)
        tell(everyone, phase)
        for half in range(2):
            spot = pl.ds(8 * half, 8)
            once = solve_inner(rows_of(half), spot)
            inside.append(solve_inner([None] + [once[i] * weight[i : i + 1, :] for i in inner], spot))
        wait(w_all.at[pl.ds(0, 7)], recv_sem.at[WEIGHTED])
        weighted_inverse()
        wait(everyone.at[pl.ds(0, 7)], recv_sem.at[phase])
        for half in range(2):
            spot = pl.ds(8 * half, 8)
            right, more = gathered(everyone, 0, half), gathered(everyone, 2, half)
            ends = [total(applied(which, right, spot)) for which in range(2)]
            ends += [total(applied(2 + k, right, spot) + applied(k, more, spot)) for k in range(2)]
            put_rows(half, [ends[2]] + [
                inside[half][i]
                + (y_factor[4, i, spot, :] * ends[0] + y_factor[5, i, spot, :] * ends[1])
                + (y_factor[2, i, spot, :] * ends[2] + y_factor[3, i, spot, :] * ends[3])
                for i in inner
            ])

    def weighted_block():
        for half in range(2):
            spot = pl.ds(8 * half, 8)
            sides = [[None] + [y_factor[2 + k, i, spot, :] for i in inner] for k in range(2)]
            loaded = [[None] + [side[i] * weight[i : i + 1, :] for i in inner] for side in sides]
            w_all[mine, 0, spot, :] = weight[0:1, :] + total([sides[0][i] * loaded[0][i] for i in inner])
            w_all[mine, 1, spot, :] = total([sides[0][i] * loaded[1][i] for i in inner])
            w_all[mine, 2, spot, :] = total([sides[1][i] * loaded[1][i] for i in inner])
            for k in range(2):
                twice = solve_inner(loaded[k], spot)
                for i in inner:
                    y_factor[4 + k, i, spot, :] = twice[i]
        tell(w_all, WEIGHTED)

    def first_between():
        wait(r_all.at[pl.ds(0, 7)], recv_sem.at[REDUCED])
        reduced_inverse()

    wait(g_recv, recv_sem.at[TO_LINES])
    longitude_solve(g_recv)
    latitude_solve(y_all.at[0], LATITUDE_A, weighted_block, first_between)
    longitude_solve(grid)
    latitude_pair(f_all, LATITUDE_B)
    longitude_solve(grid)
    latitude_solve(y_all.at[1], LATITUDE_C)
    longitude_solve(grid)

    level = level_at(x, zl)
    for a in (2, 1, 3, 0):
        x_ = (x + a) % 4
        for b in range(4):
            zl_, core_ = (2 * core + b // 2 + 2) % 4, b % 2
            src = grid.at[pl.ds(pl.multiple_of(b * 64 + x_ * 16, 16), 16)]
            target = at(y, zl_, core_, x_, zh)
            if a == 0:
                send_or_keep(src, zb_recv.at[level], BACK_COLUMNS, target, (zl_ == zl) & (core_ == core))
            else:
                send(src, zb_recv.at[level], BACK_COLUMNS, target)
    wait(zb_recv, recv_sem.at[BACK_COLUMNS])

    def put_last(k, value):
        zb_out[k] = value

    solve_levels(lambda k: zb_recv[k], put_last)
    for a in (2, 1, 3, 0):
        for b in range(2):
            x_ = (x + a) % 4
            src = zb_out.at[pl.ds(x_ * 4 + b * 2, 2)]
            dst = r_recv.at[zh, :, pl.ds(pl.multiple_of(x * 16, 16), 16)]
            send(src, dst, BACK_ROWS, at(y, zf, core, x_, b))
    wait(r_recv, recv_sem.at[BACK_ROWS])
    for t in range(2):
        for l in range(2):
            for j in range(TILES):
                spot = pl.ds(8 * j, 8)
                tile = scale[t, l, spot, :] * r_recv[t, l, spot, :]
                out_ref[t, l, :, 128 * j : 128 * j + 128] = tile[:4]
                out_ref[t, l, :, HALF + 128 * j : HALF + 128 * j + 128] = tile[4:]

    wait(z_send.at[:, :, :, :], send_sem.at[TO_COLUMNS])
    for c_send, phase in ((cy_send, COUPLE_Y), (cx_send, COUPLE_X)):
        for l in range(2):
            wait(c_send.at[l], send_sem.at[phase])

            @pl.when(jnp.logical_not((zl == 1 + l) & (core == lines_core)))
            def _():
                wait(c_send.at[l], send_sem.at[phase])

    wait(z_out.at[pl.ds(0, 15)], send_sem.at[TO_LINES])

    @pl.when(from_core != core)
    def _():
        wait(z_out.at[15], send_sem.at[TO_LINES])

    wait(n_send, send_sem.at[NEXT_ROW])
    wait(r_all.at[pl.ds(0, 7)], send_sem.at[REDUCED])
    wait(w_all.at[pl.ds(0, 7)], send_sem.at[WEIGHTED])
    wait(y_all.at[0, pl.ds(0, 7)], send_sem.at[LATITUDE_A])
    wait(f_all.at[pl.ds(0, 7)], send_sem.at[LATITUDE_B])
    wait(y_all.at[1, pl.ds(0, 7)], send_sem.at[LATITUDE_C])
    wait(zb_recv.at[pl.ds(0, 15)], send_sem.at[BACK_COLUMNS])
    base = (zl - 2 * core + 2) % 4

    @pl.when(base >= 2)
    def _():
        wait(zb_recv.at[15], send_sem.at[BACK_COLUMNS])

    wait(r_recv, send_sem.at[BACK_ROWS])


def per_device(increment, deviations, diffuse_x, diffuse_y, diffuse_z, sea_mask):
    vmem = lambda *shape: pltpu.VMEM(shape, F32)
    shape = increment.shape
    plane = diffuse_x.shape
    return pl.pallas_call(
        kernel,
        out_shape=jax.ShapeDtypeStruct(shape, F32),
        in_specs=[pl.BlockSpec(memory_space=pl.ANY)] * 6,
        out_specs=pl.BlockSpec(memory_space=pltpu.VMEM),
        scratch_shapes=[
            vmem(*shape), vmem(*shape), vmem(*plane), vmem(*plane), vmem(*plane), pltpu.VMEM(plane, jnp.int32),
            vmem(2, 2, 64, 128),
            vmem(2, 4, 2, 2, 16, 128), vmem(8, 2, 2, 16, 128), vmem(2, 16, 16, 128), vmem(16, 16, 128),
            vmem(256, 128), vmem(2, 64, 128), vmem(256, 128), vmem(2, 64, 128), vmem(256, 128), vmem(16, 128), vmem(16, 128),
            vmem(11, 2, 256, 128), vmem(256, 128), vmem(6, 16, 16, 128), vmem(8, 3, 16, 128), vmem(8, 3, 16, 128),
            vmem(6, 8, 16, 128), vmem(2, 8, 32, 128), vmem(8, 64, 128), vmem(256, 128), vmem(16, 16, 128), vmem(16, 16, 128), vmem(2, 2, 64, 128),
            pltpu.SemaphoreType.DMA((6,)), pltpu.SemaphoreType.DMA((12,)), pltpu.SemaphoreType.DMA((12,)),
        ],
        compiler_params=pltpu.CompilerParams(
            collective_id=0, has_side_effects=True, vmem_limit_bytes=60 * 1024 * 1024
        ),
        name="covariance",
    )(increment, deviations, diffuse_x, diffuse_y, diffuse_z, sea_mask)


def solution(mesh):
    in_specs = (
        P(None, "lev", "lat", None),
        P(None, "lev", "lat", None),
        P("lev", "lat", None),
        P("lev", "lat", None),
        P("lev", "lat", None),
        P("lev", "lat", None),
    )
    out_specs = P(None, "lev", "lat", None)
    return jax.shard_map(
        per_device, mesh=mesh, in_specs=in_specs, out_specs=out_specs, check_vma=False
    )
```

```python
import math

import jax
import jax.numpy as jnp
from jax import lax
from jax.experimental import pallas as pl
from jax.experimental.pallas import tpu as pltpu
from jax.sharding import PartitionSpec as P

MESH = pl.DeviceIdType.MESH
F32 = jnp.float32
LEVELS, HALF, TILES, BLOCK, ROWS = 16, 1024, 8, 16, 128
STRIDES = (1, 2, 4, 8, 16, 32, 64, 128, 256, 512, 1024)
TO_COLUMNS, TO_LINES, COUPLE_X, COUPLE_Y, NEXT_ROW, REDUCED, WEIGHTED = range(7)
LATITUDE_A, LATITUDE_B, LATITUDE_C, BACK_COLUMNS, BACK_ROWS = range(7, 12)


def swap_halves(tile):
    return pltpu.roll(tile, 4, 0)


def from_west(tiles, stride, lane):
    if stride >= 128:
        k = stride // 128
        return [tiles[j - k] if j >= k else swap_halves(tiles[TILES + j - k]) for j in range(TILES)]
    turned = [pltpu.roll(tile, stride, 1) for tile in tiles]
    carry = [swap_halves(turned[-1])] + turned[:-1]
    return [jnp.where(lane < stride, c, t) for c, t in zip(carry, turned)]


def from_east(tiles, stride, lane):
    if stride >= 128:
        k = stride // 128
        return [tiles[j + k] if j + k < TILES else swap_halves(tiles[j + k - TILES]) for j in range(TILES)]
    turned = [pltpu.roll(tile, 128 - stride, 1) for tile in tiles]
    carry = turned[1:] + [swap_halves(turned[0])]
    return [jnp.where(lane >= 128 - stride, c, t) for c, t in zip(carry, turned)]


def paired(rows):
    return jnp.concatenate([rows[:, :HALF], rows[:, HALF:]], axis=0)


def tiles_of(wide):
    return [wide[:, 128 * j : 128 * (j + 1)] for j in range(TILES)]


def kernel(
    inc_hbm, dev_hbm, dx_hbm, dy_hbm, dz_hbm, sea_hbm, out_ref,
    inc, dev, dx, dy, dz, mask, scale,
    z_send, z_recv, z_factor, z_out, g_recv, cx_send, cx_recv, cy_send, cy_recv, n_send, n_recv,
    x_factor, x_last, y_factor, r_all, w_all, inverse, y_all, f_all, grid, zb_recv, zb_out, r_recv,
    in_sem, send_sem, recv_sem,
):
    lat, lev = lax.axis_index("lat"), lax.axis_index("lev")
    y, zl, core = lat // 8, (lat // 2) % 4, lat % 2
    x, zh = lev // 2, lev % 2
    mine = y * 2 + core
    lane = lax.broadcasted_iota(jnp.int32, (8, 128), 1)
    sublane = lax.broadcasted_iota(jnp.int32, (8, 128), 0)

    def at(y_, zl_, core_, x_, zh_):
        return {"lat": y_ * 8 + zl_ * 2 + core_, "lev": x_ * 2 + zh_}

    def level_at(x_, zl_):
        inner = ((zl_ + 1) // 2) % 2
        return x_ * 4 + 2 * ((zh + 1 + inner) % 2) + zl_ // 2

    def send(src, dst, phase, target):
        pltpu.make_async_remote_copy(
            src_ref=src, dst_ref=dst, send_sem=send_sem.at[phase], recv_sem=recv_sem.at[phase],
            device_id=target, device_id_type=MESH,
        ).start()

    def send_or_keep(src, dst, phase, target, here):
        @pl.when(here)
        def _():
            pltpu.make_async_copy(src, dst, recv_sem.at[phase]).start()

        @pl.when(jnp.logical_not(here))
        def _():
            send(src, dst, phase, target)

    def wait(ref, sem):
        pltpu.make_async_copy(ref, ref, sem).wait()

    loads = [
        pltpu.make_async_copy(src, dst, in_sem.at[i])
        for i, (src, dst) in enumerate(
            [(sea_hbm, mask), (dev_hbm, dev), (inc_hbm, inc), (dz_hbm, dz), (dx_hbm, dx), (dy_hbm, dy)]
        )
    ]
    for load in loads:
        load.start()

    zf = (zl + 2) % 4
    barrier = pltpu.get_barrier_semaphore()

    def greet(target):
        pl.semaphore_signal(barrier, inc=1, device_id=target, device_id_type=MESH)

    for a in (2, 1, 3, 0):
        for b in (0, 1):
            greet(at(y, zf, core, (x + a) % 4, (zh + b) % 2))

    @pl.when(zl % 3 == 0)
    def _():
        for a in range(2):
            for d in range(2):
                greet(at(y, 2 * core + a, d, x, 1 - zh))

    for a in range(2):

        @pl.when(zl != 2 * core + a)
        def _():
            for d in range(2):
                greet(at(y, 2 * core + a, d, x, zh))

    for a in (2, 1, 3):
        for d in range(2):
            greet(at((y + a) % 4, zl, d, x, zh))
    greet(at(y, zl, 1 - core, x, zh))

    for load in loads[:4]:
        load.wait()
    sea = [paired(mask[l]).astype(F32) for l in range(2)]
    for l in range(2):
        couple = tiles_of(paired(dz[l]) * sea[l])
        for t in range(2):
            factor = paired(dev[t, l]) * sea[l]
            state = tiles_of(factor * paired(inc[t, l]))
            factor = tiles_of(factor)
            for j in range(TILES):
                scale[t, l, 8 * j : 8 * j + 8, :] = factor[j]
                spot = pl.ds(8 * (j % 2), 8)
                z_send[t, j // 2, 0, l, spot, :] = state[j]
                z_send[t, j // 2, 1, l, spot, :] = couple[j]
    for load in loads[4:]:
        load.wait()
    for l in range(2):
        sea_tiles = tiles_of(sea[l])
        west = from_west(sea_tiles, 1, lane)
        west[0] = jnp.where((lane == 0) & (sublane < 4), 0.0, west[0])
        couple_x, couple_y = tiles_of(paired(dx[l])), tiles_of(paired(dy[l]))
        for j in range(TILES):
            cx_send[l, 8 * j : 8 * j + 8, :] = couple_x[j] * sea_tiles[j] * west[j]
            cy_send[l, 8 * j : 8 * j + 8, :] = couple_y[j] * sea_tiles[j]

    pl.semaphore_wait(barrier, 20)

    for a in (2, 1, 3, 0):
        j = (x + a) % 4
        for t in range(2):
            send(z_send.at[t, j], z_recv.at[lev], TO_COLUMNS, at(y, zf, core, j, t))
    part = (zl % 2) * 2 + core
    lines_core = zl // 2
    for c_send, c_recv, phase in ((cy_send, cy_recv, COUPLE_Y), (cx_send, cx_recv, COUPLE_X)):
        for l in range(2):
            for b in (1, 0):
                zt = 3 * l if b else 1 + l
                target = at(y, zt, lines_core, x, (zh + b) % 2)
                src, dst = c_send.at[l], c_recv.at[pl.ds(pl.multiple_of(part * 64, 64), 64)]
                if b == 0:
                    send_or_keep(src, dst, phase, target, (zl == zt) & (core == lines_core))
                else:
                    send(src, dst, phase, target)

    def solve_levels(take, put):
        upper, lower = take(0), take(15)
        held = {0: upper, 15: lower}
        for k in range(7):
            held[k + 1] = take(k + 1) + z_factor[0, k] * held[k]
            held[14 - k] = take(14 - k) + z_factor[0, 15 - k] * held[15 - k]
        solved = z_factor[1, 8] * (held[8] + z_factor[0, 7] * held[7])
        put(8, solved)
        up = down = solved
        for k in range(8):
            up = z_factor[1, 7 - k] * held[7 - k] + z_factor[0, 7 - k] * up
            put(7 - k, up)
            if k < 7:
                down = z_factor[1, 9 + k] * held[9 + k] + z_factor[0, 9 + k] * down
                put(9 + k, down)

    wait(z_recv, recv_sem.at[TO_COLUMNS])
    upper = lower = jnp.ones((16, 128), F32)
    for k in range(8):
        c_up = z_recv[(k + 1) // 2, 1, (k + 1) % 2]
        inv = 1.0 / (upper + c_up)
        z_factor[0, k] = c_up * inv
        z_factor[1, k] = inv
        upper = 1.0 + c_up * inv * upper
        if k < 7:
            c_low = z_recv[(15 - k) // 2, 1, (15 - k) % 2]
            inv = 1.0 / (lower + c_low)
            z_factor[0, 15 - k] = c_low * inv
            z_factor[1, 15 - k] = inv
            lower = 1.0 + c_low * inv * lower
    z_factor[1, 8] = 1.0 / (upper + (lower - 1.0))

    def put_first(k, value):
        z_out[k] = value

    solve_levels(lambda k: z_recv[k // 2, 0, k % 2], put_first)

    from_core = zf // 2
    from_part = (zf % 2) * 2 + core
    for a in (2, 1, 3, 0):
        for b in (3, 1, 2, 0):
            x_, zl_ = (x + a) % 4, (zl + b) % 4
            src = z_out.at[level_at(x_, zl_)]
            dst = g_recv.at[pl.ds(pl.multiple_of(from_part * 64 + x * 16, 16), 16)]
            target = at(y, zl_, from_core, x_, zh)
            if a == 0 and b == 0:
                send_or_keep(src, dst, TO_LINES, target, from_core == core)
            else:
                send(src, dst, TO_LINES, target)

    wait(cy_recv, recv_sem.at[COUPLE_Y])

    def row_at(i, half):
        return pl.ds((i // 4) * 64 + (i % 4) + 32 * half, 8, stride=4)

    for half in range(2):
        n_send[8 * half : 8 * half + 8, :] = cy_recv[row_at(0, half), :]
    before = (mine + 7) % 8
    send(n_send, n_recv, NEXT_ROW, at(before // 2, zl, before % 2, x, zh))

    ring = []
    for k in (4, 5, 3, 2, 6, 7, 1):
        block = (mine + k) % 8
        ring.append(at(block // 2, zl, block % 2, x, zh))

    row = (mine * BLOCK + lax.broadcasted_iota(jnp.int32, (BLOCK, 128), 0)).astype(F32)
    weight = jnp.cos((-78.0 + 166.0 * (row + 0.5) / ROWS) * (math.pi / 180.0))
    inner = range(1, BLOCK)

    def total(terms):
        while len(terms) > 1:
            terms = [sum(terms[i : i + 2][1:], terms[i]) for i in range(0, len(terms), 2)]
        return terms[0]

    def solve_inner(rows, spot):
        here, held = None, [None] * BLOCK
        for i in inner:
            here = rows[i] if i == 1 else rows[i] + y_factor[0, i - 1, spot, :] * here
            held[i] = y_factor[1, i, spot, :] * here
        for i in range(BLOCK - 2, 0, -1):
            held[i] = held[i] + y_factor[0, i, spot, :] * held[i + 1]
        return held

    wait(n_recv, recv_sem.at[NEXT_ROW])
    for half in range(2):
        spot = pl.ds(8 * half, 8)
        faces = [cy_recv[row_at(i, half), :] for i in range(BLOCK)]
        north = jnp.where(mine < 7, n_recv[spot, :], 0.0)
        couple = [None] + [
            jnp.where(faces[i - 1] > 0.0, faces[i] if i < BLOCK else north, 0.0) for i in range(1, BLOCK + 1)
        ]
        ground = jnp.ones((8, 128), F32)
        own, link = jnp.ones((8, 128), F32), couple[1]
        to_own, to_next = [None] * BLOCK, [None] * BLOCK
        for i in inner:
            inv = 1.0 / (ground + (link + couple[i + 1]))
            to_own[i], to_next[i] = link * inv, couple[i + 1] * inv
            y_factor[0, i, spot, :] = to_next[i]
            y_factor[1, i, spot, :] = inv
            own = own + to_own[i] * ground
            link = to_own[i] * couple[i + 1]
            beyond = to_next[i] * ground
            ground = 1.0 + beyond
        r_all[mine, 0, spot, :] = own
        r_all[mine, 1, spot, :] = beyond
        r_all[mine, 2, spot, :] = link
        left, right = to_own[15], to_next[15]
        y_factor[2, 15, spot, :] = left
        y_factor[3, 15, spot, :] = right
        for i in range(BLOCK - 2, 0, -1):
            left = to_own[i] + to_next[i] * left
            right = to_next[i] * right
            y_factor[2, i, spot, :] = left
            y_factor[3, i, spot, :] = right
    for target in ring:
        send(r_all.at[mine], r_all.at[mine], REDUCED, target)

    wait(cx_recv, recv_sem.at[COUPLE_X])

    def bases():
        return [64 * part_ for part_ in range(4)]

    k = [[cx_recv[base + 8 * j : base + 8 * j + 8, :] for j in range(TILES)] for base in bases()]
    e = [[jnp.ones((8, 128), F32)] * TILES for _ in bases()]
    for i, stride in enumerate(STRIDES):
        for g, base in enumerate(bases()):
            k_east = from_east(k[g], stride, lane)
            inv = [1.0 / (a + (b + c)) for a, b, c in zip(e[g], k[g], k_east)]
            plus = [a * b for a, b in zip(k_east, inv)]
            minus = [a * b for a, b in zip(k[g], inv)]
            for j in range(TILES):
                x_factor[i, 0, base + 8 * j : base + 8 * j + 8, :] = plus[j]
                x_factor[i, 1, base + 8 * j : base + 8 * j + 8, :] = minus[j]
            west = from_west([a * b for a, b in zip(plus, e[g])], stride, lane)
            east = from_east([a * b for a, b in zip(minus, e[g])], stride, lane)
            k[g] = from_west([a * b for a, b in zip(plus, k[g])], stride, lane)
            e[g] = [a + (b + c) for a, b, c in zip(e[g], west, east)]
    for g, base in enumerate(bases()):
        for j in range(TILES):
            x_last[base + 8 * j : base + 8 * j + 8, :] = 1.0 / e[g][j]

    def longitude_solve(source, parts=(0, 1, 2, 3)):
        bases = lambda: [64 * part_ for part_ in parts]
        r = [[source[base + 8 * j : base + 8 * j + 8, :] for j in range(TILES)] for base in bases()]
        for i, stride in enumerate(STRIDES):
            for g, base in enumerate(bases()):
                plus = [x_factor[i, 0, base + 8 * j : base + 8 * j + 8, :] * r[g][j] for j in range(TILES)]
                minus = [x_factor[i, 1, base + 8 * j : base + 8 * j + 8, :] * r[g][j] for j in range(TILES)]
                west, east = from_west(plus, stride, lane), from_east(minus, stride, lane)
                r[g] = [a + (b + c) for a, b, c in zip(r[g], west, east)]
        for g, base in enumerate(bases()):
            for j in range(TILES):
                grid[base + 8 * j : base + 8 * j + 8, :] = r[g][j] * x_last[base + 8 * j : base + 8 * j + 8, :]

    def reduced_inverse():
        for half in range(2):
            spot = pl.ds(8 * half, 8)
            ground = [r_all[b, 0, spot, :] for b in range(8)]
            for b in range(1, 8):
                ground[b] = ground[b] + r_all[b - 1, 1, spot, :]
            link = [r_all[b, 2, spot, :] for b in range(7)]
            below, above = [ground[0]], [None] * 7 + [jnp.zeros((8, 128), F32)]
            north, south = [None] * 8, [None] * 8
            for b in range(7):
                inv = 1.0 / (below[b] + link[b])
                north[b] = link[b] * inv
                inverse[4, b, spot, :] = north[b]
                inverse[5, b, spot, :] = inv
                below.append(ground[b + 1] + north[b] * below[b])
            inverse[5, 7, spot, :] = 1.0 / below[7]
            for b in range(7, 0, -1):
                whole = ground[b] + above[b]
                south[b] = link[b - 1] / (whole + link[b - 1])
                above[b - 1] = south[b] * whole
            for which in range(2):
                spike = mine + which
                row_ = [None] * 8
                here = jnp.zeros((8, 128), F32)
                for b in range(7, -1, -1):
                    moved = here if b == 7 else north[b] * here
                    here = jnp.where(spike == b, 1.0 / (below[b] + above[b]), moved)
                    row_[b] = here
                here = jnp.zeros((8, 128), F32)
                for b in range(8):
                    moved = here if b == 0 else south[b] * here
                    here = jnp.where(spike < b, moved, row_[b])
                    inverse[which, b, spot, :] = here

    def weighted_inverse():
        for half in range(2):
            spot = pl.ds(8 * half, 8)
            middle = [w_all[b, 0, spot, :] for b in range(8)]
            for b in range(1, 8):
                middle[b] = middle[b] + w_all[b - 1, 2, spot, :]
            beside = [w_all[b, 1, spot, :] for b in range(7)]
            for which in range(2):
                g = [inverse[which, b, spot, :] for b in range(8)]
                right = [middle[b] * g[b] for b in range(8)]
                for b in range(7):
                    right[b] = right[b] + beside[b] * g[b + 1]
                    right[b + 1] = right[b + 1] + beside[b] * g[b]
                for b in range(7):
                    right[b + 1] = right[b + 1] + inverse[4, b, spot, :] * right[b]
                here = inverse[5, 7, spot, :] * right[7]
                inverse[2 + which, 7, spot, :] = here
                for b in range(6, -1, -1):
                    here = inverse[5, b, spot, :] * right[b] + inverse[4, b, spot, :] * here
                    inverse[2 + which, b, spot, :] = here

    def rows_of(half):
        return [grid[row_at(i, half), :] for i in range(BLOCK)]

    def put_rows(half, rows):
        for i in range(BLOCK):
            grid[row_at(i, half), :] = rows[i]

    def gathered(everyone, first, half):
        values = [everyone[b, pl.ds(16 * first + 8 * half, 8), :] for b in range(8)]
        for b in range(1, 8):
            values[b] = values[b] + everyone[b - 1, pl.ds(16 * (first + 1) + 8 * half, 8), :]
        return values

    def applied(which, values, spot):
        return [inverse[which, b, spot, :] * values[b] for b in range(8)]

    def tell(everyone, phase):
        for target in ring:
            send(everyone.at[mine], everyone.at[mine], phase, target)

    def latitude_solve(everyone, phase, behind=None, between=None):
        inside = []
        for half in range(2):
            spot = pl.ds(8 * half, 8)
            rows = rows_of(half)
            own = total([rows[0]] + [y_factor[2, i, spot, :] * rows[i] for i in inner])
            beyond = total([y_factor[3, i, spot, :] * rows[i] for i in inner])
            everyone[mine, spot, :] = own
            everyone[mine, pl.ds(16 + 8 * half, 8), :] = beyond
        tell(everyone, phase)
        if behind is not None:
            behind()
        for half in range(2):
            inside.append(solve_inner(rows_of(half), pl.ds(8 * half, 8)))
        if between is not None:
            between()
        wait(everyone.at[pl.ds(0, 7)], recv_sem.at[phase])
        for half in range(2):
            spot = pl.ds(8 * half, 8)
            right = gathered(everyone, 0, half)
            first, last = (total(applied(which, right, spot)) for which in range(2))
            put_rows(half, [first] + [
                inside[half][i] + (y_factor[2, i, spot, :] * first + y_factor[3, i, spot, :] * last) for i in inner
            ])

    def latitude_pair(everyone, phase):
        inside = []
        for half in range(2):
            spot = pl.ds(8 * half, 8)
            rows = rows_of(half)
            for k in range(4):
                terms = [y_factor[2 + k, i, spot, :] * rows[i] for i in inner]
                everyone[mine, pl.ds(16 * k + 8 * half, 8), :] = total(([rows[0]] if k == 0 else []) + terms)
        tell(everyone, phase)
        for half in range(2):
            spot = pl.ds(8 * half, 8)
            once = solve_inner(rows_of(half), spot)
            inside.append(solve_inner([None] + [once[i] * weight[i : i + 1, :] for i in inner], spot))
        wait(w_all.at[pl.ds(0, 7)], recv_sem.at[WEIGHTED])
        weighted_inverse()
        wait(everyone.at[pl.ds(0, 7)], recv_sem.at[phase])
        for half in range(2):
            spot = pl.ds(8 * half, 8)
            right, more = gathered(everyone, 0, half), gathered(everyone, 2, half)
            ends = [total(applied(which, right, spot)) for which in range(2)]
            ends += [total(applied(2 + k, right, spot) + applied(k, more, spot)) for k in range(2)]
            put_rows(half, [ends[2]] + [
                inside[half][i]
                + (y_factor[4, i, spot, :] * ends[0] + y_factor[5, i, spot, :] * ends[1])
                + (y_factor[2, i, spot, :] * ends[2] + y_factor[3, i, spot, :] * ends[3])
                for i in inner
            ])

    def weighted_block():
        for half in range(2):
            spot = pl.ds(8 * half, 8)
            sides = [[None] + [y_factor[2 + k, i, spot, :] for i in inner] for k in range(2)]
            loaded = [[None] + [side[i] * weight[i : i + 1, :] for i in inner] for side in sides]
            w_all[mine, 0, spot, :] = weight[0:1, :] + total([sides[0][i] * loaded[0][i] for i in inner])
            w_all[mine, 1, spot, :] = total([sides[0][i] * loaded[1][i] for i in inner])
            w_all[mine, 2, spot, :] = total([sides[1][i] * loaded[1][i] for i in inner])
            for k in range(2):
                twice = solve_inner(loaded[k], spot)
                for i in inner:
                    y_factor[4 + k, i, spot, :] = twice[i]
        tell(w_all, WEIGHTED)

    def first_between():
        wait(r_all.at[pl.ds(0, 7)], recv_sem.at[REDUCED])
        reduced_inverse()

    wait(g_recv, recv_sem.at[TO_LINES])
    longitude_solve(g_recv)
    latitude_solve(y_all.at[0], LATITUDE_A, weighted_block, first_between)
    longitude_solve(grid)
    latitude_pair(f_all, LATITUDE_B)
    longitude_solve(grid)
    latitude_solve(y_all.at[1], LATITUDE_C)

    level = level_at(x, zl)
    for first in (0, 2):
        longitude_solve(grid, (first, first + 1))
        for a in (2, 1, 3, 0):
            x_ = (x + a) % 4
            for b in (first, first + 1):
                zl_, core_ = (2 * core + b // 2 + 2) % 4, b % 2
                src = grid.at[pl.ds(pl.multiple_of(b * 64 + x_ * 16, 16), 16)]
                target = at(y, zl_, core_, x_, zh)
                if a == 0:
                    send_or_keep(src, zb_recv.at[level], BACK_COLUMNS, target, (zl_ == zl) & (core_ == core))
                else:
                    send(src, zb_recv.at[level], BACK_COLUMNS, target)
    wait(zb_recv, recv_sem.at[BACK_COLUMNS])

    def put_last(k, value):
        zb_out[k] = value

    solve_levels(lambda k: zb_recv[k], put_last)
    for a in (2, 1, 3, 0):
        for b in range(2):
            x_ = (x + a) % 4
            src = zb_out.at[pl.ds(x_ * 4 + b * 2, 2)]
            dst = r_recv.at[zh, :, pl.ds(pl.multiple_of(x * 16, 16), 16)]
            send(src, dst, BACK_ROWS, at(y, zf, core, x_, b))
    wait(r_recv, recv_sem.at[BACK_ROWS])
    for t in range(2):
        for l in range(2):
            for j in range(TILES):
                spot = pl.ds(8 * j, 8)
                tile = scale[t, l, spot, :] * r_recv[t, l, spot, :]
                out_ref[t, l, :, 128 * j : 128 * j + 128] = tile[:4]
                out_ref[t, l, :, HALF + 128 * j : HALF + 128 * j + 128] = tile[4:]

    wait(z_send.at[:, :, :, :], send_sem.at[TO_COLUMNS])
    for c_send, phase in ((cy_send, COUPLE_Y), (cx_send, COUPLE_X)):
        for l in range(2):
            wait(c_send.at[l], send_sem.at[phase])

            @pl.when(jnp.logical_not((zl == 1 + l) & (core == lines_core)))
            def _():
                wait(c_send.at[l], send_sem.at[phase])

    wait(z_out.at[pl.ds(0, 15)], send_sem.at[TO_LINES])

    @pl.when(from_core != core)
    def _():
        wait(z_out.at[15], send_sem.at[TO_LINES])

    wait(n_send, send_sem.at[NEXT_ROW])
    wait(r_all.at[pl.ds(0, 7)], send_sem.at[REDUCED])
    wait(w_all.at[pl.ds(0, 7)], send_sem.at[WEIGHTED])
    wait(y_all.at[0, pl.ds(0, 7)], send_sem.at[LATITUDE_A])
    wait(f_all.at[pl.ds(0, 7)], send_sem.at[LATITUDE_B])
    wait(y_all.at[1, pl.ds(0, 7)], send_sem.at[LATITUDE_C])
    wait(zb_recv.at[pl.ds(0, 15)], send_sem.at[BACK_COLUMNS])
    base = (zl - 2 * core + 2) % 4

    @pl.when(base >= 2)
    def _():
        wait(zb_recv.at[15], send_sem.at[BACK_COLUMNS])

    wait(r_recv, send_sem.at[BACK_ROWS])


def per_device(increment, deviations, diffuse_x, diffuse_y, diffuse_z, sea_mask):
    vmem = lambda *shape: pltpu.VMEM(shape, F32)
    shape = increment.shape
    plane = diffuse_x.shape
    return pl.pallas_call(
        kernel,
        out_shape=jax.ShapeDtypeStruct(shape, F32),
        in_specs=[pl.BlockSpec(memory_space=pl.ANY)] * 6,
        out_specs=pl.BlockSpec(memory_space=pltpu.VMEM),
        scratch_shapes=[
            vmem(*shape), vmem(*shape), vmem(*plane), vmem(*plane), vmem(*plane), pltpu.VMEM(plane, jnp.int32),
            vmem(2, 2, 64, 128),
            vmem(2, 4, 2, 2, 16, 128), vmem(8, 2, 2, 16, 128), vmem(2, 16, 16, 128), vmem(16, 16, 128),
            vmem(256, 128), vmem(2, 64, 128), vmem(256, 128), vmem(2, 64, 128), vmem(256, 128), vmem(16, 128), vmem(16, 128),
            vmem(11, 2, 256, 128), vmem(256, 128), vmem(6, 16, 16, 128), vmem(8, 3, 16, 128), vmem(8, 3, 16, 128),
            vmem(6, 8, 16, 128), vmem(2, 8, 32, 128), vmem(8, 64, 128), vmem(256, 128), vmem(16, 16, 128), vmem(16, 16, 128), vmem(2, 2, 64, 128),
            pltpu.SemaphoreType.DMA((6,)), pltpu.SemaphoreType.DMA((12,)), pltpu.SemaphoreType.DMA((12,)),
        ],
        compiler_params=pltpu.CompilerParams(
            collective_id=0, has_side_effects=True, vmem_limit_bytes=60 * 1024 * 1024
        ),
        name="covariance",
    )(increment, deviations, diffuse_x, diffuse_y, diffuse_z, sea_mask)


def solution(mesh):
    in_specs = (
        P(None, "lev", "lat", None),
        P(None, "lev", "lat", None),
        P("lev", "lat", None),
        P("lev", "lat", None),
        P("lev", "lat", None),
        P("lev", "lat", None),
    )
    out_specs = P(None, "lev", "lat", None)
    return jax.shard_map(
        per_device, mesh=mesh, in_specs=in_specs, out_specs=out_specs, check_vma=False
    )
```

```python
import math

import jax
import jax.numpy as jnp
from jax import lax
from jax.experimental import pallas as pl
from jax.experimental.pallas import tpu as pltpu
from jax.sharding import PartitionSpec as P

MESH = pl.DeviceIdType.MESH
F32 = jnp.float32
LEVELS, HALF, TILES, BLOCK, ROWS = 16, 1024, 8, 16, 128
STRIDES = (1, 2, 4, 8, 16, 32, 64, 128, 256, 512, 1024)
TO_COLUMNS, TO_LINES, COUPLE_X, COUPLE_Y, NEXT_ROW, REDUCED, WEIGHTED = range(7)
LATITUDE_A, LATITUDE_B, LATITUDE_C, BACK_COLUMNS, BACK_ROWS = range(7, 12)


def swap_halves(tile):
    return pltpu.roll(tile, 4, 0)


def from_west(tiles, stride, lane):
    if stride >= 128:
        k = stride // 128
        return [tiles[j - k] if j >= k else swap_halves(tiles[TILES + j - k]) for j in range(TILES)]
    turned = [pltpu.roll(tile, stride, 1) for tile in tiles]
    carry = [swap_halves(turned[-1])] + turned[:-1]
    return [jnp.where(lane < stride, c, t) for c, t in zip(carry, turned)]


def from_east(tiles, stride, lane):
    if stride >= 128:
        k = stride // 128
        return [tiles[j + k] if j + k < TILES else swap_halves(tiles[j + k - TILES]) for j in range(TILES)]
    turned = [pltpu.roll(tile, 128 - stride, 1) for tile in tiles]
    carry = turned[1:] + [swap_halves(turned[0])]
    return [jnp.where(lane >= 128 - stride, c, t) for c, t in zip(carry, turned)]


def paired(rows):
    return jnp.concatenate([rows[:, :HALF], rows[:, HALF:]], axis=0)


def tiles_of(wide):
    return [wide[:, 128 * j : 128 * (j + 1)] for j in range(TILES)]


def kernel(
    inc_hbm, dev_hbm, dx_hbm, dy_hbm, dz_hbm, sea_hbm, out_ref,
    inc, dev, dx, dy, dz, mask, scale, result,
    z_send, z_recv, z_factor, z_out, g_recv, cx_send, cx_recv, cy_send, cy_recv, n_send, n_recv,
    x_factor, x_last, y_factor, r_all, w_all, inverse, y_all, f_all, grid, zb_recv, zb_out, r_recv,
    in_sem, send_sem, recv_sem,
):
    lat, lev = lax.axis_index("lat"), lax.axis_index("lev")
    y, zl, core = lat // 8, (lat // 2) % 4, lat % 2
    x, zh = lev // 2, lev % 2
    mine = y * 2 + core
    lane = lax.broadcasted_iota(jnp.int32, (8, 128), 1)
    sublane = lax.broadcasted_iota(jnp.int32, (8, 128), 0)

    def at(y_, zl_, core_, x_, zh_):
        return {"lat": y_ * 8 + zl_ * 2 + core_, "lev": x_ * 2 + zh_}

    def level_at(x_, zl_):
        inner = ((zl_ + 1) // 2) % 2
        return x_ * 4 + 2 * ((zh + 1 + inner) % 2) + zl_ // 2

    def send(src, dst, phase, target):
        pltpu.make_async_remote_copy(
            src_ref=src, dst_ref=dst, send_sem=send_sem.at[phase], recv_sem=recv_sem.at[phase],
            device_id=target, device_id_type=MESH,
        ).start()

    def send_or_keep(src, dst, phase, target, here):
        @pl.when(here)
        def _():
            pltpu.make_async_copy(src, dst, recv_sem.at[phase]).start()

        @pl.when(jnp.logical_not(here))
        def _():
            send(src, dst, phase, target)

    def wait(ref, sem):
        pltpu.make_async_copy(ref, ref, sem).wait()

    loads = [
        pltpu.make_async_copy(src, dst, in_sem.at[i])
        for i, (src, dst) in enumerate(
            [(sea_hbm, mask), (dev_hbm, dev), (inc_hbm, inc), (dz_hbm, dz), (dx_hbm, dx), (dy_hbm, dy)]
        )
    ]
    for load in loads:
        load.start()

    zf = (zl + 2) % 4
    barrier = pltpu.get_barrier_semaphore()

    def greet(target):
        pl.semaphore_signal(barrier, inc=1, device_id=target, device_id_type=MESH)

    for a in (2, 1, 3, 0):
        for b in (0, 1):
            greet(at(y, zf, core, (x + a) % 4, (zh + b) % 2))

    @pl.when(zl % 3 == 0)
    def _():
        for a in range(2):
            for d in range(2):
                greet(at(y, 2 * core + a, d, x, 1 - zh))

    for a in range(2):

        @pl.when(zl != 2 * core + a)
        def _():
            for d in range(2):
                greet(at(y, 2 * core + a, d, x, zh))

    for a in (2, 1, 3):
        for d in range(2):
            greet(at((y + a) % 4, zl, d, x, zh))
    greet(at(y, zl, 1 - core, x, zh))

    for load in loads[:4]:
        load.wait()
    sea = [paired(mask[l]).astype(F32) for l in range(2)]
    for l in range(2):
        couple = tiles_of(paired(dz[l]) * sea[l])
        for t in range(2):
            factor = paired(dev[t, l]) * sea[l]
            state = tiles_of(factor * paired(inc[t, l]))
            factor = tiles_of(factor)
            for j in range(TILES):
                scale[t, l, 8 * j : 8 * j + 8, :] = factor[j]
                spot = pl.ds(8 * (j % 2), 8)
                z_send[t, j // 2, 0, l, spot, :] = state[j]
                z_send[t, j // 2, 1, l, spot, :] = couple[j]
    for load in loads[4:]:
        load.wait()
    for l in range(2):
        sea_tiles = tiles_of(sea[l])
        west = from_west(sea_tiles, 1, lane)
        west[0] = jnp.where((lane == 0) & (sublane < 4), 0.0, west[0])
        couple_x, couple_y = tiles_of(paired(dx[l])), tiles_of(paired(dy[l]))
        for j in range(TILES):
            cx_send[l, 8 * j : 8 * j + 8, :] = couple_x[j] * sea_tiles[j] * west[j]
            cy_send[l, 8 * j : 8 * j + 8, :] = couple_y[j] * sea_tiles[j]

    pl.semaphore_wait(barrier, 20)

    for a in (2, 1, 3, 0):
        j = (x + a) % 4
        for t in range(2):
            send(z_send.at[t, j], z_recv.at[lev], TO_COLUMNS, at(y, zf, core, j, t))
    part = (zl % 2) * 2 + core
    lines_core = zl // 2
    for c_send, c_recv, phase in ((cy_send, cy_recv, COUPLE_Y), (cx_send, cx_recv, COUPLE_X)):
        for l in range(2):
            for b in (1, 0):
                zt = 3 * l if b else 1 + l
                target = at(y, zt, lines_core, x, (zh + b) % 2)
                src, dst = c_send.at[l], c_recv.at[pl.ds(pl.multiple_of(part * 64, 64), 64)]
                if b == 0:
                    send_or_keep(src, dst, phase, target, (zl == zt) & (core == lines_core))
                else:
                    send(src, dst, phase, target)

    def solve_levels(take, put):
        upper, lower = take(0), take(15)
        held = {0: upper, 15: lower}
        for k in range(7):
            held[k + 1] = take(k + 1) + z_factor[0, k] * held[k]
            held[14 - k] = take(14 - k) + z_factor[0, 15 - k] * held[15 - k]
        solved = z_factor[1, 8] * (held[8] + z_factor[0, 7] * held[7])
        put(8, solved)
        up = down = solved
        for k in range(8):
            up = z_factor[1, 7 - k] * held[7 - k] + z_factor[0, 7 - k] * up
            put(7 - k, up)
            if k < 7:
                down = z_factor[1, 9 + k] * held[9 + k] + z_factor[0, 9 + k] * down
                put(9 + k, down)

    wait(z_recv, recv_sem.at[TO_COLUMNS])
    upper = lower = jnp.ones((16, 128), F32)
    for k in range(8):
        c_up = z_recv[(k + 1) // 2, 1, (k + 1) % 2]
        inv = 1.0 / (upper + c_up)
        z_factor[0, k] = c_up * inv
        z_factor[1, k] = inv
        upper = 1.0 + c_up * inv * upper
        if k < 7:
            c_low = z_recv[(15 - k) // 2, 1, (15 - k) % 2]
            inv = 1.0 / (lower + c_low)
            z_factor[0, 15 - k] = c_low * inv
            z_factor[1, 15 - k] = inv
            lower = 1.0 + c_low * inv * lower
    z_factor[1, 8] = 1.0 / (upper + (lower - 1.0))

    def put_first(k, value):
        z_out[k] = value

    solve_levels(lambda k: z_recv[k // 2, 0, k % 2], put_first)

    from_core = zf // 2
    from_part = (zf % 2) * 2 + core
    for a in (2, 1, 3, 0):
        for b in (3, 1, 2, 0):
            x_, zl_ = (x + a) % 4, (zl + b) % 4
            src = z_out.at[level_at(x_, zl_)]
            dst = g_recv.at[pl.ds(pl.multiple_of(from_part * 64 + x * 16, 16), 16)]
            target = at(y, zl_, from_core, x_, zh)
            if a == 0 and b == 0:
                send_or_keep(src, dst, TO_LINES, target, from_core == core)
            else:
                send(src, dst, TO_LINES, target)

    wait(cy_recv, recv_sem.at[COUPLE_Y])

    def row_at(i, half):
        return pl.ds((i // 4) * 64 + (i % 4) + 32 * half, 8, stride=4)

    for half in range(2):
        n_send[8 * half : 8 * half + 8, :] = cy_recv[row_at(0, half), :]
    before = (mine + 7) % 8
    send(n_send, n_recv, NEXT_ROW, at(before // 2, zl, before % 2, x, zh))

    ring = []
    for k in (4, 5, 3, 2, 6, 7, 1):
        block = (mine + k) % 8
        ring.append(at(block // 2, zl, block % 2, x, zh))

    row = (mine * BLOCK + lax.broadcasted_iota(jnp.int32, (BLOCK, 128), 0)).astype(F32)
    weight = jnp.cos((-78.0 + 166.0 * (row + 0.5) / ROWS) * (math.pi / 180.0))
    inner = range(1, BLOCK)

    def total(terms):
        while len(terms) > 1:
            terms = [sum(terms[i : i + 2][1:], terms[i]) for i in range(0, len(terms), 2)]
        return terms[0]

    def solve_inner(rows, spot):
        here, held = None, [None] * BLOCK
        for i in inner:
            here = rows[i] if i == 1 else rows[i] + y_factor[0, i - 1, spot, :] * here
            held[i] = y_factor[1, i, spot, :] * here
        for i in range(BLOCK - 2, 0, -1):
            held[i] = held[i] + y_factor[0, i, spot, :] * held[i + 1]
        return held

    wait(n_recv, recv_sem.at[NEXT_ROW])
    for half in range(2):
        spot = pl.ds(8 * half, 8)
        faces = [cy_recv[row_at(i, half), :] for i in range(BLOCK)]
        north = jnp.where(mine < 7, n_recv[spot, :], 0.0)
        couple = [None] + [
            jnp.where(faces[i - 1] > 0.0, faces[i] if i < BLOCK else north, 0.0) for i in range(1, BLOCK + 1)
        ]
        ground = jnp.ones((8, 128), F32)
        own, link = jnp.ones((8, 128), F32), couple[1]
        to_own, to_next = [None] * BLOCK, [None] * BLOCK
        for i in inner:
            inv = 1.0 / (ground + (link + couple[i + 1]))
            to_own[i], to_next[i] = link * inv, couple[i + 1] * inv
            y_factor[0, i, spot, :] = to_next[i]
            y_factor[1, i, spot, :] = inv
            own = own + to_own[i] * ground
            link = to_own[i] * couple[i + 1]
            beyond = to_next[i] * ground
            ground = 1.0 + beyond
        r_all[mine, 0, spot, :] = own
        r_all[mine, 1, spot, :] = beyond
        r_all[mine, 2, spot, :] = link
        left, right = to_own[15], to_next[15]
        y_factor[2, 15, spot, :] = left
        y_factor[3, 15, spot, :] = right
        for i in range(BLOCK - 2, 0, -1):
            left = to_own[i] + to_next[i] * left
            right = to_next[i] * right
            y_factor[2, i, spot, :] = left
            y_factor[3, i, spot, :] = right
    for target in ring:
        send(r_all.at[mine], r_all.at[mine], REDUCED, target)

    wait(cx_recv, recv_sem.at[COUPLE_X])

    def bases():
        return [64 * part_ for part_ in range(4)]

    k = [[cx_recv[base + 8 * j : base + 8 * j + 8, :] for j in range(TILES)] for base in bases()]
    e = [[jnp.ones((8, 128), F32)] * TILES for _ in bases()]
    for i, stride in enumerate(STRIDES):
        for g, base in enumerate(bases()):
            k_east = from_east(k[g], stride, lane)
            inv = [1.0 / (a + (b + c)) for a, b, c in zip(e[g], k[g], k_east)]
            plus = [a * b for a, b in zip(k_east, inv)]
            minus = [a * b for a, b in zip(k[g], inv)]
            for j in range(TILES):
                x_factor[i, 0, base + 8 * j : base + 8 * j + 8, :] = plus[j]
                x_factor[i, 1, base + 8 * j : base + 8 * j + 8, :] = minus[j]
            west = from_west([a * b for a, b in zip(plus, e[g])], stride, lane)
            east = from_east([a * b for a, b in zip(minus, e[g])], stride, lane)
            k[g] = from_west([a * b for a, b in zip(plus, k[g])], stride, lane)
            e[g] = [a + (b + c) for a, b, c in zip(e[g], west, east)]
    for g, base in enumerate(bases()):
        for j in range(TILES):
            x_last[base + 8 * j : base + 8 * j + 8, :] = 1.0 / e[g][j]

    def longitude_solve(source, parts=(0, 1, 2, 3)):
        bases = lambda: [64 * part_ for part_ in parts]
        r = [[source[base + 8 * j : base + 8 * j + 8, :] for j in range(TILES)] for base in bases()]
        for i, stride in enumerate(STRIDES):
            for g, base in enumerate(bases()):
                plus = [x_factor[i, 0, base + 8 * j : base + 8 * j + 8, :] * r[g][j] for j in range(TILES)]
                minus = [x_factor[i, 1, base + 8 * j : base + 8 * j + 8, :] * r[g][j] for j in range(TILES)]
                west, east = from_west(plus, stride, lane), from_east(minus, stride, lane)
                r[g] = [a + (b + c) for a, b, c in zip(r[g], west, east)]
        for g, base in enumerate(bases()):
            for j in range(TILES):
                grid[base + 8 * j : base + 8 * j + 8, :] = r[g][j] * x_last[base + 8 * j : base + 8 * j + 8, :]

    def reduced_inverse():
        for half in range(2):
            spot = pl.ds(8 * half, 8)
            ground = [r_all[b, 0, spot, :] for b in range(8)]
            for b in range(1, 8):
                ground[b] = ground[b] + r_all[b - 1, 1, spot, :]
            link = [r_all[b, 2, spot, :] for b in range(7)]
            below, above = [ground[0]], [None] * 7 + [jnp.zeros((8, 128), F32)]
            north, south = [None] * 8, [None] * 8
            for b in range(7):
                inv = 1.0 / (below[b] + link[b])
                north[b] = link[b] * inv
                inverse[4, b, spot, :] = north[b]
                inverse[5, b, spot, :] = inv
                below.append(ground[b + 1] + north[b] * below[b])
            inverse[5, 7, spot, :] = 1.0 / below[7]
            for b in range(7, 0, -1):
                whole = ground[b] + above[b]
                south[b] = link[b - 1] / (whole + link[b - 1])
                above[b - 1] = south[b] * whole
            for which in range(2):
                spike = mine + which
                row_ = [None] * 8
                here = jnp.zeros((8, 128), F32)
                for b in range(7, -1, -1):
                    moved = here if b == 7 else north[b] * here
                    here = jnp.where(spike == b, 1.0 / (below[b] + above[b]), moved)
                    row_[b] = here
                here = jnp.zeros((8, 128), F32)
                for b in range(8):
                    moved = here if b == 0 else south[b] * here
                    here = jnp.where(spike < b, moved, row_[b])
                    inverse[which, b, spot, :] = here

    def weighted_inverse():
        for half in range(2):
            spot = pl.ds(8 * half, 8)
            middle = [w_all[b, 0, spot, :] for b in range(8)]
            for b in range(1, 8):
                middle[b] = middle[b] + w_all[b - 1, 2, spot, :]
            beside = [w_all[b, 1, spot, :] for b in range(7)]
            for which in range(2):
                g = [inverse[which, b, spot, :] for b in range(8)]
                right = [middle[b] * g[b] for b in range(8)]
                for b in range(7):
                    right[b] = right[b] + beside[b] * g[b + 1]
                    right[b + 1] = right[b + 1] + beside[b] * g[b]
                for b in range(7):
                    right[b + 1] = right[b + 1] + inverse[4, b, spot, :] * right[b]
                here = inverse[5, 7, spot, :] * right[7]
                inverse[2 + which, 7, spot, :] = here
                for b in range(6, -1, -1):
                    here = inverse[5, b, spot, :] * right[b] + inverse[4, b, spot, :] * here
                    inverse[2 + which, b, spot, :] = here

    def rows_of(half):
        return [grid[row_at(i, half), :] for i in range(BLOCK)]

    def put_rows(half, rows):
        for i in range(BLOCK):
            grid[row_at(i, half), :] = rows[i]

    def gathered(everyone, first, half):
        values = [everyone[b, pl.ds(16 * first + 8 * half, 8), :] for b in range(8)]
        for b in range(1, 8):
            values[b] = values[b] + everyone[b - 1, pl.ds(16 * (first + 1) + 8 * half, 8), :]
        return values

    def applied(which, values, spot):
        return [inverse[which, b, spot, :] * values[b] for b in range(8)]

    def tell(everyone, phase):
        for target in ring:
            send(everyone.at[mine], everyone.at[mine], phase, target)

    def latitude_solve(everyone, phase, behind=None, between=None):
        inside = []
        for half in range(2):
            spot = pl.ds(8 * half, 8)
            rows = rows_of(half)
            own = total([rows[0]] + [y_factor[2, i, spot, :] * rows[i] for i in inner])
            beyond = total([y_factor[3, i, spot, :] * rows[i] for i in inner])
            everyone[mine, spot, :] = own
            everyone[mine, pl.ds(16 + 8 * half, 8), :] = beyond
        tell(everyone, phase)
        if behind is not None:
            behind()
        for half in range(2):
            inside.append(solve_inner(rows_of(half), pl.ds(8 * half, 8)))
        if between is not None:
            between()
        wait(everyone.at[pl.ds(0, 7)], recv_sem.at[phase])
        for half in range(2):
            spot = pl.ds(8 * half, 8)
            right = gathered(everyone, 0, half)
            first, last = (total(applied(which, right, spot)) for which in range(2))
            put_rows(half, [first] + [
                inside[half][i] + (y_factor[2, i, spot, :] * first + y_factor[3, i, spot, :] * last) for i in inner
            ])

    def latitude_pair(everyone, phase):
        inside = []
        for half in range(2):
            spot = pl.ds(8 * half, 8)
            rows = rows_of(half)
            for k in range(4):
                terms = [y_factor[2 + k, i, spot, :] * rows[i] for i in inner]
                everyone[mine, pl.ds(16 * k + 8 * half, 8), :] = total(([rows[0]] if k == 0 else []) + terms)
        tell(everyone, phase)
        for half in range(2):
            spot = pl.ds(8 * half, 8)
            once = solve_inner(rows_of(half), spot)
            inside.append(solve_inner([None] + [once[i] * weight[i : i + 1, :] for i in inner], spot))
        wait(w_all.at[pl.ds(0, 7)], recv_sem.at[WEIGHTED])
        weighted_inverse()
        wait(everyone.at[pl.ds(0, 7)], recv_sem.at[phase])
        for half in range(2):
            spot = pl.ds(8 * half, 8)
            right, more = gathered(everyone, 0, half), gathered(everyone, 2, half)
            ends = [total(applied(which, right, spot)) for which in range(2)]
            ends += [total(applied(2 + k, right, spot) + applied(k, more, spot)) for k in range(2)]
            put_rows(half, [ends[2]] + [
                inside[half][i]
                + (y_factor[4, i, spot, :] * ends[0] + y_factor[5, i, spot, :] * ends[1])
                + (y_factor[2, i, spot, :] * ends[2] + y_factor[3, i, spot, :] * ends[3])
                for i in inner
            ])

    def weighted_block():
        for half in range(2):
            spot = pl.ds(8 * half, 8)
            sides = [[None] + [y_factor[2 + k, i, spot, :] for i in inner] for k in range(2)]
            loaded = [[None] + [side[i] * weight[i : i + 1, :] for i in inner] for side in sides]
            w_all[mine, 0, spot, :] = weight[0:1, :] + total([sides[0][i] * loaded[0][i] for i in inner])
            w_all[mine, 1, spot, :] = total([sides[0][i] * loaded[1][i] for i in inner])
            w_all[mine, 2, spot, :] = total([sides[1][i] * loaded[1][i] for i in inner])
            for k in range(2):
                twice = solve_inner(loaded[k], spot)
                for i in inner:
                    y_factor[4 + k, i, spot, :] = twice[i]
        tell(w_all, WEIGHTED)

    def first_between():
        wait(r_all.at[pl.ds(0, 7)], recv_sem.at[REDUCED])
        reduced_inverse()

    wait(g_recv, recv_sem.at[TO_LINES])
    longitude_solve(g_recv)
    latitude_solve(y_all.at[0], LATITUDE_A, weighted_block, first_between)
    longitude_solve(grid)
    latitude_pair(f_all, LATITUDE_B)
    longitude_solve(grid)
    latitude_solve(y_all.at[1], LATITUDE_C)

    level = level_at(x, zl)
    for first in (0, 2):
        longitude_solve(grid, (first, first + 1))
        for a in (2, 1, 3, 0):
            x_ = (x + a) % 4
            for b in (first, first + 1):
                zl_, core_ = (2 * core + b // 2 + 2) % 4, b % 2
                src = grid.at[pl.ds(pl.multiple_of(b * 64 + x_ * 16, 16), 16)]
                target = at(y, zl_, core_, x_, zh)
                if a == 0:
                    send_or_keep(src, zb_recv.at[level], BACK_COLUMNS, target, (zl_ == zl) & (core_ == core))
                else:
                    send(src, zb_recv.at[level], BACK_COLUMNS, target)
    wait(zb_recv, recv_sem.at[BACK_COLUMNS])

    def put_last(k, value):
        zb_out[k] = value

    solve_levels(lambda k: zb_recv[k], put_last)
    for a in (2, 1, 3, 0):
        for b in range(2):
            x_ = (x + a) % 4
            src = zb_out.at[pl.ds(x_ * 4 + b * 2, 2)]
            dst = r_recv.at[zh, :, pl.ds(pl.multiple_of(x * 16, 16), 16)]
            send(src, dst, BACK_ROWS + zh, at(y, zf, core, x_, b))
    stores = []
    for t in range(2):
        wait(r_recv.at[t], recv_sem.at[BACK_ROWS + t])
        for l in range(2):
            for j in range(TILES):
                spot = pl.ds(8 * j, 8)
                tile = scale[t, l, spot, :] * r_recv[t, l, spot, :]
                result[t, l, :, 128 * j : 128 * j + 128] = tile[:4]
                result[t, l, :, HALF + 128 * j : HALF + 128 * j + 128] = tile[4:]
            stores.append(pltpu.make_async_copy(result.at[t, l], out_ref.at[t, l], in_sem.at[2 * t + l]))
            stores[-1].start()

    wait(z_send.at[:, :, :, :], send_sem.at[TO_COLUMNS])
    for c_send, phase in ((cy_send, COUPLE_Y), (cx_send, COUPLE_X)):
        for l in range(2):
            wait(c_send.at[l], send_sem.at[phase])

            @pl.when(jnp.logical_not((zl == 1 + l) & (core == lines_core)))
            def _():
                wait(c_send.at[l], send_sem.at[phase])

    wait(z_out.at[pl.ds(0, 15)], send_sem.at[TO_LINES])

    @pl.when(from_core != core)
    def _():
        wait(z_out.at[15], send_sem.at[TO_LINES])

    wait(n_send, send_sem.at[NEXT_ROW])
    wait(r_all.at[pl.ds(0, 7)], send_sem.at[REDUCED])
    wait(w_all.at[pl.ds(0, 7)], send_sem.at[WEIGHTED])
    wait(y_all.at[0, pl.ds(0, 7)], send_sem.at[LATITUDE_A])
    wait(f_all.at[pl.ds(0, 7)], send_sem.at[LATITUDE_B])
    wait(y_all.at[1, pl.ds(0, 7)], send_sem.at[LATITUDE_C])
    wait(zb_recv.at[pl.ds(0, 15)], send_sem.at[BACK_COLUMNS])
    base = (zl - 2 * core + 2) % 4

    @pl.when(base >= 2)
    def _():
        wait(zb_recv.at[15], send_sem.at[BACK_COLUMNS])

    wait(r_recv, send_sem.at[BACK_ROWS + zh])
    for store in stores:
        store.wait()


def per_device(increment, deviations, diffuse_x, diffuse_y, diffuse_z, sea_mask):
    vmem = lambda *shape: pltpu.VMEM(shape, F32)
    shape = increment.shape
    plane = diffuse_x.shape
    return pl.pallas_call(
        kernel,
        out_shape=jax.ShapeDtypeStruct(shape, F32),
        in_specs=[pl.BlockSpec(memory_space=pl.ANY)] * 6,
        out_specs=pl.BlockSpec(memory_space=pl.ANY),
        scratch_shapes=[
            vmem(*shape), vmem(*shape), vmem(*plane), vmem(*plane), vmem(*plane), pltpu.VMEM(plane, jnp.int32),
            vmem(2, 2, 64, 128), vmem(*shape),
            vmem(2, 4, 2, 2, 16, 128), vmem(8, 2, 2, 16, 128), vmem(2, 16, 16, 128), vmem(16, 16, 128),
            vmem(256, 128), vmem(2, 64, 128), vmem(256, 128), vmem(2, 64, 128), vmem(256, 128), vmem(16, 128), vmem(16, 128),
            vmem(11, 2, 256, 128), vmem(256, 128), vmem(6, 16, 16, 128), vmem(8, 3, 16, 128), vmem(8, 3, 16, 128),
            vmem(6, 8, 16, 128), vmem(2, 8, 32, 128), vmem(8, 64, 128), vmem(256, 128), vmem(16, 16, 128), vmem(16, 16, 128), vmem(2, 2, 64, 128),
            pltpu.SemaphoreType.DMA((6,)), pltpu.SemaphoreType.DMA((13,)), pltpu.SemaphoreType.DMA((13,)),
        ],
        compiler_params=pltpu.CompilerParams(
            collective_id=0, has_side_effects=True, vmem_limit_bytes=60 * 1024 * 1024
        ),
        name="covariance",
    )(increment, deviations, diffuse_x, diffuse_y, diffuse_z, sea_mask)


def solution(mesh):
    in_specs = (
        P(None, "lev", "lat", None),
        P(None, "lev", "lat", None),
        P("lev", "lat", None),
        P("lev", "lat", None),
        P("lev", "lat", None),
        P("lev", "lat", None),
    )
    out_specs = P(None, "lev", "lat", None)
    return jax.shard_map(
        per_device, mesh=mesh, in_specs=in_specs, out_specs=out_specs, check_vma=False
    )
```

```python
import math

import jax
import jax.numpy as jnp
from jax import lax
from jax.experimental import pallas as pl
from jax.experimental.pallas import tpu as pltpu
from jax.sharding import PartitionSpec as P

MESH = pl.DeviceIdType.MESH
F32 = jnp.float32
LEVELS, HALF, TILES, BLOCK, ROWS = 16, 1024, 8, 16, 128
STRIDES = (1, 2, 4, 8, 16, 32, 64, 128, 256, 512, 1024)
TO_COLUMNS, TO_LINES, COUPLE_X, COUPLE_Y, NEXT_ROW, REDUCED, WEIGHTED = range(7)
LATITUDE_A, LATITUDE_B, LATITUDE_C, BACK_COLUMNS, BACK_ROWS = range(7, 12)


def swap_halves(tile):
    return pltpu.roll(tile, 4, 0)


def from_west(tiles, stride, lane):
    if stride >= 128:
        k = stride // 128
        return [tiles[j - k] if j >= k else swap_halves(tiles[TILES + j - k]) for j in range(TILES)]
    turned = [pltpu.roll(tile, stride, 1) for tile in tiles]
    carry = [swap_halves(turned[-1])] + turned[:-1]
    return [jnp.where(lane < stride, c, t) for c, t in zip(carry, turned)]


def from_east(tiles, stride, lane):
    if stride >= 128:
        k = stride // 128
        return [tiles[j + k] if j + k < TILES else swap_halves(tiles[j + k - TILES]) for j in range(TILES)]
    turned = [pltpu.roll(tile, 128 - stride, 1) for tile in tiles]
    carry = turned[1:] + [swap_halves(turned[0])]
    return [jnp.where(lane >= 128 - stride, c, t) for c, t in zip(carry, turned)]


def paired(rows):
    return jnp.concatenate([rows[:, :HALF], rows[:, HALF:]], axis=0)


def tiles_of(wide):
    return [wide[:, 128 * j : 128 * (j + 1)] for j in range(TILES)]


def kernel(
    inc_hbm, dev_hbm, dx_hbm, dy_hbm, dz_hbm, sea_hbm, out_ref,
    inc, dev, dx, dy, dz, mask, scale, result,
    z_send, z_recv, z_factor, z_out, g_recv, cx_send, cx_recv, cy_send, cy_recv, n_send, n_recv,
    x_factor, x_last, y_factor, r_all, w_all, inverse, y_all, f_all, grid, zb_recv, zb_out, r_recv,
    in_sem, send_sem, recv_sem,
):
    lat, lev = lax.axis_index("lat"), lax.axis_index("lev")
    y, zl, core = lat // 8, (lat // 2) % 4, lat % 2
    x, zh = lev // 2, lev % 2
    mine = y * 2 + core
    lane = lax.broadcasted_iota(jnp.int32, (8, 128), 1)
    sublane = lax.broadcasted_iota(jnp.int32, (8, 128), 0)

    def at(y_, zl_, core_, x_, zh_):
        return {"lat": y_ * 8 + zl_ * 2 + core_, "lev": x_ * 2 + zh_}

    def level_at(x_, zl_):
        inner = ((zl_ + 1) // 2) % 2
        return x_ * 4 + 2 * ((zh + 1 + inner) % 2) + zl_ // 2

    def send(src, dst, phase, target):
        pltpu.make_async_remote_copy(
            src_ref=src, dst_ref=dst, send_sem=send_sem.at[phase], recv_sem=recv_sem.at[phase],
            device_id=target, device_id_type=MESH,
        ).start()

    def send_or_keep(src, dst, phase, target, here):
        @pl.when(here)
        def _():
            pltpu.make_async_copy(src, dst, recv_sem.at[phase]).start()

        @pl.when(jnp.logical_not(here))
        def _():
            send(src, dst, phase, target)

    def wait(ref, sem):
        pltpu.make_async_copy(ref, ref, sem).wait()

    loads = [
        pltpu.make_async_copy(src, dst, in_sem.at[i])
        for i, (src, dst) in enumerate(
            [(sea_hbm, mask), (dev_hbm, dev), (inc_hbm, inc), (dz_hbm, dz), (dx_hbm, dx), (dy_hbm, dy)]
        )
    ]
    for load in loads:
        load.start()

    zf = (zl + 2) % 4
    barrier = pltpu.get_barrier_semaphore()

    def greet(target):
        pl.semaphore_signal(barrier, inc=1, device_id=target, device_id_type=MESH)

    for a in (2, 1, 3, 0):
        for b in (0, 1):
            greet(at(y, zf, core, (x + a) % 4, (zh + b) % 2))

    @pl.when(zl % 3 == 0)
    def _():
        for a in range(2):
            for d in range(2):
                greet(at(y, 2 * core + a, d, x, 1 - zh))

    for a in range(2):

        @pl.when(zl != 2 * core + a)
        def _():
            for d in range(2):
                greet(at(y, 2 * core + a, d, x, zh))

    for a in (2, 1, 3):
        for d in range(2):
            greet(at((y + a) % 4, zl, d, x, zh))
    greet(at(y, zl, 1 - core, x, zh))

    for load in loads[:4]:
        load.wait()
    sea = [paired(mask[l]).astype(F32) for l in range(2)]
    for l in range(2):
        couple = tiles_of(paired(dz[l]) * sea[l])
        for t in range(2):
            factor = paired(dev[t, l]) * sea[l]
            state = tiles_of(factor * paired(inc[t, l]))
            factor = tiles_of(factor)
            for j in range(TILES):
                scale[t, l, 8 * j : 8 * j + 8, :] = factor[j]
                spot = pl.ds(8 * (j % 2), 8)
                z_send[t, j // 2, 0, l, spot, :] = state[j]
                z_send[t, j // 2, 1, l, spot, :] = couple[j]
    for load in loads[4:]:
        load.wait()
    for l in range(2):
        sea_tiles = tiles_of(sea[l])
        west = from_west(sea_tiles, 1, lane)
        west[0] = jnp.where((lane == 0) & (sublane < 4), 0.0, west[0])
        couple_x, couple_y = tiles_of(paired(dx[l])), tiles_of(paired(dy[l]))
        for j in range(TILES):
            cx_send[l, 8 * j : 8 * j + 8, :] = couple_x[j] * sea_tiles[j] * west[j]
            cy_send[l, 8 * j : 8 * j + 8, :] = couple_y[j] * sea_tiles[j]

    pl.semaphore_wait(barrier, 20)

    for a in (2, 1, 3, 0):
        j = (x + a) % 4
        for t in range(2):
            send(z_send.at[(zh + t) % 2, j], z_recv.at[lev], TO_COLUMNS, at(y, zf, core, j, (zh + t) % 2))
    part = (zl % 2) * 2 + core
    lines_core = zl // 2
    for c_send, c_recv, phase in ((cy_send, cy_recv, COUPLE_Y), (cx_send, cx_recv, COUPLE_X)):
        for l in range(2):
            for b in (1, 0):
                zt = 3 * l if b else 1 + l
                target = at(y, zt, lines_core, x, (zh + b) % 2)
                src, dst = c_send.at[l], c_recv.at[pl.ds(pl.multiple_of(part * 64, 64), 64)]
                if b == 0:
                    send_or_keep(src, dst, phase, target, (zl == zt) & (core == lines_core))
                else:
                    send(src, dst, phase, target)

    def solve_levels(take, put):
        upper, lower = take(0), take(15)
        held = {0: upper, 15: lower}
        for k in range(7):
            held[k + 1] = take(k + 1) + z_factor[0, k] * held[k]
            held[14 - k] = take(14 - k) + z_factor[0, 15 - k] * held[15 - k]
        solved = z_factor[1, 8] * (held[8] + z_factor[0, 7] * held[7])
        put(8, solved)
        up = down = solved
        for k in range(8):
            up = z_factor[1, 7 - k] * held[7 - k] + z_factor[0, 7 - k] * up
            put(7 - k, up)
            if k < 7:
                down = z_factor[1, 9 + k] * held[9 + k] + z_factor[0, 9 + k] * down
                put(9 + k, down)

    wait(z_recv, recv_sem.at[TO_COLUMNS])
    upper = lower = jnp.ones((16, 128), F32)
    for k in range(8):
        c_up = z_recv[(k + 1) // 2, 1, (k + 1) % 2]
        inv = 1.0 / (upper + c_up)
        z_factor[0, k] = c_up * inv
        z_factor[1, k] = inv
        upper = 1.0 + c_up * inv * upper
        if k < 7:
            c_low = z_recv[(15 - k) // 2, 1, (15 - k) % 2]
            inv = 1.0 / (lower + c_low)
            z_factor[0, 15 - k] = c_low * inv
            z_factor[1, 15 - k] = inv
            lower = 1.0 + c_low * inv * lower
    z_factor[1, 8] = 1.0 / (upper + (lower - 1.0))

    def put_first(k, value):
        z_out[k] = value

    solve_levels(lambda k: z_recv[k // 2, 0, k % 2], put_first)

    from_core = zf // 2
    from_part = (zf % 2) * 2 + core
    for a in (2, 1, 3, 0):
        for b in (3, 1, 2, 0):
            x_, zl_ = (x + a) % 4, (zl + b) % 4
            src = z_out.at[level_at(x_, zl_)]
            dst = g_recv.at[pl.ds(pl.multiple_of(from_part * 64 + x * 16, 16), 16)]
            target = at(y, zl_, from_core, x_, zh)
            if a == 0 and b == 0:
                send_or_keep(src, dst, TO_LINES, target, from_core == core)
            else:
                send(src, dst, TO_LINES, target)

    wait(cy_recv, recv_sem.at[COUPLE_Y])

    def row_at(i, half):
        return pl.ds((i // 4) * 64 + (i % 4) + 32 * half, 8, stride=4)

    for half in range(2):
        n_send[8 * half : 8 * half + 8, :] = cy_recv[row_at(0, half), :]
    before = (mine + 7) % 8
    send(n_send, n_recv, NEXT_ROW, at(before // 2, zl, before % 2, x, zh))

    ring = []
    for a in (2, 1, 3):
        for d in range(2):
            ring.append(at((y + a) % 4, zl, (core + d) % 2, x, zh))
    ring.append(at(y, zl, 1 - core, x, zh))

    row = (mine * BLOCK + lax.broadcasted_iota(jnp.int32, (BLOCK, 128), 0)).astype(F32)
    weight = jnp.cos((-78.0 + 166.0 * (row + 0.5) / ROWS) * (math.pi / 180.0))
    inner = range(1, BLOCK)

    def total(terms):
        while len(terms) > 1:
            terms = [sum(terms[i : i + 2][1:], terms[i]) for i in range(0, len(terms), 2)]
        return terms[0]

    def solve_inner(rows, spot):
        here, held = None, [None] * BLOCK
        for i in inner:
            here = rows[i] if i == 1 else rows[i] + y_factor[0, i - 1, spot, :] * here
            held[i] = y_factor[1, i, spot, :] * here
        for i in range(BLOCK - 2, 0, -1):
            held[i] = held[i] + y_factor[0, i, spot, :] * held[i + 1]
        return held

    wait(n_recv, recv_sem.at[NEXT_ROW])
    for half in range(2):
        spot = pl.ds(8 * half, 8)
        faces = [cy_recv[row_at(i, half), :] for i in range(BLOCK)]
        north = jnp.where(mine < 7, n_recv[spot, :], 0.0)
        couple = [None] + [
            jnp.where(faces[i - 1] > 0.0, faces[i] if i < BLOCK else north, 0.0) for i in range(1, BLOCK + 1)
        ]
        ground = jnp.ones((8, 128), F32)
        own, link = jnp.ones((8, 128), F32), couple[1]
        to_own, to_next = [None] * BLOCK, [None] * BLOCK
        for i in inner:
            inv = 1.0 / (ground + (link + couple[i + 1]))
            to_own[i], to_next[i] = link * inv, couple[i + 1] * inv
            y_factor[0, i, spot, :] = to_next[i]
            y_factor[1, i, spot, :] = inv
            own = own + to_own[i] * ground
            link = to_own[i] * couple[i + 1]
            beyond = to_next[i] * ground
            ground = 1.0 + beyond
        r_all[mine, 0, spot, :] = own
        r_all[mine, 1, spot, :] = beyond
        r_all[mine, 2, spot, :] = link
        left, right = to_own[15], to_next[15]
        y_factor[2, 15, spot, :] = left
        y_factor[3, 15, spot, :] = right
        for i in range(BLOCK - 2, 0, -1):
            left = to_own[i] + to_next[i] * left
            right = to_next[i] * right
            y_factor[2, i, spot, :] = left
            y_factor[3, i, spot, :] = right
    for target in ring:
        send(r_all.at[mine], r_all.at[mine], REDUCED, target)

    wait(cx_recv, recv_sem.at[COUPLE_X])

    def bases():
        return [64 * part_ for part_ in range(4)]

    k = [[cx_recv[base + 8 * j : base + 8 * j + 8, :] for j in range(TILES)] for base in bases()]
    e = [[jnp.ones((8, 128), F32)] * TILES for _ in bases()]
    for i, stride in enumerate(STRIDES):
        for g, base in enumerate(bases()):
            k_east = from_east(k[g], stride, lane)
            inv = [1.0 / (a + (b + c)) for a, b, c in zip(e[g], k[g], k_east)]
            plus = [a * b for a, b in zip(k_east, inv)]
            minus = [a * b for a, b in zip(k[g], inv)]
            for j in range(TILES):
                x_factor[i, 0, base + 8 * j : base + 8 * j + 8, :] = plus[j]
                x_factor[i, 1, base + 8 * j : base + 8 * j + 8, :] = minus[j]
            west = from_west([a * b for a, b in zip(plus, e[g])], stride, lane)
            east = from_east([a * b for a, b in zip(minus, e[g])], stride, lane)
            k[g] = from_west([a * b for a, b in zip(plus, k[g])], stride, lane)
            e[g] = [a + (b + c) for a, b, c in zip(e[g], west, east)]
    for g, base in enumerate(bases()):
        for j in range(TILES):
            x_last[base + 8 * j : base + 8 * j + 8, :] = 1.0 / e[g][j]

    def longitude_solve(source, parts=(0, 1, 2, 3)):
        bases = lambda: [64 * part_ for part_ in parts]
        r = [[source[base + 8 * j : base + 8 * j + 8, :] for j in range(TILES)] for base in bases()]
        for i, stride in enumerate(STRIDES):
            for g, base in enumerate(bases()):
                plus = [x_factor[i, 0, base + 8 * j : base + 8 * j + 8, :] * r[g][j] for j in range(TILES)]
                minus = [x_factor[i, 1, base + 8 * j : base + 8 * j + 8, :] * r[g][j] for j in range(TILES)]
                west, east = from_west(plus, stride, lane), from_east(minus, stride, lane)
                r[g] = [a + (b + c) for a, b, c in zip(r[g], west, east)]
        for g, base in enumerate(bases()):
            for j in range(TILES):
                grid[base + 8 * j : base + 8 * j + 8, :] = r[g][j] * x_last[base + 8 * j : base + 8 * j + 8, :]

    def reduced_inverse():
        for half in range(2):
            spot = pl.ds(8 * half, 8)
            ground = [r_all[b, 0, spot, :] for b in range(8)]
            for b in range(1, 8):
                ground[b] = ground[b] + r_all[b - 1, 1, spot, :]
            link = [r_all[b, 2, spot, :] for b in range(7)]
            below, above = [ground[0]], [None] * 7 + [jnp.zeros((8, 128), F32)]
            north, south = [None] * 8, [None] * 8
            for b in range(7):
                inv = 1.0 / (below[b] + link[b])
                north[b] = link[b] * inv
                inverse[4, b, spot, :] = north[b]
                inverse[5, b, spot, :] = inv
                below.append(ground[b + 1] + north[b] * below[b])
            inverse[5, 7, spot, :] = 1.0 / below[7]
            for b in range(7, 0, -1):
                whole = ground[b] + above[b]
                south[b] = link[b - 1] / (whole + link[b - 1])
                above[b - 1] = south[b] * whole
            for which in range(2):
                spike = mine + which
                row_ = [None] * 8
                here = jnp.zeros((8, 128), F32)
                for b in range(7, -1, -1):
                    moved = here if b == 7 else north[b] * here
                    here = jnp.where(spike == b, 1.0 / (below[b] + above[b]), moved)
                    row_[b] = here
                here = jnp.zeros((8, 128), F32)
                for b in range(8):
                    moved = here if b == 0 else south[b] * here
                    here = jnp.where(spike < b, moved, row_[b])
                    inverse[which, b, spot, :] = here

    def weighted_inverse():
        for half in range(2):
            spot = pl.ds(8 * half, 8)
            middle = [w_all[b, 0, spot, :] for b in range(8)]
            for b in range(1, 8):
                middle[b] = middle[b] + w_all[b - 1, 2, spot, :]
            beside = [w_all[b, 1, spot, :] for b in range(7)]
            for which in range(2):
                g = [inverse[which, b, spot, :] for b in range(8)]
                right = [middle[b] * g[b] for b in range(8)]
                for b in range(7):
                    right[b] = right[b] + beside[b] * g[b + 1]
                    right[b + 1] = right[b + 1] + beside[b] * g[b]
                for b in range(7):
                    right[b + 1] = right[b + 1] + inverse[4, b, spot, :] * right[b]
                here = inverse[5, 7, spot, :] * right[7]
                inverse[2 + which, 7, spot, :] = here
                for b in range(6, -1, -1):
                    here = inverse[5, b, spot, :] * right[b] + inverse[4, b, spot, :] * here
                    inverse[2 + which, b, spot, :] = here

    def rows_of(half):
        return [grid[row_at(i, half), :] for i in range(BLOCK)]

    def put_rows(half, rows):
        for i in range(BLOCK):
            grid[row_at(i, half), :] = rows[i]

    def gathered(everyone, first, half):
        values = [everyone[b, pl.ds(16 * first + 8 * half, 8), :] for b in range(8)]
        for b in range(1, 8):
            values[b] = values[b] + everyone[b - 1, pl.ds(16 * (first + 1) + 8 * half, 8), :]
        return values

    def applied(which, values, spot):
        return [inverse[which, b, spot, :] * values[b] for b in range(8)]

    def tell(everyone, phase):
        for target in ring:
            send(everyone.at[mine], everyone.at[mine], phase, target)

    def latitude_solve(everyone, phase, behind=None, between=None):
        inside = []
        for half in range(2):
            spot = pl.ds(8 * half, 8)
            rows = rows_of(half)
            own = total([rows[0]] + [y_factor[2, i, spot, :] * rows[i] for i in inner])
            beyond = total([y_factor[3, i, spot, :] * rows[i] for i in inner])
            everyone[mine, spot, :] = own
            everyone[mine, pl.ds(16 + 8 * half, 8), :] = beyond
        tell(everyone, phase)
        if behind is not None:
            behind()
        for half in range(2):
            inside.append(solve_inner(rows_of(half), pl.ds(8 * half, 8)))
        if between is not None:
            between()
        wait(everyone.at[pl.ds(0, 7)], recv_sem.at[phase])
        for half in range(2):
            spot = pl.ds(8 * half, 8)
            right = gathered(everyone, 0, half)
            first, last = (total(applied(which, right, spot)) for which in range(2))
            put_rows(half, [first] + [
                inside[half][i] + (y_factor[2, i, spot, :] * first + y_factor[3, i, spot, :] * last) for i in inner
            ])

    def latitude_pair(everyone, phase):
        inside = []
        for half in range(2):
            spot = pl.ds(8 * half, 8)
            rows = rows_of(half)
            for k in range(4):
                terms = [y_factor[2 + k, i, spot, :] * rows[i] for i in inner]
                everyone[mine, pl.ds(16 * k + 8 * half, 8), :] = total(([rows[0]] if k == 0 else []) + terms)
        tell(everyone, phase)
        for half in range(2):
            spot = pl.ds(8 * half, 8)
            once = solve_inner(rows_of(half), spot)
            inside.append(solve_inner([None] + [once[i] * weight[i : i + 1, :] for i in inner], spot))
        wait(w_all.at[pl.ds(0, 7)], recv_sem.at[WEIGHTED])
        weighted_inverse()
        wait(everyone.at[pl.ds(0, 7)], recv_sem.at[phase])
        for half in range(2):
            spot = pl.ds(8 * half, 8)
            right, more = gathered(everyone, 0, half), gathered(everyone, 2, half)
            ends = [total(applied(which, right, spot)) for which in range(2)]
            ends += [total(applied(2 + k, right, spot) + applied(k, more, spot)) for k in range(2)]
            put_rows(half, [ends[2]] + [
                inside[half][i]
                + (y_factor[4, i, spot, :] * ends[0] + y_factor[5, i, spot, :] * ends[1])
                + (y_factor[2, i, spot, :] * ends[2] + y_factor[3, i, spot, :] * ends[3])
                for i in inner
            ])

    def weighted_block():
        for half in range(2):
            spot = pl.ds(8 * half, 8)
            sides = [[None] + [y_factor[2 + k, i, spot, :] for i in inner] for k in range(2)]
            loaded = [[None] + [side[i] * weight[i : i + 1, :] for i in inner] for side in sides]
            w_all[mine, 0, spot, :] = weight[0:1, :] + total([sides[0][i] * loaded[0][i] for i in inner])
            w_all[mine, 1, spot, :] = total([sides[0][i] * loaded[1][i] for i in inner])
            w_all[mine, 2, spot, :] = total([sides[1][i] * loaded[1][i] for i in inner])
            for k in range(2):
                twice = solve_inner(loaded[k], spot)
                for i in inner:
                    y_factor[4 + k, i, spot, :] = twice[i]
        tell(w_all, WEIGHTED)

    def first_between():
        wait(r_all.at[pl.ds(0, 7)], recv_sem.at[REDUCED])
        reduced_inverse()

    wait(g_recv, recv_sem.at[TO_LINES])
    longitude_solve(g_recv)
    latitude_solve(y_all.at[0], LATITUDE_A, weighted_block, first_between)
    longitude_solve(grid)
    latitude_pair(f_all, LATITUDE_B)
    longitude_solve(grid)
    latitude_solve(y_all.at[1], LATITUDE_C)

    level = level_at(x, zl)
    for first in (0, 2):
        longitude_solve(grid, (first, first + 1))
        for a in (2, 1, 3, 0):
            x_ = (x + a) % 4
            for b in (first, first + 1):
                zl_, core_ = (2 * core + b // 2 + 2) % 4, b % 2
                src = grid.at[pl.ds(pl.multiple_of(b * 64 + x_ * 16, 16), 16)]
                target = at(y, zl_, core_, x_, zh)
                if a == 0:
                    send_or_keep(src, zb_recv.at[level], BACK_COLUMNS, target, (zl_ == zl) & (core_ == core))
                else:
                    send(src, zb_recv.at[level], BACK_COLUMNS, target)
    wait(zb_recv, recv_sem.at[BACK_COLUMNS])

    def put_last(k, value):
        zb_out[k] = value

    solve_levels(lambda k: zb_recv[k], put_last)
    for a in (2, 1, 3, 0):
        for b in range(2):
            x_ = (x + a) % 4
            src = zb_out.at[pl.ds(x_ * 4 + b * 2, 2)]
            dst = r_recv.at[zh, :, pl.ds(pl.multiple_of(x * 16, 16), 16)]
            send(src, dst, BACK_ROWS + zh, at(y, zf, core, x_, b))
    stores = []
    for t in range(2):
        wait(r_recv.at[t], recv_sem.at[BACK_ROWS + t])
        for l in range(2):
            for j in range(TILES):
                spot = pl.ds(8 * j, 8)
                tile = scale[t, l, spot, :] * r_recv[t, l, spot, :]
                result[t, l, :, 128 * j : 128 * j + 128] = tile[:4]
                result[t, l, :, HALF + 128 * j : HALF + 128 * j + 128] = tile[4:]
            stores.append(pltpu.make_async_copy(result.at[t, l], out_ref.at[t, l], in_sem.at[2 * t + l]))
            stores[-1].start()

    wait(z_send.at[:, :, :, :], send_sem.at[TO_COLUMNS])
    for c_send, phase in ((cy_send, COUPLE_Y), (cx_send, COUPLE_X)):
        for l in range(2):
            wait(c_send.at[l], send_sem.at[phase])

            @pl.when(jnp.logical_not((zl == 1 + l) & (core == lines_core)))
            def _():
                wait(c_send.at[l], send_sem.at[phase])

    wait(z_out.at[pl.ds(0, 15)], send_sem.at[TO_LINES])

    @pl.when(from_core != core)
    def _():
        wait(z_out.at[15], send_sem.at[TO_LINES])

    wait(n_send, send_sem.at[NEXT_ROW])
    wait(r_all.at[pl.ds(0, 7)], send_sem.at[REDUCED])
    wait(w_all.at[pl.ds(0, 7)], send_sem.at[WEIGHTED])
    wait(y_all.at[0, pl.ds(0, 7)], send_sem.at[LATITUDE_A])
    wait(f_all.at[pl.ds(0, 7)], send_sem.at[LATITUDE_B])
    wait(y_all.at[1, pl.ds(0, 7)], send_sem.at[LATITUDE_C])
    wait(zb_recv.at[pl.ds(0, 15)], send_sem.at[BACK_COLUMNS])
    base = (zl - 2 * core + 2) % 4

    @pl.when(base >= 2)
    def _():
        wait(zb_recv.at[15], send_sem.at[BACK_COLUMNS])

    wait(r_recv, send_sem.at[BACK_ROWS + zh])
    for store in stores:
        store.wait()


def per_device(increment, deviations, diffuse_x, diffuse_y, diffuse_z, sea_mask):
    vmem = lambda *shape: pltpu.VMEM(shape, F32)
    shape = increment.shape
    plane = diffuse_x.shape
    return pl.pallas_call(
        kernel,
        out_shape=jax.ShapeDtypeStruct(shape, F32),
        in_specs=[pl.BlockSpec(memory_space=pl.ANY)] * 6,
        out_specs=pl.BlockSpec(memory_space=pl.ANY),
        scratch_shapes=[
            vmem(*shape), vmem(*shape), vmem(*plane), vmem(*plane), vmem(*plane), pltpu.VMEM(plane, jnp.int32),
            vmem(2, 2, 64, 128), vmem(*shape),
            vmem(2, 4, 2, 2, 16, 128), vmem(8, 2, 2, 16, 128), vmem(2, 16, 16, 128), vmem(16, 16, 128),
            vmem(256, 128), vmem(2, 64, 128), vmem(256, 128), vmem(2, 64, 128), vmem(256, 128), vmem(16, 128), vmem(16, 128),
            vmem(11, 2, 256, 128), vmem(256, 128), vmem(6, 16, 16, 128), vmem(8, 3, 16, 128), vmem(8, 3, 16, 128),
            vmem(6, 8, 16, 128), vmem(2, 8, 32, 128), vmem(8, 64, 128), vmem(256, 128), vmem(16, 16, 128), vmem(16, 16, 128), vmem(2, 2, 64, 128),
            pltpu.SemaphoreType.DMA((6,)), pltpu.SemaphoreType.DMA((13,)), pltpu.SemaphoreType.DMA((13,)),
        ],
        compiler_params=pltpu.CompilerParams(
            collective_id=0, has_side_effects=True, vmem_limit_bytes=60 * 1024 * 1024
        ),
        name="covariance",
    )(increment, deviations, diffuse_x, diffuse_y, diffuse_z, sea_mask)


def solution(mesh):
    in_specs = (
        P(None, "lev", "lat", None),
        P(None, "lev", "lat", None),
        P("lev", "lat", None),
        P("lev", "lat", None),
        P("lev", "lat", None),
        P("lev", "lat", None),
    )
    out_specs = P(None, "lev", "lat", None)
    return jax.shard_map(
        per_device, mesh=mesh, in_specs=in_specs, out_specs=out_specs, check_vma=False
    )
```

```python
import math

import jax
import jax.numpy as jnp
from jax import lax
from jax.experimental import pallas as pl
from jax.experimental.pallas import tpu as pltpu
from jax.sharding import PartitionSpec as P

MESH = pl.DeviceIdType.MESH
F32 = jnp.float32
LEVELS, HALF, TILES, BLOCK, ROWS = 16, 1024, 8, 16, 128
STRIDES = (1, 2, 4, 8, 16, 32, 64, 128, 256, 512, 1024)
TO_COLUMNS, TO_LINES, COUPLE_X, COUPLE_Y, NEXT_ROW, REDUCED, WEIGHTED = range(7)
LATITUDE_A, LATITUDE_B, LATITUDE_C, BACK_COLUMNS, BACK_ROWS = range(7, 12)


def swap_halves(tile):
    return pltpu.roll(tile, 4, 0)


def from_west(tiles, stride, lane):
    if stride >= 128:
        k = stride // 128
        return [tiles[j - k] if j >= k else swap_halves(tiles[TILES + j - k]) for j in range(TILES)]
    turned = [pltpu.roll(tile, stride, 1) for tile in tiles]
    carry = [swap_halves(turned[-1])] + turned[:-1]
    return [jnp.where(lane < stride, c, t) for c, t in zip(carry, turned)]


def from_east(tiles, stride, lane):
    if stride >= 128:
        k = stride // 128
        return [tiles[j + k] if j + k < TILES else swap_halves(tiles[j + k - TILES]) for j in range(TILES)]
    turned = [pltpu.roll(tile, 128 - stride, 1) for tile in tiles]
    carry = turned[1:] + [swap_halves(turned[0])]
    return [jnp.where(lane >= 128 - stride, c, t) for c, t in zip(carry, turned)]


def paired(rows):
    return jnp.concatenate([rows[:, :HALF], rows[:, HALF:]], axis=0)


def tiles_of(wide):
    return [wide[:, 128 * j : 128 * (j + 1)] for j in range(TILES)]


def kernel(
    inc_hbm, dev_hbm, dx_hbm, dy_hbm, dz_hbm, sea_hbm, out_ref,
    inc, dev, dx, dy, dz, mask, scale, result,
    z_send, z_recv, z_factor, z_out, g_recv, cx_send, cx_recv, cy_send, cy_recv, n_send, n_recv,
    x_factor, x_last, y_factor, r_all, w_all, inverse, y_all, f_all, grid, zb_recv, zb_out, r_recv,
    in_sem, send_sem, recv_sem,
):
    lat, lev = lax.axis_index("lat"), lax.axis_index("lev")
    y, zl, core = lat // 8, (lat // 2) % 4, lat % 2
    x, zh = lev // 2, lev % 2
    mine = y * 2 + core
    lane = lax.broadcasted_iota(jnp.int32, (8, 128), 1)
    sublane = lax.broadcasted_iota(jnp.int32, (8, 128), 0)

    def at(y_, zl_, core_, x_, zh_):
        return {"lat": y_ * 8 + zl_ * 2 + core_, "lev": x_ * 2 + zh_}

    def level_at(x_, zl_):
        inner = ((zl_ + 1) // 2) % 2
        return x_ * 4 + 2 * ((zh + 1 + inner) % 2) + zl_ // 2

    def send(src, dst, phase, target):
        pltpu.make_async_remote_copy(
            src_ref=src, dst_ref=dst, send_sem=send_sem.at[phase], recv_sem=recv_sem.at[phase],
            device_id=target, device_id_type=MESH,
        ).start()

    def send_or_keep(src, dst, phase, target, here):
        @pl.when(here)
        def _():
            pltpu.make_async_copy(src, dst, recv_sem.at[phase]).start()

        @pl.when(jnp.logical_not(here))
        def _():
            send(src, dst, phase, target)

    def wait(ref, sem):
        pltpu.make_async_copy(ref, ref, sem).wait()

    loads = [
        pltpu.make_async_copy(src, dst, in_sem.at[i])
        for i, (src, dst) in enumerate(
            [(sea_hbm, mask), (dev_hbm, dev), (inc_hbm, inc), (dz_hbm, dz), (dx_hbm, dx), (dy_hbm, dy)]
        )
    ]
    for load in loads:
        load.start()

    zf = (zl + 2) % 4
    barrier = pltpu.get_barrier_semaphore()

    def greet(target):
        pl.semaphore_signal(barrier, inc=1, device_id=target, device_id_type=MESH)

    for a in (2, 1, 3, 0):
        for b in (0, 1):
            greet(at(y, zf, core, (x + a) % 4, (zh + b) % 2))

    @pl.when(zl % 3 == 0)
    def _():
        for a in range(2):
            for d in range(2):
                greet(at(y, 2 * core + a, d, x, 1 - zh))

    for a in range(2):

        @pl.when(zl != 2 * core + a)
        def _():
            for d in range(2):
                greet(at(y, 2 * core + a, d, x, zh))

    for a in (2, 1, 3):
        for d in range(2):
            greet(at((y + a) % 4, zl, d, x, zh))
    greet(at(y, zl, 1 - core, x, zh))

    for load in loads[:4]:
        load.wait()
    sea = [paired(mask[l]).astype(F32) for l in range(2)]
    for l in range(2):
        couple = tiles_of(paired(dz[l]) * sea[l])
        for t in range(2):
            factor = paired(dev[t, l]) * sea[l]
            state = tiles_of(factor * paired(inc[t, l]))
            factor = tiles_of(factor)
            for j in range(TILES):
                scale[t, l, 8 * j : 8 * j + 8, :] = factor[j]
                spot = pl.ds(8 * (j % 2), 8)
                z_send[t, j // 2, 0, l, spot, :] = state[j]
                z_send[t, j // 2, 1, l, spot, :] = couple[j]
    for load in loads[4:]:
        load.wait()
    for l in range(2):
        sea_tiles = tiles_of(sea[l])
        west = from_west(sea_tiles, 1, lane)
        west[0] = jnp.where((lane == 0) & (sublane < 4), 0.0, west[0])
        couple_x, couple_y = tiles_of(paired(dx[l])), tiles_of(paired(dy[l]))
        for j in range(TILES):
            cx_send[l, 8 * j : 8 * j + 8, :] = couple_x[j] * sea_tiles[j] * west[j]
            cy_send[l, 8 * j : 8 * j + 8, :] = couple_y[j] * sea_tiles[j]

    pl.semaphore_wait(barrier, 20)

    for a in (2, 1, 3, 0):
        j = (x + a) % 4
        for t in range(2):
            send(z_send.at[(zh + t) % 2, j], z_recv.at[lev], TO_COLUMNS, at(y, zf, core, j, (zh + t) % 2))
    part = (zl % 2) * 2 + core
    lines_core = zl // 2
    for c_send, c_recv, phase in ((cy_send, cy_recv, COUPLE_Y),):
        for l in range(2):
            for b in (1, 0):
                zt = 3 * l if b else 1 + l
                target = at(y, zt, lines_core, x, (zh + b) % 2)
                src, dst = c_send.at[l], c_recv.at[pl.ds(pl.multiple_of(part * 64, 64), 64)]
                if b == 0:
                    send_or_keep(src, dst, phase, target, (zl == zt) & (core == lines_core))
                else:
                    send(src, dst, phase, target)

    def solve_levels(take, put):
        upper, lower = take(0), take(15)
        held = {0: upper, 15: lower}
        for k in range(7):
            held[k + 1] = take(k + 1) + z_factor[0, k] * held[k]
            held[14 - k] = take(14 - k) + z_factor[0, 15 - k] * held[15 - k]
        solved = z_factor[1, 8] * (held[8] + z_factor[0, 7] * held[7])
        put(8, solved)
        up = down = solved
        for k in range(8):
            up = z_factor[1, 7 - k] * held[7 - k] + z_factor[0, 7 - k] * up
            put(7 - k, up)
            if k < 7:
                down = z_factor[1, 9 + k] * held[9 + k] + z_factor[0, 9 + k] * down
                put(9 + k, down)

    wait(z_recv, recv_sem.at[TO_COLUMNS])
    for c_send, c_recv, phase in ((cx_send, cx_recv, COUPLE_X),):
        for l in range(2):
            for b in (1, 0):
                zt = 3 * l if b else 1 + l
                target = at(y, zt, lines_core, x, (zh + b) % 2)
                src, dst = c_send.at[l], c_recv.at[pl.ds(pl.multiple_of(part * 64, 64), 64)]
                if b == 0:
                    send_or_keep(src, dst, phase, target, (zl == zt) & (core == lines_core))
                else:
                    send(src, dst, phase, target)

    upper = lower = jnp.ones((16, 128), F32)
    for k in range(8):
        c_up = z_recv[(k + 1) // 2, 1, (k + 1) % 2]
        inv = 1.0 / (upper + c_up)
        z_factor[0, k] = c_up * inv
        z_factor[1, k] = inv
        upper = 1.0 + c_up * inv * upper
        if k < 7:
            c_low = z_recv[(15 - k) // 2, 1, (15 - k) % 2]
            inv = 1.0 / (lower + c_low)
            z_factor[0, 15 - k] = c_low * inv
            z_factor[1, 15 - k] = inv
            lower = 1.0 + c_low * inv * lower
    z_factor[1, 8] = 1.0 / (upper + (lower - 1.0))

    def put_first(k, value):
        z_out[k] = value

    solve_levels(lambda k: z_recv[k // 2, 0, k % 2], put_first)

    from_core = zf // 2
    from_part = (zf % 2) * 2 + core
    for a in (2, 1, 3, 0):
        for b in (3, 1, 2, 0):
            x_, zl_ = (x + a) % 4, (zl + b) % 4
            src = z_out.at[level_at(x_, zl_)]
            dst = g_recv.at[pl.ds(pl.multiple_of(from_part * 64 + x * 16, 16), 16)]
            target = at(y, zl_, from_core, x_, zh)
            if a == 0 and b == 0:
                send_or_keep(src, dst, TO_LINES, target, from_core == core)
            else:
                send(src, dst, TO_LINES, target)

    wait(cy_recv, recv_sem.at[COUPLE_Y])

    def row_at(i, half):
        return pl.ds((i // 4) * 64 + (i % 4) + 32 * half, 8, stride=4)

    for half in range(2):
        n_send[8 * half : 8 * half + 8, :] = cy_recv[row_at(0, half), :]
    before = (mine + 7) % 8
    send(n_send, n_recv, NEXT_ROW, at(before // 2, zl, before % 2, x, zh))

    ring = []
    for a in (2, 1, 3):
        for d in range(2):
            ring.append(at((y + a) % 4, zl, (core + d) % 2, x, zh))
    ring.append(at(y, zl, 1 - core, x, zh))

    row = (mine * BLOCK + lax.broadcasted_iota(jnp.int32, (BLOCK, 128), 0)).astype(F32)
    weight = jnp.cos((-78.0 + 166.0 * (row + 0.5) / ROWS) * (math.pi / 180.0))
    inner = range(1, BLOCK)

    def total(terms):
        while len(terms) > 1:
            terms = [sum(terms[i : i + 2][1:], terms[i]) for i in range(0, len(terms), 2)]
        return terms[0]

    def solve_inner(rows, spot):
        here, held = None, [None] * BLOCK
        for i in inner:
            here = rows[i] if i == 1 else rows[i] + y_factor[0, i - 1, spot, :] * here
            held[i] = y_factor[1, i, spot, :] * here
        for i in range(BLOCK - 2, 0, -1):
            held[i] = held[i] + y_factor[0, i, spot, :] * held[i + 1]
        return held

    wait(n_recv, recv_sem.at[NEXT_ROW])
    for half in range(2):
        spot = pl.ds(8 * half, 8)
        faces = [cy_recv[row_at(i, half), :] for i in range(BLOCK)]
        north = jnp.where(mine < 7, n_recv[spot, :], 0.0)
        couple = [None] + [
            jnp.where(faces[i - 1] > 0.0, faces[i] if i < BLOCK else north, 0.0) for i in range(1, BLOCK + 1)
        ]
        ground = jnp.ones((8, 128), F32)
        own, link = jnp.ones((8, 128), F32), couple[1]
        to_own, to_next = [None] * BLOCK, [None] * BLOCK
        for i in inner:
            inv = 1.0 / (ground + (link + couple[i + 1]))
            to_own[i], to_next[i] = link * inv, couple[i + 1] * inv
            y_factor[0, i, spot, :] = to_next[i]
            y_factor[1, i, spot, :] = inv
            own = own + to_own[i] * ground
            link = to_own[i] * couple[i + 1]
            beyond = to_next[i] * ground
            ground = 1.0 + beyond
        r_all[mine, 0, spot, :] = own
        r_all[mine, 1, spot, :] = beyond
        r_all[mine, 2, spot, :] = link
        left, right = to_own[15], to_next[15]
        y_factor[2, 15, spot, :] = left
        y_factor[3, 15, spot, :] = right
        for i in range(BLOCK - 2, 0, -1):
            left = to_own[i] + to_next[i] * left
            right = to_next[i] * right
            y_factor[2, i, spot, :] = left
            y_factor[3, i, spot, :] = right
    for target in ring:
        send(r_all.at[mine], r_all.at[mine], REDUCED, target)

    wait(cx_recv, recv_sem.at[COUPLE_X])

    def bases():
        return [64 * part_ for part_ in range(4)]

    k = [[cx_recv[base + 8 * j : base + 8 * j + 8, :] for j in range(TILES)] for base in bases()]
    e = [[jnp.ones((8, 128), F32)] * TILES for _ in bases()]
    for i, stride in enumerate(STRIDES):
        for g, base in enumerate(bases()):
            k_east = from_east(k[g], stride, lane)
            inv = [1.0 / (a + (b + c)) for a, b, c in zip(e[g], k[g], k_east)]
            plus = [a * b for a, b in zip(k_east, inv)]
            minus = [a * b for a, b in zip(k[g], inv)]
            for j in range(TILES):
                x_factor[i, 0, base + 8 * j : base + 8 * j + 8, :] = plus[j]
                x_factor[i, 1, base + 8 * j : base + 8 * j + 8, :] = minus[j]
            west = from_west([a * b for a, b in zip(plus, e[g])], stride, lane)
            east = from_east([a * b for a, b in zip(minus, e[g])], stride, lane)
            k[g] = from_west([a * b for a, b in zip(plus, k[g])], stride, lane)
            e[g] = [a + (b + c) for a, b, c in zip(e[g], west, east)]
    for g, base in enumerate(bases()):
        for j in range(TILES):
            x_last[base + 8 * j : base + 8 * j + 8, :] = 1.0 / e[g][j]

    def longitude_solve(source, parts=(0, 1, 2, 3)):
        bases = lambda: [64 * part_ for part_ in parts]
        r = [[source[base + 8 * j : base + 8 * j + 8, :] for j in range(TILES)] for base in bases()]
        for i, stride in enumerate(STRIDES):
            for g, base in enumerate(bases()):
                plus = [x_factor[i, 0, base + 8 * j : base + 8 * j + 8, :] * r[g][j] for j in range(TILES)]
                minus = [x_factor[i, 1, base + 8 * j : base + 8 * j + 8, :] * r[g][j] for j in range(TILES)]
                west, east = from_west(plus, stride, lane), from_east(minus, stride, lane)
                r[g] = [a + (b + c) for a, b, c in zip(r[g], west, east)]
        for g, base in enumerate(bases()):
            for j in range(TILES):
                grid[base + 8 * j : base + 8 * j + 8, :] = r[g][j] * x_last[base + 8 * j : base + 8 * j + 8, :]

    def reduced_inverse():
        for half in range(2):
            spot = pl.ds(8 * half, 8)
            ground = [r_all[b, 0, spot, :] for b in range(8)]
            for b in range(1, 8):
                ground[b] = ground[b] + r_all[b - 1, 1, spot, :]
            link = [r_all[b, 2, spot, :] for b in range(7)]
            below, above = [ground[0]], [None] * 7 + [jnp.zeros((8, 128), F32)]
            north, south = [None] * 8, [None] * 8
            for b in range(7):
                inv = 1.0 / (below[b] + link[b])
                north[b] = link[b] * inv
                inverse[4, b, spot, :] = north[b]
                inverse[5, b, spot, :] = inv
                below.append(ground[b + 1] + north[b] * below[b])
            inverse[5, 7, spot, :] = 1.0 / below[7]
            for b in range(7, 0, -1):
                whole = ground[b] + above[b]
                south[b] = link[b - 1] / (whole + link[b - 1])
                above[b - 1] = south[b] * whole
            for which in range(2):
                spike = mine + which
                row_ = [None] * 8
                here = jnp.zeros((8, 128), F32)
                for b in range(7, -1, -1):
                    moved = here if b == 7 else north[b] * here
                    here = jnp.where(spike == b, 1.0 / (below[b] + above[b]), moved)
                    row_[b] = here
                here = jnp.zeros((8, 128), F32)
                for b in range(8):
                    moved = here if b == 0 else south[b] * here
                    here = jnp.where(spike < b, moved, row_[b])
                    inverse[which, b, spot, :] = here

    def weighted_inverse():
        for half in range(2):
            spot = pl.ds(8 * half, 8)
            middle = [w_all[b, 0, spot, :] for b in range(8)]
            for b in range(1, 8):
                middle[b] = middle[b] + w_all[b - 1, 2, spot, :]
            beside = [w_all[b, 1, spot, :] for b in range(7)]
            for which in range(2):
                g = [inverse[which, b, spot, :] for b in range(8)]
                right = [middle[b] * g[b] for b in range(8)]
                for b in range(7):
                    right[b] = right[b] + beside[b] * g[b + 1]
                    right[b + 1] = right[b + 1] + beside[b] * g[b]
                for b in range(7):
                    right[b + 1] = right[b + 1] + inverse[4, b, spot, :] * right[b]
                here = inverse[5, 7, spot, :] * right[7]
                inverse[2 + which, 7, spot, :] = here
                for b in range(6, -1, -1):
                    here = inverse[5, b, spot, :] * right[b] + inverse[4, b, spot, :] * here
                    inverse[2 + which, b, spot, :] = here

    def rows_of(half):
        return [grid[row_at(i, half), :] for i in range(BLOCK)]

    def put_rows(half, rows):
        for i in range(BLOCK):
            grid[row_at(i, half), :] = rows[i]

    def gathered(everyone, first, half):
        values = [everyone[b, pl.ds(16 * first + 8 * half, 8), :] for b in range(8)]
        for b in range(1, 8):
            values[b] = values[b] + everyone[b - 1, pl.ds(16 * (first + 1) + 8 * half, 8), :]
        return values

    def applied(which, values, spot):
        return [inverse[which, b, spot, :] * values[b] for b in range(8)]

    def tell(everyone, phase):
        for target in ring:
            send(everyone.at[mine], everyone.at[mine], phase, target)

    def latitude_solve(everyone, phase, behind=None, between=None):
        inside = []
        for half in range(2):
            spot = pl.ds(8 * half, 8)
            rows = rows_of(half)
            own = total([rows[0]] + [y_factor[2, i, spot, :] * rows[i] for i in inner])
            beyond = total([y_factor[3, i, spot, :] * rows[i] for i in inner])
            everyone[mine, spot, :] = own
            everyone[mine, pl.ds(16 + 8 * half, 8), :] = beyond
        tell(everyone, phase)
        if behind is not None:
            behind()
        for half in range(2):
            inside.append(solve_inner(rows_of(half), pl.ds(8 * half, 8)))
        if between is not None:
            between()
        wait(everyone.at[pl.ds(0, 7)], recv_sem.at[phase])
        for half in range(2):
            spot = pl.ds(8 * half, 8)
            right = gathered(everyone, 0, half)
            first, last = (total(applied(which, right, spot)) for which in range(2))
            put_rows(half, [first] + [
                inside[half][i] + (y_factor[2, i, spot, :] * first + y_factor[3, i, spot, :] * last) for i in inner
            ])

    def latitude_pair(everyone, phase):
        inside = []
        for half in range(2):
            spot = pl.ds(8 * half, 8)
            rows = rows_of(half)
            for k in range(4):
                terms = [y_factor[2 + k, i, spot, :] * rows[i] for i in inner]
                everyone[mine, pl.ds(16 * k + 8 * half, 8), :] = total(([rows[0]] if k == 0 else []) + terms)
        tell(everyone, phase)
        for half in range(2):
            spot = pl.ds(8 * half, 8)
            once = solve_inner(rows_of(half), spot)
            inside.append(solve_inner([None] + [once[i] * weight[i : i + 1, :] for i in inner], spot))
        wait(w_all.at[pl.ds(0, 7)], recv_sem.at[WEIGHTED])
        weighted_inverse()
        wait(everyone.at[pl.ds(0, 7)], recv_sem.at[phase])
        for half in range(2):
            spot = pl.ds(8 * half, 8)
            right, more = gathered(everyone, 0, half), gathered(everyone, 2, half)
            ends = [total(applied(which, right, spot)) for which in range(2)]
            ends += [total(applied(2 + k, right, spot) + applied(k, more, spot)) for k in range(2)]
            put_rows(half, [ends[2]] + [
                inside[half][i]
                + (y_factor[4, i, spot, :] * ends[0] + y_factor[5, i, spot, :] * ends[1])
                + (y_factor[2, i, spot, :] * ends[2] + y_factor[3, i, spot, :] * ends[3])
                for i in inner
            ])

    def weighted_block():
        for half in range(2):
            spot = pl.ds(8 * half, 8)
            sides = [[None] + [y_factor[2 + k, i, spot, :] for i in inner] for k in range(2)]
            loaded = [[None] + [side[i] * weight[i : i + 1, :] for i in inner] for side in sides]
            w_all[mine, 0, spot, :] = weight[0:1, :] + total([sides[0][i] * loaded[0][i] for i in inner])
            w_all[mine, 1, spot, :] = total([sides[0][i] * loaded[1][i] for i in inner])
            w_all[mine, 2, spot, :] = total([sides[1][i] * loaded[1][i] for i in inner])
            for k in range(2):
                twice = solve_inner(loaded[k], spot)
                for i in inner:
                    y_factor[4 + k, i, spot, :] = twice[i]
        tell(w_all, WEIGHTED)

    def first_between():
        wait(r_all.at[pl.ds(0, 7)], recv_sem.at[REDUCED])
        reduced_inverse()

    wait(g_recv, recv_sem.at[TO_LINES])
    longitude_solve(g_recv)
    latitude_solve(y_all.at[0], LATITUDE_A, weighted_block, first_between)
    longitude_solve(grid)
    latitude_pair(f_all, LATITUDE_B)
    longitude_solve(grid)
    latitude_solve(y_all.at[1], LATITUDE_C)

    level = level_at(x, zl)
    for first in (0, 2):
        longitude_solve(grid, (first, first + 1))
        for a in (2, 1, 3, 0):
            x_ = (x + a) % 4
            for b in (first, first + 1):
                zl_, core_ = (2 * core + b // 2 + 2) % 4, b % 2
                src = grid.at[pl.ds(pl.multiple_of(b * 64 + x_ * 16, 16), 16)]
                target = at(y, zl_, core_, x_, zh)
                if a == 0:
                    send_or_keep(src, zb_recv.at[level], BACK_COLUMNS, target, (zl_ == zl) & (core_ == core))
                else:
                    send(src, zb_recv.at[level], BACK_COLUMNS, target)
    wait(zb_recv, recv_sem.at[BACK_COLUMNS])

    def put_last(k, value):
        zb_out[k] = value

    solve_levels(lambda k: zb_recv[k], put_last)
    for a in (2, 1, 3, 0):
        for b in range(2):
            x_ = (x + a) % 4
            src = zb_out.at[pl.ds(x_ * 4 + b * 2, 2)]
            dst = r_recv.at[zh, :, pl.ds(pl.multiple_of(x * 16, 16), 16)]
            send(src, dst, BACK_ROWS + zh, at(y, zf, core, x_, b))
    stores = []
    for t in range(2):
        wait(r_recv.at[t], recv_sem.at[BACK_ROWS + t])
        for l in range(2):
            for j in range(TILES):
                spot = pl.ds(8 * j, 8)
                tile = scale[t, l, spot, :] * r_recv[t, l, spot, :]
                result[t, l, :, 128 * j : 128 * j + 128] = tile[:4]
                result[t, l, :, HALF + 128 * j : HALF + 128 * j + 128] = tile[4:]
            stores.append(pltpu.make_async_copy(result.at[t, l], out_ref.at[t, l], in_sem.at[2 * t + l]))
            stores[-1].start()

    wait(z_send.at[:, :, :, :], send_sem.at[TO_COLUMNS])
    for c_send, phase in ((cy_send, COUPLE_Y), (cx_send, COUPLE_X)):
        for l in range(2):
            wait(c_send.at[l], send_sem.at[phase])

            @pl.when(jnp.logical_not((zl == 1 + l) & (core == lines_core)))
            def _():
                wait(c_send.at[l], send_sem.at[phase])

    wait(z_out.at[pl.ds(0, 15)], send_sem.at[TO_LINES])

    @pl.when(from_core != core)
    def _():
        wait(z_out.at[15], send_sem.at[TO_LINES])

    wait(n_send, send_sem.at[NEXT_ROW])
    wait(r_all.at[pl.ds(0, 7)], send_sem.at[REDUCED])
    wait(w_all.at[pl.ds(0, 7)], send_sem.at[WEIGHTED])
    wait(y_all.at[0, pl.ds(0, 7)], send_sem.at[LATITUDE_A])
    wait(f_all.at[pl.ds(0, 7)], send_sem.at[LATITUDE_B])
    wait(y_all.at[1, pl.ds(0, 7)], send_sem.at[LATITUDE_C])
    wait(zb_recv.at[pl.ds(0, 15)], send_sem.at[BACK_COLUMNS])
    base = (zl - 2 * core + 2) % 4

    @pl.when(base >= 2)
    def _():
        wait(zb_recv.at[15], send_sem.at[BACK_COLUMNS])

    wait(r_recv, send_sem.at[BACK_ROWS + zh])
    for store in stores:
        store.wait()


def per_device(increment, deviations, diffuse_x, diffuse_y, diffuse_z, sea_mask):
    vmem = lambda *shape: pltpu.VMEM(shape, F32)
    shape = increment.shape
    plane = diffuse_x.shape
    return pl.pallas_call(
        kernel,
        out_shape=jax.ShapeDtypeStruct(shape, F32),
        in_specs=[pl.BlockSpec(memory_space=pl.ANY)] * 6,
        out_specs=pl.BlockSpec(memory_space=pl.ANY),
        scratch_shapes=[
            vmem(*shape), vmem(*shape), vmem(*plane), vmem(*plane), vmem(*plane), pltpu.VMEM(plane, jnp.int32),
            vmem(2, 2, 64, 128), vmem(*shape),
            vmem(2, 4, 2, 2, 16, 128), vmem(8, 2, 2, 16, 128), vmem(2, 16, 16, 128), vmem(16, 16, 128),
            vmem(256, 128), vmem(2, 64, 128), vmem(256, 128), vmem(2, 64, 128), vmem(256, 128), vmem(16, 128), vmem(16, 128),
            vmem(11, 2, 256, 128), vmem(256, 128), vmem(6, 16, 16, 128), vmem(8, 3, 16, 128), vmem(8, 3, 16, 128),
            vmem(6, 8, 16, 128), vmem(2, 8, 32, 128), vmem(8, 64, 128), vmem(256, 128), vmem(16, 16, 128), vmem(16, 16, 128), vmem(2, 2, 64, 128),
            pltpu.SemaphoreType.DMA((6,)), pltpu.SemaphoreType.DMA((13,)), pltpu.SemaphoreType.DMA((13,)),
        ],
        compiler_params=pltpu.CompilerParams(
            collective_id=0, has_side_effects=True, vmem_limit_bytes=60 * 1024 * 1024
        ),
        name="covariance",
    )(increment, deviations, diffuse_x, diffuse_y, diffuse_z, sea_mask)


def solution(mesh):
    in_specs = (
        P(None, "lev", "lat", None),
        P(None, "lev", "lat", None),
        P("lev", "lat", None),
        P("lev", "lat", None),
        P("lev", "lat", None),
        P("lev", "lat", None),
    )
    out_specs = P(None, "lev", "lat", None)
    return jax.shard_map(
        per_device, mesh=mesh, in_specs=in_specs, out_specs=out_specs, check_vma=False
    )
```
